1024 devices in a mesh: expert: 16 (over z), dp: 64 (over x, y, core).
Axes of the slice: x: 4, y: 8, z: 16, core: 2. Of those that a mesh axis runs over, the one named last changes fastest.
Arguments:
- tokens: bfloat16 [8192, 3584], P('dp', 'expert'), may hold values from -6 to 6
- cotangent: bfloat16 [8192, 3584], P('dp', 'expert'), may hold values from -6 to 6
- routes: int32 [8192, 8], P('dp'), may hold values from 0 to 255, all different within a row; in each aligned block of 128 rows (0 to 127, 128 to 255, ...) at most 6 rows name the same one
- route_weights: float32 [8192, 8], P('dp'), may hold values from 0.1 to 1
- owner_slots: int32 [64], replicated, may hold values from 1 to 4
- gate_weight: bfloat16 [64, 3584, 1024], P('dp', 'expert'), may hold values from -0.09375 to 0.09375
- up_weight: bfloat16 [64, 3584, 1024], P('dp', 'expert'), may hold values from -0.09375 to 0.09375
- down_weight: bfloat16 [64, 1024, 3584], P('dp', None, 'expert'), may hold values from -0.1875 to 0.1875
Outputs:
- mixed: bfloat16 [8192, 3584], P('dp', 'expert')
- input_gradient: bfloat16 [8192, 3584], P('dp', 'expert')
- route_gradient: float32 [8192, 8], P('dp')
- gate_gradient: bfloat16 [64, 3584, 1024], P('dp', 'expert')
- up_gradient: bfloat16 [64, 3584, 1024], P('dp', 'expert')
- down_gradient: bfloat16 [64, 1024, 3584], P('dp', None, 'expert')
The draws below stay inside these ranges and needn't reach their ends.
Inputs may be any that keep to these rules, and one draw needn't show every extreme that they name: `routes`: each row names 8 different experts. In the 128 rows of one index of dp no expert is named more than 6 times, and some expert held is named exactly 6 times in some such block.
All inputs are finite; a program needn't handle non-finite values.
Results may differ from the reference program's by a relative error of at most 0.035.
Values may be sent and summed in bfloat16 or wider, within the bound.
No kernel may reach another device: no remote copies, remote signals or barrier semaphores. Data moves between devices by JAX's collectives and lax.ppermute only.
A program may use at most 32 MiB of HBM per device.

```python
import math
import jax
import jax.numpy as jnp
import numpy as np
from jax import lax

D = 3584
HID = 1024
EXPERTS_ALL = 256
TOPK = 8
TOK_DEV = 128
CAP = 6
SPARE = 2
OWN_MAX = 4
WINDOW = 64
TOKENS = 8192
N_EXPERT = 16
N_DP = 64


def place_ends(entries, rng, least, largest):
    longest = entries.shape.index(max(entries.shape))
    spots = []
    for shift in (0, 1):
        where = [jax.random.randint(jax.random.fold_in(rng, axis), (), 0, length) for axis, length in enumerate(entries.shape)]
        where[longest] = (where[longest] + shift) % entries.shape[longest]
        spots.append(tuple(where))
    return entries.at[spots[0]].set(least).at[spots[1]].set(largest)


def block_levels(rng, extent, cuts, smallest, high):
    def one(axis_at, shards_of):
        steps = jax.random.uniform(jax.random.fold_in(jax.random.fold_in(rng, 6), axis_at), (shards_of,), jnp.float32, smallest / len(cuts), high / len(cuts))
        return jnp.repeat(jnp.exp(steps), extent[axis_at] // shards_of).reshape((-1,) + (1,) * (len(extent) - axis_at - 1))

    level = one(*cuts[0])
    for cut in cuts[1:]:
        level = level * one(*cut)
    return level


def deal_out(own_key, own, number, rows, amount, top, most, lean):
    sequence = jax.random.permutation(own_key, amount)
    crowded, common = portions_of(amount, rows * top, most, lean, True), portions_of(amount, rows * top, most, lean, False)
    places = jnp.arange(amount)

    def named(sizes, rotation):
        used = int((sizes > 0).sum())
        fixed = max(1, used // 4)
        passed = fixed + (places - fixed + rotation * (used - fixed)) % max(1, amount - fixed)
        return jnp.zeros((amount,), jnp.int32).at[sequence[jnp.where(places < fixed, places, passed)]].set(jnp.asarray(sizes, jnp.int32))

    sizes = jnp.where(number % 4 == 0, named(crowded, number // 4), named(common, number - number // 4 - 1))
    mixed = jax.random.permutation(jax.random.fold_in(own, 3), amount)
    donor, receiver = mixed[0:amount // 2 * 2:2], mixed[1:amount // 2 * 2:2]
    slack = jnp.minimum(sizes[donor] - 1, most - sizes[receiver]) // 2
    slack = jnp.where((donor == sequence[0]) | (receiver == sequence[0]) | (sizes[receiver] == 0), 0, jnp.maximum(slack, 0))
    passed = jax.random.randint(jax.random.fold_in(own, 4), (amount // 2,), 0, 1 << 20) % (slack + 1)
    sizes = sizes.at[donor].add(-passed).at[receiver].add(passed)
    members = jnp.searchsorted(jnp.cumsum(sizes), jnp.arange(rows * top), side="right").astype(jnp.int32)
    grid = members.reshape(top, rows).T
    grid = grid[jax.random.permutation(jax.random.fold_in(own, 1), rows)]
    rotation = jax.random.randint(jax.random.fold_in(own, 2), (rows, 1), 0, top)
    return jnp.take_along_axis(grid, (jnp.arange(top)[None, :] + rotation) % top, axis=1)


def portions_of(number_of, total, limit, skew, full):
    weights = [(1 << 20) // math.isqrt(standing ** skew) + 1 for standing in range(1, number_of + 1)]
    largest = limit if full else min(limit, max(-(-total // number_of), total * weights[0] // sum(weights)))
    least = 1 if total - largest >= number_of - 1 else 0
    holding, spare = [largest] + [least] * (number_of - 1), total - largest - least * (number_of - 1)
    while spare > 0:
        movable = [i for i in range(1, number_of) if holding[i] < largest] or [i for i in range(1, number_of) if holding[i] < limit]
        whole, remaining = sum([weights[i] for i in movable]), spare
        for i in movable:
            extra = min(limit - holding[i], max(1, remaining * weights[i] // whole), spare)
            holding[i] = holding[i] + extra
            spare = spare - extra
    return np.array(holding)


def noise(key, extent, scale, reach, cuts=(), kind=jnp.bfloat16):
    array = scale * jax.random.normal(key, extent, jnp.float32)
    if cuts:
        array = array * block_levels(key, extent, cuts, -0.22, 0.18)
    return jnp.clip(array, -reach, reach).astype(kind)


def setup_inputs(seed: int = 0) -> dict:
    seeds = jax.random.split(jax.random.key(seed), 9)
    tokens = noise(seeds[0], (TOKENS, D), 1.0, 6.0, ((0, 64), (1, 16)))
    cotangent = noise(seeds[1], (TOKENS, D), 1.0, 6.0, ((0, 64), (1, 16)))
    routes_keys = jax.random.split(jax.random.fold_in(seeds[2], 1), TOKENS // TOK_DEV)
    routes_turns = jax.random.permutation(jax.random.fold_in(seeds[2], 3), TOKENS // TOK_DEV)
    routes = jax.vmap(lambda own, number: deal_out(jax.random.fold_in(seeds[2], 2), own, number, TOK_DEV, EXPERTS_ALL, TOPK, CAP, 1))(routes_keys, routes_turns).reshape((TOKENS, TOPK))
    route_weights = jnp.clip(jnp.exp(math.log(1.0) - 2.3025851 * jax.random.uniform(seeds[3], (TOKENS, TOPK), jnp.float32) ** block_levels(seeds[3], (TOKENS, TOPK), ((0, 64),), -0.2, 0.2)), 0.1, 1.0)
    owner_slots = place_ends(jax.random.randint(seeds[4], (WINDOW,), 1, OWN_MAX + 1), jax.random.fold_in(seeds[4], 1), 1, OWN_MAX).astype(jnp.int32)
    gate_weight = noise(seeds[5], (WINDOW, D, HID), D ** -0.5, 0.09375, ((0, 64), (1, 16)))
    up_weight = noise(seeds[6], (WINDOW, D, HID), D ** -0.5, 0.09375, ((0, 64), (1, 16)))
    down_weight = noise(seeds[7], (WINDOW, HID, D), HID ** -0.5, 0.1875, ((0, 64), (2, 16)))
    return {"tokens": tokens, "cotangent": cotangent, "routes": routes, "route_weights": route_weights, "owner_slots": owner_slots, "gate_weight": gate_weight, "up_weight": up_weight, "down_weight": down_weight}


def route_slots(block_routes, owner_slots, experts_here, slot_count, spare_count):
    flat_routes = block_routes.reshape(-1)
    route_count = flat_routes.shape[0]
    inside = flat_routes < experts_here
    expert_ids = jnp.arange(experts_here, dtype=jnp.int32)
    onehot = (flat_routes[:, None] == expert_ids[None, :]).astype(jnp.int32)
    before = (jnp.cumsum(onehot, axis=0) - onehot).astype(jnp.int32)
    route_rank = jnp.sum(before * onehot, axis=1).astype(jnp.int32)
    owner_share = jnp.sum(onehot * owner_slots[None, :], axis=1).astype(jnp.int32)
    to_owner = inside & (route_rank < owner_share)
    to_copy = inside & (route_rank >= owner_share) & (route_rank < owner_share + spare_count)
    served = to_owner | to_copy
    half_way = experts_here // 2
    target_dev = jnp.where(to_owner, flat_routes, (flat_routes + half_way) % experts_here)
    target = jnp.where(served, target_dev, experts_here).astype(jnp.int32)
    slot_place = jnp.where(to_owner, route_rank, slot_count - spare_count + route_rank - owner_share)
    slot_place = jnp.where(served, slot_place, 0).astype(jnp.int32)
    route_order = jnp.arange(route_count, dtype=jnp.int32)
    slot_table = jnp.zeros((experts_here + 1, slot_count), jnp.int32).at[target, slot_place].set(route_order)
    filled = jnp.zeros((experts_here + 1, slot_count), jnp.int32).at[target, slot_place].set(1)
    return slot_table[:experts_here], filled[:experts_here] > 0, target, slot_place, served


def block_sum(split_rows, split_matrix, form):
    partial_value = jnp.einsum(form, split_rows.astype(jnp.float32), split_matrix.astype(jnp.float32))
    rounded = lax.optimization_barrier(partial_value.astype(jnp.bfloat16)).astype(jnp.float32)
    return jnp.sum(rounded, axis=0)


def owner_rows(values):
    width = values.shape[-1]
    return values.reshape(N_DP, CAP, width)[:, :OWN_MAX].reshape(-1, width)


def spare_rows(values):
    width = values.shape[-1]
    return values.reshape(N_DP, CAP, width)[:, OWN_MAX:].reshape(-1, width)


def split_outer(left, right):
    contract_first = (((0,), (0,)), ((), ()))
    owner_term = lax.dot_general(owner_rows(left), owner_rows(right), contract_first, preferred_element_type=jnp.float32)
    copy_term = lax.dot_general(spare_rows(left), spare_rows(right), contract_first, preferred_element_type=jnp.float32)
    copy_rounded = lax.optimization_barrier(copy_term.astype(jnp.bfloat16)).astype(jnp.float32)
    return (owner_term + copy_rounded).astype(jnp.bfloat16)


def reference(tokens, cotangent, routes, route_weights, owner_slots, gate_weight, up_weight, down_weight):
    experts_here = N_DP
    half_way = experts_here // 2
    part_count = N_EXPERT
    feature_count = tokens.shape[1]
    piece_width = feature_count // part_count
    top_count = routes.shape[1]
    hidden_count = gate_weight.shape[2]
    block_routes = routes.reshape(N_DP, TOK_DEV, top_count)
    tables, filled = jax.vmap(lambda one_block: route_slots(one_block, owner_slots, experts_here, CAP, SPARE)[:2])(block_routes)
    block_base = (jnp.arange(N_DP, dtype=jnp.int32) * (TOK_DEV * top_count))[:, None]
    flat_weights = route_weights.reshape(-1)
    contract_last = (((1,), (1,)), ((), ()))

    def expert_step(running, expert):
        out_sum, input_sum, score_sum = running
        partner = ((expert + half_way) % experts_here).astype(jnp.int32)
        own_index = tables[:, expert, :OWN_MAX]
        copy_index = tables[:, partner, OWN_MAX:]
        route_index = (jnp.concatenate([own_index, copy_index], axis=1) + block_base).reshape(-1)
        live_rows = jnp.concatenate([filled[:, expert, :OWN_MAX], filled[:, partner, OWN_MAX:]], axis=1).reshape(-1)
        token_ids = route_index // top_count
        token_rows = jnp.where(live_rows[:, None], tokens[token_ids], 0).astype(jnp.bfloat16)
        cot_rows = cotangent[token_ids].astype(jnp.float32)
        route_scale = jnp.where(live_rows, flat_weights[route_index], 0.0)
        scaled_rows = (cot_rows * route_scale[:, None]).astype(jnp.bfloat16)
        row_count = token_rows.shape[0]
        gate_matrix = gate_weight[expert]
        up_matrix = up_weight[expert]
        down_matrix = down_weight[expert]
        split_tokens = token_rows.reshape(row_count, part_count, piece_width)
        gate_full = block_sum(split_tokens, gate_matrix.reshape(part_count, piece_width, hidden_count), "rjd,jdh->jrh")
        up_full = block_sum(split_tokens, up_matrix.reshape(part_count, piece_width, hidden_count), "rjd,jdh->jrh")
        sigmoid_gate = jax.nn.sigmoid(gate_full)
        hidden = (gate_full * sigmoid_gate * up_full).astype(jnp.bfloat16)
        out_rows = jnp.dot(hidden, down_matrix, preferred_element_type=jnp.float32).astype(jnp.bfloat16)
        down_grad = split_outer(hidden, scaled_rows)
        hidden_grad = block_sum(scaled_rows.reshape(row_count, part_count, piece_width), down_matrix.reshape(hidden_count, part_count, piece_width), "rjd,hjd->jrh")
        gate_delta = (hidden_grad * up_full * sigmoid_gate * (1.0 + gate_full * (1.0 - sigmoid_gate))).astype(jnp.bfloat16)
        up_delta = (hidden_grad * gate_full * sigmoid_gate).astype(jnp.bfloat16)
        input_rows = (lax.dot_general(gate_delta, gate_matrix, contract_last, preferred_element_type=jnp.float32)
                      + lax.dot_general(up_delta, up_matrix, contract_last, preferred_element_type=jnp.float32)).astype(jnp.bfloat16)
        gate_grad = split_outer(token_rows, gate_delta)
        up_grad = split_outer(token_rows, up_delta)
        out_f32 = jnp.where(live_rows[:, None], out_rows.astype(jnp.float32), 0.0)
        input_f32 = jnp.where(live_rows[:, None], input_rows.astype(jnp.float32), 0.0)
        out_sum = out_sum.at[token_ids].add(route_scale[:, None] * out_f32)
        input_sum = input_sum.at[token_ids].add(input_f32)
        score = jnp.sum(cot_rows * out_f32, axis=1)
        score_sum = score_sum.at[route_index].add(jnp.where(live_rows, score, 0.0))
        return (out_sum, input_sum, score_sum), (gate_grad, up_grad, down_grad)

    start = (jnp.zeros(tokens.shape, jnp.float32), jnp.zeros(tokens.shape, jnp.float32),
             jnp.zeros((routes.shape[0] * top_count,), jnp.float32))
    finals, grads = lax.scan(expert_step, start, jnp.arange(experts_here, dtype=jnp.int32))
    out_sum, input_sum, score_sum = finals
    mixed = out_sum.astype(jnp.bfloat16)
    input_gradient = input_sum.astype(jnp.bfloat16)
    route_gradient = score_sum.reshape(routes.shape[0], top_count)
    return mixed, input_gradient, route_gradient, grads[0], grads[1], grads[2]
```

```python
import jax
import jax.numpy as jnp
from jax import lax
from jax.experimental import pallas as pl
from jax.experimental.pallas import tpu as pltpu
from jax.sharding import PartitionSpec as P

CAP = 6
SPARE = 2
LANES = 128
TILES = 4
GROUP = CAP * TILES
SOURCES = 16
SCORE_LANE = 96
VMEM_LIMIT = 48 * 1024 * 1024

F32 = jnp.float32
BF16 = jnp.bfloat16
CONTRACT_LAST = (((1,), (1,)), ((), ()))
CONTRACT_FIRST = (((0,), (0,)), ((), ()))


def dot(left, right, dims=(((1,), (0,)), ((), ()))):
    return lax.dot_general(left, right, dims, preferred_element_type=F32)


def one_zero(condition):
    return jnp.where(condition, 1.0, 0.0).astype(BF16)


def three_parts(value):
    high = value.astype(BF16)
    rest = value - high.astype(F32)
    middle = rest.astype(BF16)
    return high, middle, (rest - middle.astype(F32)).astype(BF16)


def iota(shape, axis):
    return lax.broadcasted_iota(jnp.int32, shape, axis)


def expert_of_row(row, expert):
    offset = row - GROUP * expert
    return (offset >= 0) & (offset < GROUP)


def tile_and_slot(row):
    place = row - GROUP * lax.shift_right_logical(row * 2731, 16)
    tile = (
        (place >= CAP).astype(jnp.int32)
        + (place >= 2 * CAP).astype(jnp.int32)
        + (place >= 3 * CAP).astype(jnp.int32)
    )
    return tile, place - CAP * tile


def reorder_matrix(sorted_row, sent_row):
    per_tile = SOURCES * CAP
    tile = (
        (sorted_row >= per_tile).astype(jnp.int32)
        + (sorted_row >= 2 * per_tile).astype(jnp.int32)
        + (sorted_row >= 3 * per_tile).astype(jnp.int32)
    )
    within = sorted_row - per_tile * tile
    source = lax.shift_right_logical(within * 43, 8)
    return one_zero(sent_row == within + (GROUP - CAP) * source + CAP * tile)


def dispatch_kernel(tok_ref, cot_ref, routes_ref, weight_ref, slots_ref, send_ref, rank_ref, scale_ref):
    token_count, top_count = routes_ref.shape
    experts = slots_ref.shape[1]
    rows = experts * GROUP
    expert = iota((token_count, experts), 1)
    named = jnp.zeros((token_count, experts), F32)
    scale = jnp.zeros((token_count, experts), F32)
    for k in range(top_count):
        hit = routes_ref[:, k : k + 1] == expert
        named = named + jnp.where(hit, 1.0, 0.0)
        scale = scale + jnp.where(hit, weight_ref[:, k : k + 1], 0.0)
    earlier = one_zero(iota((token_count, token_count), 0) > iota((token_count, token_count), 1))
    rank = dot(earlier, named.astype(BF16))
    limit = slots_ref[...].astype(F32) + float(SPARE)
    rank = jnp.where((named > 0.0) & (rank < limit), rank, -1.0)
    rank_ref[...] = rank
    scale_ref[...] = scale
    spread = one_zero(expert_of_row(iota((rows, experts), 0), iota((rows, experts), 1)))
    tile, slot = tile_and_slot(iota((rows, token_count), 0))
    taken = dot(spread, rank.astype(BF16), CONTRACT_LAST) == slot.astype(F32)
    row_scale = sum(dot(spread, part, CONTRACT_LAST) for part in three_parts(scale))
    row_scale = jnp.sum(jnp.where(taken, row_scale, 0.0), axis=1, keepdims=True)
    row_scale = jnp.where(tile[:, :1] >= 2, row_scale, 1.0)
    width = tok_ref.shape[1]
    picked = jnp.zeros((rows, LANES), F32)
    for index, ref in ((0, tok_ref), (2, cot_ref)):
        low = ref[:, :LANES]
        high = jnp.concatenate(
            [ref[:, LANES:].astype(F32), jnp.zeros((token_count, 2 * LANES - width), F32)], axis=1
        ).astype(BF16)
        picked = picked + dot(one_zero(taken & (tile == index)), low)
        picked = picked + dot(one_zero(taken & (tile == index + 1)), high)
    send_ref[...] = (picked * row_scale).astype(BF16).reshape(send_ref.shape)


def partial_kernel(recv_ref, gate_ref, up_ref, down_ref, part_ref, tok_ref, scaled_ref):
    experts = recv_ref.shape[0]
    hidden = gate_ref.shape[2]
    width = gate_ref.shape[1]
    block = SOURCES * GROUP
    per_tile = SOURCES * CAP
    reorder = reorder_matrix(iota((block, block), 0), iota((block, block), 1))
    for b in range(experts // SOURCES):
        sent = recv_ref[b * SOURCES : (b + 1) * SOURCES].reshape(block, LANES)
        rows = dot(reorder, sent).astype(BF16)
        place = slice(b * per_tile, (b + 1) * per_tile)
        for ref, index in ((tok_ref, 0), (scaled_ref, 2)):
            ref[place, :LANES] = rows[index * per_tile : (index + 1) * per_tile]
            ref[place, LANES:] = rows[(index + 1) * per_tile : (index + 2) * per_tile, : width - LANES]
    step = 256
    for start in range(0, hidden, step):
        columns = slice(start, start + step)
        part_ref[:, start : start + step] = dot(tok_ref[...], gate_ref[0, :, columns]).astype(BF16)
        part_ref[:, hidden + start : hidden + start + step] = dot(
            tok_ref[...], up_ref[0, :, columns]
        ).astype(BF16)
        part_ref[:, 2 * hidden + start : 2 * hidden + start + step] = dot(
            scaled_ref[...], down_ref[0, columns, :], CONTRACT_LAST
        ).astype(BF16)


def middle_kernel(sum_ref, out_ref):
    hidden = sum_ref.shape[1] // 3
    gate = sum_ref[:, :hidden].astype(F32)
    up = sum_ref[:, hidden : 2 * hidden].astype(F32)
    grad = sum_ref[:, 2 * hidden :].astype(F32)
    sigmoid = jax.nn.sigmoid(gate)
    gated = gate * sigmoid
    hidden_value = (gated * up).astype(BF16)
    out_ref[:, :hidden] = hidden_value
    out_ref[:, hidden : 2 * hidden] = (grad * up * sigmoid * (1.0 + gate * (1.0 - sigmoid))).astype(BF16)
    out_ref[:, 2 * hidden : 3 * hidden] = (grad * gated).astype(BF16)
    score = jnp.sum(hidden_value.astype(F32) * grad, axis=1, keepdims=True)
    lane = iota((gate.shape[0], LANES), 1)
    packed = jnp.zeros(lane.shape, F32)
    for index, part in enumerate(three_parts(score)):
        packed = jnp.where(lane == SCORE_LANE + index, part.astype(F32), packed)
    out_ref[:, 3 * hidden :] = packed.astype(BF16)


def rows_kernel(full_ref, gate_ref, up_ref, down_ref, back_ref, tiles_ref):
    experts = back_ref.shape[0]
    hidden = gate_ref.shape[2]
    width = gate_ref.shape[1]
    block = SOURCES * GROUP
    per_tile = SOURCES * CAP
    out_rows = dot(full_ref[:, :hidden], down_ref[0])
    in_rows = dot(full_ref[:, hidden : 2 * hidden], gate_ref[0], CONTRACT_LAST) + dot(
        full_ref[:, 2 * hidden : 3 * hidden], up_ref[0], CONTRACT_LAST
    )
    tiles_ref[0] = out_rows[:, :LANES]
    tiles_ref[1] = full_ref[:, 3 * hidden :].astype(F32)
    tiles_ref[1, :, : width - LANES] = out_rows[:, LANES:]
    tiles_ref[2] = in_rows[:, :LANES]
    tiles_ref[3] = jnp.zeros(tiles_ref.shape[1:], F32)
    tiles_ref[3, :, : width - LANES] = in_rows[:, LANES:]
    restore = reorder_matrix(iota((block, block), 1), iota((block, block), 0))
    for b in range(experts // SOURCES):
        place = slice(b * per_tile, (b + 1) * per_tile)
        stacked = tiles_ref[:, place].astype(BF16).reshape(block, LANES)
        back_ref[b * SOURCES : (b + 1) * SOURCES] = (
            dot(restore, stacked).astype(BF16).reshape(SOURCES, GROUP, LANES)
        )


def combine_kernel(
    back_ref, rank_ref, scale_ref, routes_ref, weight_ref, mixed_ref, input_ref, score_ref
):
    token_count, experts = rank_ref.shape
    top_count = routes_ref.shape[1]
    width = mixed_ref.shape[1]
    rows = experts * GROUP
    back = back_ref[...].reshape(rows, LANES)
    spread = one_zero(expert_of_row(iota((experts, rows), 1), iota((experts, rows), 0)))
    tile, slot = tile_and_slot(iota((token_count, rows), 1))
    taken = dot(rank_ref[...].astype(BF16), spread) == slot.astype(F32)
    mixed = [jnp.zeros((token_count, LANES), F32) for _ in range(2)]
    for part in three_parts(scale_ref[...]):
        scale = dot(part, spread)
        for index in range(2):
            chosen = jnp.where(taken & (tile == index), scale, 0.0).astype(BF16)
            mixed[index] = mixed[index] + dot(chosen, back)
    mixed_ref[:, :LANES] = mixed[0].astype(BF16)
    mixed_ref[:, LANES:] = mixed[1][:, : width - LANES].astype(BF16)
    input_ref[:, :LANES] = dot(one_zero(taken & (tile == 2)), back).astype(BF16)
    input_ref[:, LANES:] = dot(one_zero(taken & (tile == 3)), back)[:, : width - LANES].astype(BF16)
    lane = iota((8, LANES), 1)
    score_lanes = one_zero((lane >= SCORE_LANE) & (lane < SCORE_LANE + 3))
    row_score = dot(score_lanes, back, CONTRACT_LAST)[:1]
    routed = jnp.where(taken & (tile == 1), row_score, 0.0)
    by_expert = sum(dot(part, spread, CONTRACT_LAST) for part in three_parts(routed))
    expert = iota((token_count, experts), 1)
    for k in range(top_count):
        hit = routes_ref[:, k : k + 1] == expert
        value = jnp.sum(jnp.where(hit, by_expert, 0.0), axis=1, keepdims=True)
        score_ref[:, k : k + 1] = value / weight_ref[:, k : k + 1]


def kernel_call(body, out_shape, flops, moved, scratch=()):
    return pl.pallas_call(
        body,
        out_shape=out_shape,
        scratch_shapes=scratch,
        compiler_params=pltpu.CompilerParams(vmem_limit_bytes=VMEM_LIMIT),
        cost_estimate=pl.CostEstimate(flops=flops, bytes_accessed=moved, transcendentals=0),
    )


def per_device(
    tokens, cotangent, routes, route_weights, owner_slots, gate_weight, up_weight, down_weight
):
    experts = lax.axis_size("dp")
    parts = lax.axis_size("expert")
    token_count, width = tokens.shape
    hidden = gate_weight.shape[2]
    row_count = experts * CAP
    shape = jax.ShapeDtypeStruct
    exchanged = shape((experts, GROUP, LANES), BF16)
    per_expert = shape((token_count, experts), F32)
    send, rank, scale = kernel_call(
        dispatch_kernel, (exchanged, per_expert, per_expert), 300_000_000, 1_000_000
    )(tokens, cotangent, routes, route_weights, owner_slots.reshape(1, experts))
    arrived = lax.all_to_all(send, "dp", split_axis=0, concat_axis=0, tiled=True)
    rows = shape((row_count, width), BF16)
    part, token_rows, scaled_rows = kernel_call(
        partial_kernel, (shape((row_count, 3 * hidden), BF16), rows, rows), 700_000_000, 4_500_000
    )(arrived, gate_weight, up_weight, down_weight)
    summed = lax.psum_scatter(part, "expert", scatter_dimension=0, tiled=True)
    share = kernel_call(
        middle_kernel, shape((row_count // parts, 3 * hidden + LANES), BF16), 1_000_000, 300_000
    )(summed)
    full = lax.all_gather(share, "expert", axis=0, tiled=True)
    back = kernel_call(
        rows_kernel,
        exchanged,
        700_000_000,
        4_500_000,
        scratch=[pltpu.VMEM((TILES, row_count, LANES), F32)],
    )(full, gate_weight, up_weight, down_weight)
    returned = lax.all_to_all(back, "dp", split_axis=0, concat_axis=0, tiled=True)
    gate_grad = dot(token_rows, full[:, hidden : 2 * hidden], CONTRACT_FIRST).astype(BF16)
    up_grad = dot(token_rows, full[:, 2 * hidden : 3 * hidden], CONTRACT_FIRST).astype(BF16)
    down_grad = dot(full[:, :hidden], scaled_rows, CONTRACT_FIRST).astype(BF16)
    token_shape = shape(tokens.shape, BF16)
    mixed, input_gradient, route_gradient = kernel_call(
        combine_kernel,
        (token_shape, token_shape, shape(routes.shape, F32)),
        500_000_000,
        1_000_000,
    )(returned, rank, scale, routes, route_weights)
    return (mixed, input_gradient, route_gradient, gate_grad[None], up_grad[None], down_grad[None])


def solution(mesh):
    return jax.shard_map(
        per_device,
        mesh=mesh,
        in_specs=(
            P("dp", "expert"),
            P("dp", "expert"),
            P("dp", None),
            P("dp", None),
            P(),
            P("dp", "expert", None),
            P("dp", "expert", None),
            P("dp", None, "expert"),
        ),
        out_specs=(
            P("dp", "expert"),
            P("dp", "expert"),
            P("dp", None),
            P("dp", "expert", None),
            P("dp", "expert", None),
            P("dp", None, "expert"),
        ),
        check_vma=False,
    )
```

```python
import functools

import jax
import jax.numpy as jnp
from jax import lax
from jax.experimental import pallas as pl
from jax.experimental.pallas import tpu as pltpu
from jax.sharding import PartitionSpec as P

CAP = 6
SPARE = 2
LANES = 128
TILES = 4
GROUP = CAP * TILES
SOURCES = 16
RING = 4
SCORE_LANE = 96
VMEM_LIMIT = 24 * 1024 * 1024

F32 = jnp.float32
BF16 = jnp.bfloat16
CONTRACT_LAST = (((1,), (1,)), ((), ()))
CONTRACT_FIRST = (((0,), (0,)), ((), ()))


def dot(left, right, dims=(((1,), (0,)), ((), ()))):
    return lax.dot_general(left, right, dims, preferred_element_type=F32)


def one_zero(condition):
    return jnp.where(condition, 1.0, 0.0).astype(BF16)


def three_parts(value):
    high = value.astype(BF16)
    rest = value - high.astype(F32)
    middle = rest.astype(BF16)
    return high, middle, (rest - middle.astype(F32)).astype(BF16)


def iota(shape, axis):
    return lax.broadcasted_iota(jnp.int32, shape, axis)


def expert_of_row(row, expert):
    offset = row - GROUP * expert
    return (offset >= 0) & (offset < GROUP)


def tile_and_slot(row):
    place = row - GROUP * lax.shift_right_logical(row * 2731, 16)
    tile = (
        (place >= CAP).astype(jnp.int32)
        + (place >= 2 * CAP).astype(jnp.int32)
        + (place >= 3 * CAP).astype(jnp.int32)
    )
    return tile, place - CAP * tile


def reorder_matrix(sorted_row, sent_row):
    per_tile = SOURCES * CAP
    tile = (
        (sorted_row >= per_tile).astype(jnp.int32)
        + (sorted_row >= 2 * per_tile).astype(jnp.int32)
        + (sorted_row >= 3 * per_tile).astype(jnp.int32)
    )
    within = sorted_row - per_tile * tile
    source = lax.shift_right_logical(within * 43, 8)
    return one_zero(sent_row == within + (GROUP - CAP) * source + CAP * tile)


def interleave_matrix(row_count, parts):
    share = row_count // parts
    row = iota((row_count, 1), 0)
    part = sum((row >= share * i).astype(jnp.int32) for i in range(1, parts))
    ring = lax.shift_right_logical(part, 2)
    member = part - RING * ring
    kept = row + share * (member * (parts // RING) + ring - part)
    return one_zero(iota((row_count, row_count), 1) == kept)


def dispatch_kernel(tok_ref, cot_ref, routes_ref, weight_ref, slots_ref, send_ref, plan_ref):
    top_count, token_count = routes_ref.shape
    experts = slots_ref.shape[1]
    rows = experts * GROUP
    expert = iota((experts, token_count), 0)
    named = jnp.zeros((experts, token_count), F32)
    scale = jnp.zeros((experts, token_count), F32)
    for k in range(top_count):
        hit = routes_ref[k : k + 1] == expert
        named = named + jnp.where(hit, 1.0, 0.0)
        scale = scale + jnp.where(hit, weight_ref[k : k + 1], 0.0)
    earlier = one_zero(iota((token_count, token_count), 0) < iota((token_count, token_count), 1))
    rank = dot(named.astype(BF16), earlier)
    diagonal = iota((experts, experts), 0) == iota((experts, experts), 1)
    limit = jnp.sum(jnp.where(diagonal, slots_ref[...].astype(F32), 0.0), axis=1, keepdims=True)
    rank = jnp.where((named > 0.0) & (rank < limit + float(SPARE)), rank, -1.0)
    plan_ref[:experts] = rank
    plan_ref[experts:] = scale
    spread = one_zero(expert_of_row(iota((rows, experts), 0), iota((rows, experts), 1)))
    tile, slot = tile_and_slot(iota((rows, token_count), 0))
    taken = dot(spread, rank.astype(BF16)) == slot.astype(F32)
    row_scale = sum(dot(spread, part) for part in three_parts(scale))
    row_scale = jnp.sum(jnp.where(taken, row_scale, 0.0), axis=1, keepdims=True)
    row_scale = jnp.where(tile[:, :1] >= 2, row_scale, 1.0)
    width = tok_ref.shape[0]
    picked = jnp.zeros((rows, LANES), F32)
    for index, ref in ((0, tok_ref), (2, cot_ref)):
        high = jnp.concatenate(
            [ref[LANES:], jnp.zeros((2 * LANES - width, token_count), BF16)], axis=0
        )
        picked = picked + dot(one_zero(taken & (tile == index)), ref[:LANES], CONTRACT_LAST)
        picked = picked + dot(one_zero(taken & (tile == index + 1)), high, CONTRACT_LAST)
    send_ref[...] = (picked * row_scale).astype(BF16).reshape(send_ref.shape)


def partial_kernel(parts, recv_ref, gate_ref, up_ref, down_ref, part_ref, tok_ref, scaled_ref):
    experts = recv_ref.shape[0]
    width, hidden = gate_ref.shape
    block = SOURCES * GROUP
    per_tile = SOURCES * CAP
    reorder = reorder_matrix(iota((block, block), 0), iota((block, block), 1))
    for b in range(experts // SOURCES):
        sent = recv_ref[b * SOURCES : (b + 1) * SOURCES].reshape(block, LANES)
        rows = dot(reorder, sent).astype(BF16)
        place = slice(b * per_tile, (b + 1) * per_tile)
        for ref, index in ((tok_ref, 0), (scaled_ref, 2)):
            ref[place, :LANES] = rows[index * per_tile : (index + 1) * per_tile]
            ref[place, LANES:] = rows[(index + 1) * per_tile : (index + 2) * per_tile, : width - LANES]
    interleave = interleave_matrix(tok_ref.shape[0], parts)
    token_rows = dot(interleave, tok_ref[...]).astype(BF16)
    scaled_rows = dot(interleave, scaled_ref[...]).astype(BF16)
    step = 256
    for index, (rows, ref) in enumerate(
        ((token_rows, gate_ref), (token_rows, up_ref), (scaled_rows, down_ref))
    ):
        for start in range(0, hidden, step):
            value = dot(rows, ref[:, start : start + step]).astype(BF16)
            part_ref[:, index * hidden + start : index * hidden + start + step] = value


def middle_kernel(sum_ref, out_ref):
    hidden = sum_ref.shape[1] // 3
    gate = sum_ref[:, :hidden].astype(F32)
    up = sum_ref[:, hidden : 2 * hidden].astype(F32)
    grad = sum_ref[:, 2 * hidden :].astype(F32)
    sigmoid = jax.nn.sigmoid(gate)
    gated = gate * sigmoid
    hidden_value = (gated * up).astype(BF16)
    out_ref[:, :hidden] = hidden_value
    out_ref[:, hidden : 2 * hidden] = (grad * up * sigmoid * (1.0 + gate * (1.0 - sigmoid))).astype(BF16)
    out_ref[:, 2 * hidden : 3 * hidden] = (grad * gated).astype(BF16)
    score = jnp.sum(hidden_value.astype(F32) * grad, axis=1, keepdims=True)
    lane = iota((gate.shape[0], LANES), 1)
    packed = jnp.zeros(lane.shape, F32)
    for index, part in enumerate(three_parts(score)):
        packed = jnp.where(lane == SCORE_LANE + index, part.astype(F32), packed)
    out_ref[:, 3 * hidden :] = packed.astype(BF16)


def rows_kernel(
    place_ref,
    own_ref,
    left_ref,
    right_ref,
    far_left_ref,
    far_right_ref,
    gate_ref,
    up_ref,
    down_ref,
    back_ref,
    full_ref,
    tiles_ref,
):
    experts = back_ref.shape[0]
    width, hidden = gate_ref.shape
    block = SOURCES * GROUP
    per_tile = SOURCES * CAP
    held = own_ref.shape[0]
    half = held // 2
    for ref, step, start in (
        (own_ref, 0, 0),
        (right_ref, 1, 0),
        (left_ref, RING - 1, 0),
        (far_left_ref, RING // 2, 0),
        (far_right_ref, RING // 2, half),
    ):
        member = (place_ref[0] + step) & (RING - 1)
        begin = pl.multiple_of(member * held + start, half)
        full_ref[pl.ds(begin, ref.shape[0])] = ref[...]
    out_rows = dot(full_ref[:, :hidden], down_ref[...], CONTRACT_LAST)
    in_rows = dot(full_ref[:, hidden : 2 * hidden], gate_ref[...], CONTRACT_LAST) + dot(
        full_ref[:, 2 * hidden : 3 * hidden], up_ref[...], CONTRACT_LAST
    )
    tiles_ref[0] = out_rows[:, :LANES]
    tiles_ref[1] = full_ref[:, 3 * hidden :].astype(F32)
    tiles_ref[1, :, : width - LANES] = out_rows[:, LANES:]
    tiles_ref[2] = in_rows[:, :LANES]
    tiles_ref[3] = jnp.zeros(tiles_ref.shape[1:], F32)
    tiles_ref[3, :, : width - LANES] = in_rows[:, LANES:]
    restore = reorder_matrix(iota((block, block), 1), iota((block, block), 0))
    for b in range(experts // SOURCES):
        place = slice(b * per_tile, (b + 1) * per_tile)
        stacked = tiles_ref[:, place].astype(BF16).reshape(block, LANES)
        back_ref[b * SOURCES : (b + 1) * SOURCES] = (
            dot(restore, stacked).astype(BF16).reshape(SOURCES, GROUP, LANES)
        )


def combine_kernel(back_ref, plan_ref, routes_ref, weight_ref, mixed_ref, input_ref, score_ref):
    top_count, token_count = routes_ref.shape
    experts = plan_ref.shape[0] // 2
    width = mixed_ref.shape[0]
    rows = experts * GROUP
    back = back_ref[...].reshape(rows, LANES)
    plan = plan_ref[...].T
    rank, scale = plan[:, :experts], plan[:, experts:]
    spread = one_zero(expert_of_row(iota((experts, rows), 1), iota((experts, rows), 0)))
    tile, slot = tile_and_slot(iota((token_count, rows), 1))
    taken = dot(rank.astype(BF16), spread) == slot.astype(F32)
    mixed = [jnp.zeros((token_count, LANES), F32) for _ in range(2)]
    for part in three_parts(scale):
        row_scale = dot(part, spread)
        for index in range(2):
            chosen = jnp.where(taken & (tile == index), row_scale, 0.0).astype(BF16)
            mixed[index] = mixed[index] + dot(chosen, back)
    for ref, low, high in (
        (mixed_ref, mixed[0], mixed[1]),
        (
            input_ref,
            dot(one_zero(taken & (tile == 2)), back),
            dot(one_zero(taken & (tile == 3)), back),
        ),
    ):
        ref[:LANES] = low.T.astype(BF16)
        ref[LANES:] = high.T[: width - LANES].astype(BF16)
    lane = iota((8, LANES), 1)
    score_lanes = one_zero((lane >= SCORE_LANE) & (lane < SCORE_LANE + 3))
    row_score = dot(score_lanes, back, CONTRACT_LAST)[:1]
    routed = jnp.where(taken & (tile == 1), row_score, 0.0)
    by_expert = sum(dot(spread, part, CONTRACT_LAST) for part in three_parts(routed))
    expert = iota((experts, token_count), 0)
    for k in range(top_count):
        hit = routes_ref[k : k + 1] == expert
        value = jnp.sum(jnp.where(hit, by_expert, 0.0), axis=0, keepdims=True)
        score_ref[k : k + 1] = value / weight_ref[k : k + 1]


def kernel_call(body, out_shape, flops, moved, scalars=0, inputs=0, scratch=()):
    places = {}
    if scalars:
        places["in_specs"] = [pl.BlockSpec(memory_space=pltpu.SMEM)] * scalars + [
            pl.BlockSpec(memory_space=pltpu.VMEM)
        ] * inputs
    return pl.pallas_call(
        body,
        out_shape=out_shape,
        scratch_shapes=scratch,
        compiler_params=pltpu.CompilerParams(vmem_limit_bytes=VMEM_LIMIT),
        cost_estimate=pl.CostEstimate(flops=flops, bytes_accessed=moved, transcendentals=0),
        **places,
    )


def shifted(block, distance):
    parts = lax.axis_size("expert")
    return lax.ppermute(block, "expert", [(i, (i + distance) % parts) for i in range(parts)])


def per_device(
    tokens, cotangent, routes, route_weights, owner_slots, gate_weight, up_weight, down_weight
):
    experts = lax.axis_size("dp")
    parts = lax.axis_size("expert")
    token_count, width = tokens.shape
    hidden = gate_weight.shape[2]
    row_count = experts * CAP
    shape = jax.ShapeDtypeStruct
    exchanged = shape((experts, GROUP, LANES), BF16)
    routes_by_rank, weights_by_rank = routes.T, route_weights.T
    gate_matrix, up_matrix, down_matrix = gate_weight[0], up_weight[0], down_weight[0].T
    send, plan = kernel_call(
        dispatch_kernel, (exchanged, shape((2 * experts, token_count), F32)), 300_000_000, 1_000_000
    )(tokens.T, cotangent.T, routes_by_rank, weights_by_rank, owner_slots.reshape(1, experts))
    arrived = lax.all_to_all(send, "dp", split_axis=0, concat_axis=0, tiled=True)
    rows = shape((row_count, width), BF16)
    part, token_rows, scaled_rows = kernel_call(
        functools.partial(partial_kernel, parts),
        (shape((row_count, 3 * hidden), BF16), rows, rows),
        700_000_000,
        4_500_000,
    )(arrived, gate_matrix, up_matrix, down_matrix)
    summed = lax.psum_scatter(part, "expert", scatter_dimension=0, tiled=True)
    share = kernel_call(
        middle_kernel, shape((row_count // parts, 3 * hidden + LANES), BF16), 1_000_000, 300_000
    )(summed)
    own = lax.all_gather(
        share,
        "expert",
        axis=0,
        tiled=True,
        axis_index_groups=[list(range(i, parts, RING)) for i in range(RING)],
    )
    half = own.shape[0] // 2
    left, right = shifted(own, 1), shifted(own, -1)
    far_left, far_right = shifted(left[:half], 1), shifted(right[half:], -1)
    member = (lax.axis_index("expert") % RING).astype(jnp.int32).reshape(1)
    back, full = kernel_call(
        rows_kernel,
        (exchanged, shape((row_count, 3 * hidden + LANES), BF16)),
        700_000_000,
        4_500_000,
        scalars=1,
        inputs=8,
        scratch=[pltpu.VMEM((TILES, row_count, LANES), F32)],
    )(member, own, left, right, far_left, far_right, gate_matrix, up_matrix, down_matrix)
    returned = lax.all_to_all(back, "dp", split_axis=0, concat_axis=0, tiled=True)
    gate_grad = dot(token_rows, full[:, hidden : 2 * hidden], CONTRACT_FIRST).astype(BF16)
    up_grad = dot(token_rows, full[:, 2 * hidden : 3 * hidden], CONTRACT_FIRST).astype(BF16)
    down_grad = dot(scaled_rows, full[:, :hidden], CONTRACT_FIRST).astype(BF16).T
    token_shape = shape((width, token_count), BF16)
    mixed, input_gradient, route_gradient = kernel_call(
        combine_kernel,
        (token_shape, token_shape, shape(routes_by_rank.shape, F32)),
        500_000_000,
        1_000_000,
    )(returned, plan, routes_by_rank, weights_by_rank)
    return (
        mixed.T,
        input_gradient.T,
        route_gradient.T,
        gate_grad[None],
        up_grad[None],
        down_grad[None],
    )


def solution(mesh):
    return jax.shard_map(
        per_device,
        mesh=mesh,
        in_specs=(
            P("dp", "expert"),
            P("dp", "expert"),
            P("dp", None),
            P("dp", None),
            P(),
            P("dp", "expert", None),
            P("dp", "expert", None),
            P("dp", None, "expert"),
        ),
        out_specs=(
            P("dp", "expert"),
            P("dp", "expert"),
            P("dp", None),
            P("dp", "expert", None),
            P("dp", "expert", None),
            P("dp", None, "expert"),
        ),
        check_vma=False,
    )
```

```python
import jax
import jax.numpy as jnp
from jax import lax
from jax.experimental import pallas as pl
from jax.experimental.pallas import tpu as pltpu
from jax.sharding import PartitionSpec as P

CAP = 6
SPARE = 2
LANES = 128
TILES = 4
GROUP = CAP * TILES
SOURCES = 16
RING = 4
SCORE_LANE = 96
VMEM_LIMIT = 24 * 1024 * 1024

F32 = jnp.float32
BF16 = jnp.bfloat16
CONTRACT_LAST = (((1,), (1,)), ((), ()))
CONTRACT_FIRST = (((0,), (0,)), ((), ()))


def dot(left, right, dims=(((1,), (0,)), ((), ()))):
    return lax.dot_general(left, right, dims, preferred_element_type=F32)


def one_zero(condition):
    return jnp.where(condition, 1.0, 0.0).astype(BF16)


def three_parts(value):
    high = value.astype(BF16)
    rest = value - high.astype(F32)
    middle = rest.astype(BF16)
    return high, middle, (rest - middle.astype(F32)).astype(BF16)


def iota(shape, axis):
    return lax.broadcasted_iota(jnp.int32, shape, axis)


def expert_of_row(row, expert):
    offset = row - GROUP * expert
    return (offset >= 0) & (offset < GROUP)


def tile_and_slot(row):
    place = row - GROUP * lax.shift_right_logical(row * 2731, 16)
    tile = (
        (place >= CAP).astype(jnp.int32)
        + (place >= 2 * CAP).astype(jnp.int32)
        + (place >= 3 * CAP).astype(jnp.int32)
    )
    return tile, place - CAP * tile


def reorder_matrix(sorted_row, sent_row):
    per_tile = SOURCES * CAP
    tile = (
        (sorted_row >= per_tile).astype(jnp.int32)
        + (sorted_row >= 2 * per_tile).astype(jnp.int32)
        + (sorted_row >= 3 * per_tile).astype(jnp.int32)
    )
    within = sorted_row - per_tile * tile
    source = lax.shift_right_logical(within * 43, 8)
    return one_zero(sent_row == within + (GROUP - CAP) * source + CAP * tile)


def fetch(sources, targets, sems):
    copies = [
        pltpu.make_async_copy(source, target, sems.at[i])
        for i, (source, target) in enumerate(zip(sources, targets))
    ]
    for copy in copies:
        copy.start()
    return copies


def dispatch_kernel(
    routes_hbm,
    weight_hbm,
    slots_hbm,
    tok_hbm,
    cot_hbm,
    send_ref,
    plan_ref,
    routes_ref,
    weight_ref,
    slots_ref,
    tok_ref,
    cot_ref,
    sems,
):
    arguments = (routes_hbm, weight_hbm, slots_hbm, tok_hbm, cot_hbm)
    held = (routes_ref, weight_ref, slots_ref, tok_ref, cot_ref)
    for copy in fetch(arguments, held, sems):
        copy.wait()
    top_count, token_count = routes_ref.shape
    experts = slots_ref.shape[1]
    rows = experts * GROUP
    expert = iota((experts, token_count), 0)
    named = jnp.zeros((experts, token_count), F32)
    scale = jnp.zeros((experts, token_count), F32)
    for k in range(top_count):
        hit = routes_ref[k : k + 1] == expert
        named = named + jnp.where(hit, 1.0, 0.0)
        scale = scale + jnp.where(hit, weight_ref[k : k + 1], 0.0)
    earlier = one_zero(iota((token_count, token_count), 0) < iota((token_count, token_count), 1))
    rank = dot(named.astype(BF16), earlier)
    diagonal = iota((experts, experts), 0) == iota((experts, experts), 1)
    limit = jnp.sum(jnp.where(diagonal, slots_ref[...].astype(F32), 0.0), axis=1, keepdims=True)
    rank = jnp.where((named > 0.0) & (rank < limit + float(SPARE)), rank, -1.0)
    plan_ref[:experts] = rank
    plan_ref[experts:] = scale
    spread = one_zero(expert_of_row(iota((rows, experts), 0), iota((rows, experts), 1)))
    tile, slot = tile_and_slot(iota((rows, token_count), 0))
    taken = dot(spread, rank.astype(BF16)) == slot.astype(F32)
    row_scale = sum(dot(spread, part) for part in three_parts(scale))
    row_scale = jnp.sum(jnp.where(taken, row_scale, 0.0), axis=1, keepdims=True)
    row_scale = jnp.where(tile[:, :1] >= 2, row_scale, 1.0)
    width = tok_ref.shape[0]
    picked = jnp.zeros((rows, LANES), F32)
    for index, ref in ((0, tok_ref), (2, cot_ref)):
        high = jnp.concatenate(
            [ref[LANES:], jnp.zeros((2 * LANES - width, token_count), BF16)], axis=0
        )
        picked = picked + dot(one_zero(taken & (tile == index)), ref[:LANES], CONTRACT_LAST)
        picked = picked + dot(one_zero(taken & (tile == index + 1)), high, CONTRACT_LAST)
    send_ref[...] = (picked * row_scale).astype(BF16).reshape(send_ref.shape)


def partial_kernel(
    place_ref,
    recv_ref,
    gate_hbm,
    up_hbm,
    down_hbm,
    own_ref,
    to_right_ref,
    to_left_ref,
    next_ref,
    previous_ref,
    tok_ref,
    scaled_ref,
    gate_ref,
    up_ref,
    down_ref,
    sems,
):
    copies = fetch((gate_hbm, up_hbm, down_hbm), (gate_ref, up_ref, down_ref), sems)
    experts = recv_ref.shape[0]
    width, hidden = gate_ref.shape
    block = SOURCES * GROUP
    per_tile = SOURCES * CAP
    reorder = reorder_matrix(iota((block, block), 0), iota((block, block), 1))
    for b in range(experts // SOURCES):
        sent = recv_ref[b * SOURCES : (b + 1) * SOURCES].reshape(block, LANES)
        rows = dot(reorder, sent).astype(BF16)
        place = slice(b * per_tile, (b + 1) * per_tile)
        for ref, index in ((tok_ref, 0), (scaled_ref, 2)):
            ref[place, :LANES] = rows[index * per_tile : (index + 1) * per_tile]
            ref[place, LANES:] = rows[(index + 1) * per_tile : (index + 2) * per_tile, : width - LANES]
    held = tok_ref.shape[0] // RING
    half = held // 2
    for copy in copies:
        copy.wait()
    for index, (rows_ref, ref) in enumerate(
        ((tok_ref, gate_ref), (tok_ref, up_ref), (scaled_ref, down_ref))
    ):
        columns = slice(index * hidden, (index + 1) * hidden)
        for step, pieces in (
            (RING // 2, ((to_right_ref, 0), (to_left_ref, half))),
            (1, ((next_ref, 0), (to_right_ref, half))),
            (RING - 1, ((to_left_ref, 0), (previous_ref, 0))),
            (0, ((own_ref, 0), (own_ref, half))),
        ):
            member = (place_ref[0] + step) & (RING - 1)
            begin = pl.multiple_of(member * held, held)
            value = dot(rows_ref[pl.ds(begin, held)], ref[...]).astype(BF16)
            for part, (out_ref, start) in enumerate(pieces):
                out_ref[start : start + half, columns] = value[part * half : (part + 1) * half]


def relay_kernel(next_ref, previous_ref, from_left_ref, from_right_ref, to_right_ref, to_left_ref):
    half = next_ref.shape[0]
    to_right_ref[...] = (next_ref[...].astype(F32) + from_left_ref[:half].astype(F32)).astype(BF16)
    to_left_ref[...] = (previous_ref[...].astype(F32) + from_right_ref[half:].astype(F32)).astype(BF16)


def window_kernel(own_ref, from_left_ref, from_right_ref, far_left_ref, far_right_ref, out_ref):
    half = far_left_ref.shape[0]
    out_ref[:half] = (
        own_ref[:half].astype(F32) + from_right_ref[:half].astype(F32) + far_left_ref[...].astype(F32)
    ).astype(BF16)
    out_ref[half:] = (
        own_ref[half:].astype(F32) + from_left_ref[half:].astype(F32) + far_right_ref[...].astype(F32)
    ).astype(BF16)


def middle_kernel(sum_ref, out_ref):
    hidden = sum_ref.shape[1] // 3
    share = out_ref.shape[0]

    def summed(index):
        values = sum_ref[:, index * hidden : (index + 1) * hidden].astype(F32)
        return sum(values[i * share : (i + 1) * share] for i in range(sum_ref.shape[0] // share))

    gate, up, grad = summed(0), summed(1), summed(2)
    sigmoid = jax.nn.sigmoid(gate)
    gated = gate * sigmoid
    hidden_value = (gated * up).astype(BF16)
    out_ref[:, :hidden] = hidden_value
    out_ref[:, hidden : 2 * hidden] = (grad * up * sigmoid * (1.0 + gate * (1.0 - sigmoid))).astype(BF16)
    out_ref[:, 2 * hidden : 3 * hidden] = (grad * gated).astype(BF16)
    score = jnp.sum(hidden_value.astype(F32) * grad, axis=1, keepdims=True)
    lane = iota((gate.shape[0], LANES), 1)
    packed = jnp.zeros(lane.shape, F32)
    for index, part in enumerate(three_parts(score)):
        packed = jnp.where(lane == SCORE_LANE + index, part.astype(F32), packed)
    out_ref[:, 3 * hidden :] = packed.astype(BF16)


def gathered(full_ref, place_ref, own_ref, left_ref, right_ref, far_left_ref, far_right_ref):
    held = own_ref.shape[0]
    half = held // 2
    for ref, step, start in (
        (own_ref, 0, 0),
        (right_ref, 1, 0),
        (left_ref, RING - 1, 0),
        (far_left_ref, RING // 2, 0),
        (far_right_ref, RING // 2, half),
    ):
        member = (place_ref[0] + step) & (RING - 1)
        begin = pl.multiple_of(member * held + start, half)
        full_ref[pl.ds(begin, ref.shape[0])] = ref[...]


def gradient_kernel(
    place_ref,
    own_ref,
    left_ref,
    right_ref,
    far_left_ref,
    far_right_ref,
    tok_ref,
    scaled_ref,
    gate_ref,
    up_ref,
    down_ref,
    full_ref,
):
    hidden = gate_ref.shape[1]
    gathered(full_ref, place_ref, own_ref, left_ref, right_ref, far_left_ref, far_right_ref)
    for index, (rows_ref, out_ref) in enumerate(
        ((scaled_ref, down_ref), (tok_ref, gate_ref), (tok_ref, up_ref))
    ):
        columns = slice(index * hidden, (index + 1) * hidden)
        out_ref[...] = dot(rows_ref[...], full_ref[:, columns], CONTRACT_FIRST).astype(BF16)


def rows_kernel(
    place_ref,
    own_ref,
    left_ref,
    right_ref,
    far_left_ref,
    far_right_ref,
    gate_hbm,
    up_hbm,
    down_hbm,
    back_ref,
    full_ref,
    tiles_ref,
    gate_ref,
    up_ref,
    down_ref,
    sems,
):
    copies = fetch((gate_hbm, up_hbm, down_hbm), (gate_ref, up_ref, down_ref), sems)
    experts = back_ref.shape[0]
    width, hidden = gate_ref.shape
    block = SOURCES * GROUP
    per_tile = SOURCES * CAP
    gathered(full_ref, place_ref, own_ref, left_ref, right_ref, far_left_ref, far_right_ref)
    for copy in copies:
        copy.wait()
    out_rows = dot(full_ref[:, :hidden], down_ref[...], CONTRACT_LAST)
    in_rows = dot(full_ref[:, hidden : 2 * hidden], gate_ref[...], CONTRACT_LAST) + dot(
        full_ref[:, 2 * hidden : 3 * hidden], up_ref[...], CONTRACT_LAST
    )
    tiles_ref[0] = out_rows[:, :LANES]
    tiles_ref[1] = full_ref[:, 3 * hidden :].astype(F32)
    tiles_ref[1, :, : width - LANES] = out_rows[:, LANES:]
    tiles_ref[2] = in_rows[:, :LANES]
    tiles_ref[3] = jnp.zeros(tiles_ref.shape[1:], F32)
    tiles_ref[3, :, : width - LANES] = in_rows[:, LANES:]
    restore = reorder_matrix(iota((block, block), 1), iota((block, block), 0))
    for b in range(experts // SOURCES):
        place = slice(b * per_tile, (b + 1) * per_tile)
        stacked = tiles_ref[:, place].astype(BF16).reshape(block, LANES)
        back_ref[b * SOURCES : (b + 1) * SOURCES] = (
            dot(restore, stacked).astype(BF16).reshape(SOURCES, GROUP, LANES)
        )


def combine_kernel(back_ref, plan_ref, routes_ref, weight_ref, mixed_ref, input_ref, score_ref):
    top_count, token_count = routes_ref.shape
    experts = plan_ref.shape[0] // 2
    width = mixed_ref.shape[0]
    rows = experts * GROUP
    back = back_ref[...].reshape(rows, LANES)
    plan = plan_ref[...].T
    rank, scale = plan[:, :experts], plan[:, experts:]
    spread = one_zero(expert_of_row(iota((experts, rows), 1), iota((experts, rows), 0)))
    tile, slot = tile_and_slot(iota((token_count, rows), 1))
    taken = dot(rank.astype(BF16), spread) == slot.astype(F32)
    mixed = [jnp.zeros((token_count, LANES), F32) for _ in range(2)]
    for part in three_parts(scale):
        row_scale = dot(part, spread)
        for index in range(2):
            chosen = jnp.where(taken & (tile == index), row_scale, 0.0).astype(BF16)
            mixed[index] = mixed[index] + dot(chosen, back)
    for ref, low, high in (
        (mixed_ref, mixed[0], mixed[1]),
        (
            input_ref,
            dot(one_zero(taken & (tile == 2)), back),
            dot(one_zero(taken & (tile == 3)), back),
        ),
    ):
        ref[:LANES] = low.T.astype(BF16)
        ref[LANES:] = high.T[: width - LANES].astype(BF16)
    lane = iota((8, LANES), 1)
    score_lanes = one_zero((lane >= SCORE_LANE) & (lane < SCORE_LANE + 3))
    row_score = dot(score_lanes, back, CONTRACT_LAST)[:1]
    routed = jnp.where(taken & (tile == 1), row_score, 0.0)
    by_expert = sum(dot(spread, part, CONTRACT_LAST) for part in three_parts(routed))
    expert = iota((experts, token_count), 0)
    for k in range(top_count):
        hit = routes_ref[k : k + 1] == expert
        value = jnp.sum(jnp.where(hit, by_expert, 0.0), axis=0, keepdims=True)
        score_ref[k : k + 1] = value / weight_ref[k : k + 1]


def kernel_call(body, out_shape, flops, moved, spaces=None, scratch=()):
    places = {}
    if spaces is not None:
        kinds = {"s": pltpu.SMEM, "v": pltpu.VMEM, "a": pl.ANY}
        places["in_specs"] = [pl.BlockSpec(memory_space=kinds[kind]) for kind in spaces]
    return pl.pallas_call(
        body,
        out_shape=out_shape,
        scratch_shapes=scratch,
        compiler_params=pltpu.CompilerParams(vmem_limit_bytes=VMEM_LIMIT),
        cost_estimate=pl.CostEstimate(flops=flops, bytes_accessed=moved, transcendentals=0),
        **places,
    )


def held_copies(*arrays):
    return [pltpu.VMEM(array.shape, array.dtype) for array in arrays] + [
        pltpu.SemaphoreType.DMA((len(arrays),))
    ]


def shifted(block, distance):
    parts = lax.axis_size("expert")
    return lax.ppermute(block, "expert", [(i, (i + distance) % parts) for i in range(parts)])


def per_device(
    tokens, cotangent, routes, route_weights, owner_slots, gate_weight, up_weight, down_weight
):
    experts = lax.axis_size("dp")
    parts = lax.axis_size("expert")
    token_count, width = tokens.shape
    hidden = gate_weight.shape[2]
    row_count = experts * CAP
    held = row_count // RING
    shape = jax.ShapeDtypeStruct
    exchanged = shape((experts, GROUP, LANES), BF16)
    rows = shape((row_count, width), BF16)
    whole, halved = (shape((size, 3 * hidden), BF16) for size in (held, held // 2))
    groups = [list(range(i, parts, RING)) for i in range(RING)]
    member = (lax.axis_index("expert") % RING).astype(jnp.int32).reshape(1)
    weights = (gate_weight[0], up_weight[0], down_weight[0].T)
    arguments = (routes.T, route_weights.T, owner_slots.reshape(1, experts), tokens.T, cotangent.T)
    send, plan = kernel_call(
        dispatch_kernel,
        (exchanged, shape((2 * experts, token_count), F32)),
        300_000_000,
        1_000_000,
        spaces="aaaaa",
        scratch=held_copies(*arguments),
    )(*arguments)
    arrived = lax.all_to_all(send, "dp", split_axis=0, concat_axis=0, tiled=True)
    own, to_right, to_left, following, previous, token_rows, scaled_rows = kernel_call(
        partial_kernel,
        (whole, whole, whole, halved, halved, rows, rows),
        700_000_000,
        4_500_000,
        spaces="svaaa",
        scratch=held_copies(*weights),
    )(member, arrived, *weights)
    from_left, from_right = shifted(to_right, 1), shifted(to_left, -1)
    relay_right, relay_left = kernel_call(relay_kernel, (halved, halved), 300_000, 1_500_000)(
        following, previous, from_left, from_right
    )
    far_left, far_right = shifted(relay_right, 1), shifted(relay_left, -1)
    window = kernel_call(window_kernel, whole, 600_000, 2_000_000)(
        own, from_left, from_right, far_left, far_right
    )
    summands = lax.all_to_all(
        window, "expert", split_axis=0, concat_axis=0, tiled=True, axis_index_groups=groups
    )
    share = kernel_call(
        middle_kernel, shape((row_count // parts, 3 * hidden + LANES), BF16), 1_000_000, 700_000
    )(summands)
    own = lax.all_gather(share, "expert", axis=0, tiled=True, axis_index_groups=groups)
    half = held // 2
    left, right = shifted(own, 1), shifted(own, -1)
    pieces = (own, left, right, shifted(left[:half], 1), shifted(right[half:], -1))
    full = pltpu.VMEM((row_count, 3 * hidden + LANES), BF16)
    back = kernel_call(
        rows_kernel,
        exchanged,
        700_000_000,
        4_500_000,
        spaces="svvvvvaaa",
        scratch=[full, pltpu.VMEM((TILES, row_count, LANES), F32)] + held_copies(*weights),
    )(member, *pieces, *weights)
    returned = lax.all_to_all(back, "dp", split_axis=0, concat_axis=0, tiled=True)
    matrix = shape((width, hidden), BF16)
    gate_grad, up_grad, down_grad = kernel_call(
        gradient_kernel,
        (matrix, matrix, matrix),
        700_000_000,
        4_500_000,
        spaces="svvvvvvv",
        scratch=[full],
    )(member, *pieces, token_rows, scaled_rows)
    down_grad = down_grad.T
    token_shape = shape((width, token_count), BF16)
    mixed, input_gradient, route_gradient = kernel_call(
        combine_kernel,
        (token_shape, token_shape, shape(arguments[0].shape, F32)),
        500_000_000,
        1_000_000,
    )(returned, plan, arguments[0], arguments[1])
    return (
        mixed.T,
        input_gradient.T,
        route_gradient.T,
        gate_grad[None],
        up_grad[None],
        down_grad[None],
    )


def solution(mesh):
    return jax.shard_map(
        per_device,
        mesh=mesh,
        in_specs=(
            P("dp", "expert"),
            P("dp", "expert"),
            P("dp", None),
            P("dp", None),
            P(),
            P("dp", "expert", None),
            P("dp", "expert", None),
            P("dp", None, "expert"),
        ),
        out_specs=(
            P("dp", "expert"),
            P("dp", "expert"),
            P("dp", None),
            P("dp", "expert", None),
            P("dp", "expert", None),
            P("dp", None, "expert"),
        ),
        check_vma=False,
    )
```

```python
import jax
import jax.numpy as jnp
from jax import lax
from jax.experimental import pallas as pl
from jax.experimental.pallas import tpu as pltpu
from jax.sharding import PartitionSpec as P

CAP = 6
SPARE = 2
LANES = 128
TILES = 4
GROUP = CAP * TILES
SOURCES = 16
RING = 4
SCORE_LANE = 96
VMEM_LIMIT = 24 * 1024 * 1024
WHOLE_VMEM = 63 * 1024 * 1024

F32 = jnp.float32
BF16 = jnp.bfloat16
CONTRACT_LAST = (((1,), (1,)), ((), ()))
CONTRACT_FIRST = (((0,), (0,)), ((), ()))


def dot(left, right, dims=(((1,), (0,)), ((), ()))):
    return lax.dot_general(left, right, dims, preferred_element_type=F32)


def one_zero(condition):
    return jnp.where(condition, 1.0, 0.0).astype(BF16)


def three_parts(value):
    high = value.astype(BF16)
    rest = value - high.astype(F32)
    middle = rest.astype(BF16)
    return high, middle, (rest - middle.astype(F32)).astype(BF16)


def iota(shape, axis):
    return lax.broadcasted_iota(jnp.int32, shape, axis)


def expert_of_row(row, expert):
    offset = row - GROUP * expert
    return (offset >= 0) & (offset < GROUP)


def tile_and_slot(row):
    place = row - GROUP * lax.shift_right_logical(row * 2731, 16)
    tile = (
        (place >= CAP).astype(jnp.int32)
        + (place >= 2 * CAP).astype(jnp.int32)
        + (place >= 3 * CAP).astype(jnp.int32)
    )
    return tile, place - CAP * tile


def reorder_matrix(sorted_row, sent_row):
    per_tile = SOURCES * CAP
    tile = (
        (sorted_row >= per_tile).astype(jnp.int32)
        + (sorted_row >= 2 * per_tile).astype(jnp.int32)
        + (sorted_row >= 3 * per_tile).astype(jnp.int32)
    )
    within = sorted_row - per_tile * tile
    source = lax.shift_right_logical(within * 43, 8)
    return one_zero(sent_row == within + (GROUP - CAP) * source + CAP * tile)


def fetch(sources, targets, sems):
    copies = [
        pltpu.make_async_copy(source, target, sems.at[i])
        for i, (source, target) in enumerate(zip(sources, targets))
    ]
    for copy in copies:
        copy.start()
    return copies


def dispatch_kernel(
    routes_hbm,
    weight_hbm,
    slots_hbm,
    tok_hbm,
    cot_hbm,
    send_ref,
    plan_ref,
    routes_ref,
    weight_ref,
    slots_ref,
    tok_ref,
    cot_ref,
    sems,
):
    arguments = (routes_hbm, weight_hbm, slots_hbm, tok_hbm, cot_hbm)
    held = (routes_ref, weight_ref, slots_ref, tok_ref, cot_ref)
    for copy in fetch(arguments, held, sems):
        copy.wait()
    top_count, token_count = routes_ref.shape
    experts = slots_ref.shape[1]
    rows = experts * GROUP
    expert = iota((experts, token_count), 0)
    named = jnp.zeros((experts, token_count), F32)
    scale = jnp.zeros((experts, token_count), F32)
    for k in range(top_count):
        hit = routes_ref[k : k + 1] == expert
        named = named + jnp.where(hit, 1.0, 0.0)
        scale = scale + jnp.where(hit, weight_ref[k : k + 1], 0.0)
    earlier = one_zero(iota((token_count, token_count), 0) < iota((token_count, token_count), 1))
    rank = dot(named.astype(BF16), earlier)
    diagonal = iota((experts, experts), 0) == iota((experts, experts), 1)
    limit = jnp.sum(jnp.where(diagonal, slots_ref[...].astype(F32), 0.0), axis=1, keepdims=True)
    rank = jnp.where((named > 0.0) & (rank < limit + float(SPARE)), rank, -1.0)
    plan_ref[:experts] = rank
    plan_ref[experts:] = scale
    spread = one_zero(expert_of_row(iota((rows, experts), 0), iota((rows, experts), 1)))
    tile, slot = tile_and_slot(iota((rows, token_count), 0))
    taken = dot(spread, rank.astype(BF16)) == slot.astype(F32)
    row_scale = sum(dot(spread, part) for part in three_parts(scale))
    row_scale = jnp.sum(jnp.where(taken, row_scale, 0.0), axis=1, keepdims=True)
    row_scale = jnp.where(tile[:, :1] >= 2, row_scale, 1.0)
    width = tok_ref.shape[0]
    picked = jnp.zeros((rows, LANES), F32)
    for index, ref in ((0, tok_ref), (2, cot_ref)):
        high = jnp.concatenate(
            [ref[LANES:], jnp.zeros((2 * LANES - width, token_count), BF16)], axis=0
        )
        picked = picked + dot(one_zero(taken & (tile == index)), ref[:LANES], CONTRACT_LAST)
        picked = picked + dot(one_zero(taken & (tile == index + 1)), high, CONTRACT_LAST)
    send_ref[...] = (picked * row_scale).astype(BF16).reshape(send_ref.shape)


def partial_kernel(
    place_ref,
    recv_ref,
    gate_hbm,
    up_hbm,
    down_hbm,
    own_ref,
    to_right_ref,
    to_left_ref,
    next_ref,
    previous_ref,
    tok_ref,
    scaled_ref,
    gate_ref,
    up_ref,
    down_ref,
    sems,
):
    copies = fetch((gate_hbm, up_hbm, down_hbm), (gate_ref, up_ref, down_ref), sems)
    experts = recv_ref.shape[0]
    width, hidden = gate_ref.shape
    block = SOURCES * GROUP
    per_tile = SOURCES * CAP
    reorder = reorder_matrix(iota((block, block), 0), iota((block, block), 1))
    for b in range(experts // SOURCES):
        sent = recv_ref[b * SOURCES : (b + 1) * SOURCES].reshape(block, LANES)
        rows = dot(reorder, sent).astype(BF16)
        place = slice(b * per_tile, (b + 1) * per_tile)
        for ref, index in ((tok_ref, 0), (scaled_ref, 2)):
            ref[place, :LANES] = rows[index * per_tile : (index + 1) * per_tile]
            ref[place, LANES:] = rows[(index + 1) * per_tile : (index + 2) * per_tile, : width - LANES]
    held = tok_ref.shape[0] // RING
    half = held // 2
    for copy in copies:
        copy.wait()
    for index, (rows_ref, ref) in enumerate(
        ((tok_ref, gate_ref), (tok_ref, up_ref), (scaled_ref, down_ref))
    ):
        columns = slice(index * hidden, (index + 1) * hidden)
        for step, pieces in (
            (RING // 2, ((to_right_ref, 0), (to_left_ref, half))),
            (1, ((next_ref, 0), (to_right_ref, half))),
            (RING - 1, ((to_left_ref, 0), (previous_ref, 0))),
            (0, ((own_ref, 0), (own_ref, half))),
        ):
            member = (place_ref[0] + step) & (RING - 1)
            begin = pl.multiple_of(member * held, held)
            value = dot(rows_ref[pl.ds(begin, held)], ref[...]).astype(BF16)
            for part, (out_ref, start) in enumerate(pieces):
                out_ref[start : start + half, columns] = value[part * half : (part + 1) * half]


def relay_kernel(next_ref, previous_ref, from_left_ref, from_right_ref, to_right_ref, to_left_ref):
    half = next_ref.shape[0]
    to_right_ref[...] = (next_ref[...].astype(F32) + from_left_ref[:half].astype(F32)).astype(BF16)
    to_left_ref[...] = (previous_ref[...].astype(F32) + from_right_ref[half:].astype(F32)).astype(BF16)


def window_kernel(
    place_ref,
    own_ref,
    from_left_ref,
    from_right_ref,
    far_left_ref,
    far_right_ref,
    kept_ref,
    to_right_ref,
    to_left_ref,
    next_ref,
    previous_ref,
    window_ref,
):
    half = far_left_ref.shape[0]
    window_ref[:half] = (
        own_ref[:half].astype(F32) + from_right_ref[:half].astype(F32) + far_left_ref[...].astype(F32)
    )
    window_ref[half:] = (
        own_ref[half:].astype(F32) + from_left_ref[half:].astype(F32) + far_right_ref[...].astype(F32)
    )
    share, columns = kept_ref.shape
    split = columns // 2

    def chunk(step, part):
        member = (lax.shift_right_logical(place_ref[0], 2) + step) & (RING - 1)
        begin = pl.multiple_of(member * share, share)
        return window_ref[pl.ds(begin, share), part].astype(BF16)

    low, high = slice(0, split), slice(split, columns)
    kept_ref[...] = chunk(0, slice(0, columns))
    to_right_ref[:, low] = chunk(RING // 2, low)
    to_right_ref[:, high] = chunk(1, high)
    to_left_ref[:, low] = chunk(RING - 1, low)
    to_left_ref[:, high] = chunk(RING // 2, high)
    next_ref[...] = chunk(1, low)
    previous_ref[...] = chunk(RING - 1, high)


def second_relay_kernel(
    next_ref, previous_ref, from_left_ref, from_right_ref, to_right_ref, to_left_ref
):
    split = next_ref.shape[1]
    to_right_ref[...] = (next_ref[...].astype(F32) + from_left_ref[:, :split].astype(F32)).astype(BF16)
    to_left_ref[...] = (
        previous_ref[...].astype(F32) + from_right_ref[:, split:].astype(F32)
    ).astype(BF16)


def middle_kernel(
    kept_ref, from_left_ref, from_right_ref, far_left_ref, far_right_ref, out_ref, sum_ref
):
    hidden = kept_ref.shape[1] // 3
    split = far_left_ref.shape[1]
    sum_ref[:, :split] = (
        kept_ref[:, :split].astype(F32)
        + from_right_ref[:, :split].astype(F32)
        + far_left_ref[...].astype(F32)
    )
    sum_ref[:, split:] = (
        kept_ref[:, split:].astype(F32)
        + from_left_ref[:, split:].astype(F32)
        + far_right_ref[...].astype(F32)
    )
    gate, up, grad = (sum_ref[:, i * hidden : (i + 1) * hidden] for i in range(3))
    sigmoid = jax.nn.sigmoid(gate)
    gated = gate * sigmoid
    hidden_value = (gated * up).astype(BF16)
    out_ref[:, :hidden] = hidden_value
    out_ref[:, hidden : 2 * hidden] = (grad * up * sigmoid * (1.0 + gate * (1.0 - sigmoid))).astype(BF16)
    out_ref[:, 2 * hidden : 3 * hidden] = (grad * gated).astype(BF16)
    score = jnp.sum(hidden_value.astype(F32) * grad, axis=1, keepdims=True)
    lane = iota((gate.shape[0], LANES), 1)
    packed = jnp.zeros(lane.shape, F32)
    for index, part in enumerate(three_parts(score)):
        packed = jnp.where(lane == SCORE_LANE + index, part.astype(F32), packed)
    out_ref[:, 3 * hidden :] = packed.astype(BF16)


def gathered(full_ref, place_ref, own_ref, left_ref, right_ref, far_left_ref, far_right_ref):
    held = own_ref.shape[0]
    half = held // 2
    for ref, step, start in (
        (own_ref, 0, 0),
        (right_ref, 1, 0),
        (left_ref, RING - 1, 0),
        (far_left_ref, RING // 2, 0),
        (far_right_ref, RING // 2, half),
    ):
        member = (place_ref[0] + step) & (RING - 1)
        begin = pl.multiple_of(member * held + start, half)
        full_ref[pl.ds(begin, ref.shape[0])] = ref[...]


def gradient_kernel(
    place_ref,
    own_ref,
    left_ref,
    right_ref,
    far_left_ref,
    far_right_ref,
    tok_ref,
    scaled_ref,
    gate_ref,
    up_ref,
    down_ref,
    full_ref,
):
    hidden = gate_ref.shape[1]
    gathered(full_ref, place_ref, own_ref, left_ref, right_ref, far_left_ref, far_right_ref)
    for index, (rows_ref, out_ref) in enumerate(
        ((scaled_ref, down_ref), (tok_ref, gate_ref), (tok_ref, up_ref))
    ):
        columns = slice(index * hidden, (index + 1) * hidden)
        out_ref[...] = dot(rows_ref[...], full_ref[:, columns], CONTRACT_FIRST).astype(BF16)


def rows_kernel(
    place_ref,
    own_ref,
    left_ref,
    right_ref,
    far_left_ref,
    far_right_ref,
    gate_hbm,
    up_hbm,
    down_hbm,
    back_ref,
    full_ref,
    tiles_ref,
    gate_ref,
    up_ref,
    down_ref,
    sems,
):
    copies = fetch((gate_hbm, up_hbm, down_hbm), (gate_ref, up_ref, down_ref), sems)
    experts = back_ref.shape[0]
    width, hidden = gate_ref.shape
    block = SOURCES * GROUP
    per_tile = SOURCES * CAP
    gathered(full_ref, place_ref, own_ref, left_ref, right_ref, far_left_ref, far_right_ref)
    for copy in copies:
        copy.wait()
    out_rows = dot(full_ref[:, :hidden], down_ref[...], CONTRACT_LAST)
    in_rows = dot(full_ref[:, hidden : 2 * hidden], gate_ref[...], CONTRACT_LAST) + dot(
        full_ref[:, 2 * hidden : 3 * hidden], up_ref[...], CONTRACT_LAST
    )
    tiles_ref[0] = out_rows[:, :LANES]
    tiles_ref[1] = full_ref[:, 3 * hidden :].astype(F32)
    tiles_ref[1, :, : width - LANES] = out_rows[:, LANES:]
    tiles_ref[2] = in_rows[:, :LANES]
    tiles_ref[3] = jnp.zeros(tiles_ref.shape[1:], F32)
    tiles_ref[3, :, : width - LANES] = in_rows[:, LANES:]
    restore = reorder_matrix(iota((block, block), 1), iota((block, block), 0))
    for b in range(experts // SOURCES):
        place = slice(b * per_tile, (b + 1) * per_tile)
        stacked = tiles_ref[:, place].astype(BF16).reshape(block, LANES)
        back_ref[b * SOURCES : (b + 1) * SOURCES] = (
            dot(restore, stacked).astype(BF16).reshape(SOURCES, GROUP, LANES)
        )


def combine_kernel(back_ref, plan_ref, routes_ref, weight_ref, mixed_ref, input_ref, score_ref):
    top_count, token_count = routes_ref.shape
    experts = plan_ref.shape[0] // 2
    width = mixed_ref.shape[0]
    rows = experts * GROUP
    back = back_ref[...].reshape(rows, LANES)
    plan = plan_ref[...].T
    rank, scale = plan[:, :experts], plan[:, experts:]
    spread = one_zero(expert_of_row(iota((experts, rows), 1), iota((experts, rows), 0)))
    tile, slot = tile_and_slot(iota((token_count, rows), 1))
    taken = dot(rank.astype(BF16), spread) == slot.astype(F32)
    mixed = [jnp.zeros((token_count, LANES), F32) for _ in range(2)]
    for part in three_parts(scale):
        row_scale = dot(part, spread)
        for index in range(2):
            chosen = jnp.where(taken & (tile == index), row_scale, 0.0).astype(BF16)
            mixed[index] = mixed[index] + dot(chosen, back)
    for ref, low, high in (
        (mixed_ref, mixed[0], mixed[1]),
        (
            input_ref,
            dot(one_zero(taken & (tile == 2)), back),
            dot(one_zero(taken & (tile == 3)), back),
        ),
    ):
        ref[:LANES] = low.T.astype(BF16)
        ref[LANES:] = high.T[: width - LANES].astype(BF16)
    lane = iota((8, LANES), 1)
    score_lanes = one_zero((lane >= SCORE_LANE) & (lane < SCORE_LANE + 3))
    row_score = dot(score_lanes, back, CONTRACT_LAST)[:1]
    routed = jnp.where(taken & (tile == 1), row_score, 0.0)
    by_expert = sum(dot(spread, part, CONTRACT_LAST) for part in three_parts(routed))
    expert = iota((experts, token_count), 0)
    for k in range(top_count):
        hit = routes_ref[k : k + 1] == expert
        value = jnp.sum(jnp.where(hit, by_expert, 0.0), axis=0, keepdims=True)
        score_ref[k : k + 1] = value / weight_ref[k : k + 1]


def kernel_call(body, out_shape, flops, moved, spaces=None, scratch=(), limit=VMEM_LIMIT):
    places = {}
    if spaces is not None:
        kinds = {"s": pltpu.SMEM, "v": pltpu.VMEM, "h": pltpu.HBM}
        places["in_specs"] = [pl.BlockSpec(memory_space=kinds[kind]) for kind in spaces]
    return pl.pallas_call(
        body,
        out_shape=out_shape,
        scratch_shapes=scratch,
        compiler_params=pltpu.CompilerParams(vmem_limit_bytes=limit),
        cost_estimate=pl.CostEstimate(flops=flops, bytes_accessed=moved, transcendentals=0),
        **places,
    )


def held_copies(*arrays):
    return [pltpu.VMEM(array.shape, array.dtype) for array in arrays] + [
        pltpu.SemaphoreType.DMA((len(arrays),))
    ]


def shifted(block, distance):
    parts = lax.axis_size("expert")
    return lax.ppermute(block, "expert", [(i, (i + distance) % parts) for i in range(parts)])


def per_device(
    tokens, cotangent, routes, route_weights, owner_slots, gate_weight, up_weight, down_weight
):
    experts = lax.axis_size("dp")
    parts = lax.axis_size("expert")
    token_count, width = tokens.shape
    hidden = gate_weight.shape[2]
    row_count = experts * CAP
    held = row_count // RING
    shape = jax.ShapeDtypeStruct
    exchanged = shape((experts, GROUP, LANES), BF16)
    rows = shape((row_count, width), BF16)
    whole, halved = (shape((size, 3 * hidden), BF16) for size in (held, held // 2))
    groups = [list(range(i, parts, RING)) for i in range(RING)]
    member = lax.axis_index("expert").astype(jnp.int32).reshape(1)
    weights = (gate_weight[0], up_weight[0], down_weight[0].T)
    arguments = (routes.T, route_weights.T, owner_slots.reshape(1, experts), tokens.T, cotangent.T)
    send, plan = kernel_call(
        dispatch_kernel,
        (exchanged, shape((2 * experts, token_count), F32)),
        300_000_000,
        1_000_000,
        spaces="hhhhh",
        limit=WHOLE_VMEM,
        scratch=held_copies(*arguments),
    )(*arguments)
    arrived = lax.all_to_all(send, "dp", split_axis=0, concat_axis=0, tiled=True)
    own, to_right, to_left, following, previous, token_rows, scaled_rows = kernel_call(
        partial_kernel,
        (whole, whole, whole, halved, halved, rows, rows),
        700_000_000,
        4_500_000,
        spaces="svhhh",
        scratch=held_copies(*weights),
    )(member, arrived, *weights)
    from_left, from_right = shifted(to_right, 1), shifted(to_left, -1)
    relay_right, relay_left = kernel_call(relay_kernel, (halved, halved), 300_000, 1_500_000)(
        following, previous, from_left, from_right
    )
    far_left, far_right = shifted(relay_right, 1), shifted(relay_left, -1)
    chunk, chunk_half = (
        shape((row_count // parts, columns), BF16) for columns in (3 * hidden, 3 * hidden // 2)
    )
    kept, to_right, to_left, following, previous = kernel_call(
        window_kernel,
        (chunk, chunk, chunk, chunk_half, chunk_half),
        600_000,
        2_000_000,
        spaces="svvvvv",
        scratch=[pltpu.VMEM(whole.shape, F32)],
    )(member, own, from_left, from_right, far_left, far_right)
    from_left, from_right = shifted(to_right, RING), shifted(to_left, -RING)
    relay_right, relay_left = kernel_call(
        second_relay_kernel, (chunk_half, chunk_half), 100_000, 400_000
    )(following, previous, from_left, from_right)
    far_left, far_right = shifted(relay_right, RING), shifted(relay_left, -RING)
    share = kernel_call(
        middle_kernel,
        shape((row_count // parts, 3 * hidden + LANES), BF16),
        1_000_000,
        700_000,
        scratch=[pltpu.VMEM(chunk.shape, F32)],
    )(kept, from_left, from_right, far_left, far_right)
    own = lax.all_gather(share, "expert", axis=0, tiled=True, axis_index_groups=groups)
    half = held // 2
    left, right = shifted(own, 1), shifted(own, -1)
    pieces = (own, left, right, shifted(left[:half], 1), shifted(right[half:], -1))
    full = pltpu.VMEM((row_count, 3 * hidden + LANES), BF16)
    back = kernel_call(
        rows_kernel,
        exchanged,
        700_000_000,
        4_500_000,
        spaces="svvvvvhhh",
        scratch=[full, pltpu.VMEM((TILES, row_count, LANES), F32)] + held_copies(*weights),
    )(member, *pieces, *weights)
    returned = lax.all_to_all(back, "dp", split_axis=0, concat_axis=0, tiled=True)
    matrix = shape((width, hidden), BF16)
    gate_grad, up_grad, down_grad = kernel_call(
        gradient_kernel,
        (matrix, matrix, matrix),
        700_000_000,
        4_500_000,
        spaces="svvvvvvv",
        scratch=[full],
    )(member, *pieces, token_rows, scaled_rows)
    down_grad = down_grad.T
    token_shape = shape((width, token_count), BF16)
    mixed, input_gradient, route_gradient = kernel_call(
        combine_kernel,
        (token_shape, token_shape, shape(arguments[0].shape, F32)),
        500_000_000,
        1_000_000,
    )(returned, plan, arguments[0], arguments[1])
    return (
        mixed.T,
        input_gradient.T,
        route_gradient.T,
        gate_grad[None],
        up_grad[None],
        down_grad[None],
    )


def solution(mesh):
    return jax.shard_map(
        per_device,
        mesh=mesh,
        in_specs=(
            P("dp", "expert"),
            P("dp", "expert"),
            P("dp", None),
            P("dp", None),
            P(),
            P("dp", "expert", None),
            P("dp", "expert", None),
            P("dp", None, "expert"),
        ),
        out_specs=(
            P("dp", "expert"),
            P("dp", "expert"),
            P("dp", None),
            P("dp", "expert", None),
            P("dp", "expert", None),
            P("dp", None, "expert"),
        ),
        check_vma=False,
    )
```

```python
import jax
import jax.numpy as jnp
from jax import lax
from jax.experimental import pallas as pl
from jax.experimental.pallas import tpu as pltpu
from jax.sharding import PartitionSpec as P

CAP = 6
SPARE = 2
LANES = 128
TILES = 4
GROUP = CAP * TILES
SOURCES = 16
RING = 4
SCORE_LANE = 96
WEIGHT_PARTS = 2
VMEM_LIMIT = 24 * 1024 * 1024

F32 = jnp.float32
BF16 = jnp.bfloat16
CONTRACT_LAST = (((1,), (1,)), ((), ()))
CONTRACT_FIRST = (((0,), (0,)), ((), ()))


def dot(left, right, dims=(((1,), (0,)), ((), ()))):
    return lax.dot_general(left, right, dims, preferred_element_type=F32)


def one_zero(condition):
    return jnp.where(condition, 1.0, 0.0).astype(BF16)


def three_parts(value):
    high = value.astype(BF16)
    rest = value - high.astype(F32)
    middle = rest.astype(BF16)
    return high, middle, (rest - middle.astype(F32)).astype(BF16)


def iota(shape, axis):
    return lax.broadcasted_iota(jnp.int32, shape, axis)


def expert_of_row(row, expert):
    offset = row - GROUP * expert
    return (offset >= 0) & (offset < GROUP)


def tile_and_slot(row):
    place = row - GROUP * lax.shift_right_logical(row * 2731, 16)
    tile = (
        (place >= CAP).astype(jnp.int32)
        + (place >= 2 * CAP).astype(jnp.int32)
        + (place >= 3 * CAP).astype(jnp.int32)
    )
    return tile, place - CAP * tile


def reorder_matrix(sorted_row, sent_row):
    per_tile = SOURCES * CAP
    tile = (
        (sorted_row >= per_tile).astype(jnp.int32)
        + (sorted_row >= 2 * per_tile).astype(jnp.int32)
        + (sorted_row >= 3 * per_tile).astype(jnp.int32)
    )
    within = sorted_row - per_tile * tile
    source = lax.shift_right_logical(within * 43, 8)
    return one_zero(sent_row == within + (GROUP - CAP) * source + CAP * tile)


def fetch(sources, targets, sems):
    copies = [
        pltpu.make_async_copy(source, target, sems.at[i])
        for i, (source, target) in enumerate(zip(sources, targets))
    ]
    for copy in copies:
        copy.start()
    return copies


def dispatch_kernel(
    routes_hbm,
    weight_hbm,
    slots_hbm,
    tok_hbm,
    cot_hbm,
    send_ref,
    plan_ref,
    routes_ref,
    weight_ref,
    slots_ref,
    tok_ref,
    cot_ref,
    sems,
):
    arguments = (routes_hbm, weight_hbm, slots_hbm, tok_hbm, cot_hbm)
    held = (routes_ref, weight_ref, slots_ref, tok_ref, cot_ref)
    for copy in fetch(arguments, held, sems):
        copy.wait()
    top_count, token_count = routes_ref.shape
    experts = slots_ref.shape[1]
    rows = experts * GROUP
    expert = iota((experts, token_count), 0)
    named = jnp.zeros((experts, token_count), F32)
    scale = jnp.zeros((experts, token_count), F32)
    for k in range(top_count):
        hit = routes_ref[k : k + 1] == expert
        named = named + jnp.where(hit, 1.0, 0.0)
        scale = scale + jnp.where(hit, weight_ref[k : k + 1], 0.0)
    earlier = one_zero(iota((token_count, token_count), 0) < iota((token_count, token_count), 1))
    rank = dot(named.astype(BF16), earlier)
    diagonal = iota((experts, experts), 0) == iota((experts, experts), 1)
    limit = jnp.sum(jnp.where(diagonal, slots_ref[...].astype(F32), 0.0), axis=1, keepdims=True)
    rank = jnp.where((named > 0.0) & (rank < limit + float(SPARE)), rank, -1.0)
    plan_ref[:experts] = rank
    plan_ref[experts:] = scale
    spread = one_zero(expert_of_row(iota((rows, experts), 0), iota((rows, experts), 1)))
    tile, slot = tile_and_slot(iota((rows, token_count), 0))
    taken = dot(spread, rank.astype(BF16)) == slot.astype(F32)
    row_scale = sum(dot(spread, part) for part in three_parts(scale))
    row_scale = jnp.sum(jnp.where(taken, row_scale, 0.0), axis=1, keepdims=True)
    row_scale = jnp.where(tile[:, :1] >= 2, row_scale, 1.0)
    width = tok_ref.shape[0]
    picked = jnp.zeros((rows, LANES), F32)
    for index, ref in ((0, tok_ref), (2, cot_ref)):
        high = jnp.concatenate(
            [ref[LANES:], jnp.zeros((2 * LANES - width, token_count), BF16)], axis=0
        )
        picked = picked + dot(one_zero(taken & (tile == index)), ref[:LANES], CONTRACT_LAST)
        picked = picked + dot(one_zero(taken & (tile == index + 1)), high, CONTRACT_LAST)
    send_ref[...] = (picked * row_scale).astype(BF16).reshape(send_ref.shape)


def partial_kernel(
    place_ref,
    recv_ref,
    gate_hbm,
    up_hbm,
    down_hbm,
    own_ref,
    to_right_ref,
    to_left_ref,
    next_ref,
    previous_ref,
    tok_ref,
    scaled_ref,
    gate_ref,
    up_ref,
    down_ref,
    sems,
):
    copies = fetch((gate_hbm, up_hbm, down_hbm), (gate_ref, up_ref, down_ref), sems)
    experts = recv_ref.shape[0]
    width, hidden = gate_ref.shape
    block = SOURCES * GROUP
    per_tile = SOURCES * CAP
    reorder = reorder_matrix(iota((block, block), 0), iota((block, block), 1))
    for b in range(experts // SOURCES):
        sent = recv_ref[b * SOURCES : (b + 1) * SOURCES].reshape(block, LANES)
        rows = dot(reorder, sent).astype(BF16)
        place = slice(b * per_tile, (b + 1) * per_tile)
        for ref, index in ((tok_ref, 0), (scaled_ref, 2)):
            ref[place, :LANES] = rows[index * per_tile : (index + 1) * per_tile]
            ref[place, LANES:] = rows[(index + 1) * per_tile : (index + 2) * per_tile, : width - LANES]
    held = tok_ref.shape[0] // RING
    half = held // 2
    for copy in copies:
        copy.wait()
    for index, (rows_ref, ref) in enumerate(
        ((tok_ref, gate_ref), (tok_ref, up_ref), (scaled_ref, down_ref))
    ):
        columns = slice(index * hidden, (index + 1) * hidden)
        for step, pieces in (
            (RING // 2, ((to_right_ref, 0), (to_left_ref, half))),
            (1, ((next_ref, 0), (to_right_ref, half))),
            (RING - 1, ((to_left_ref, 0), (previous_ref, 0))),
            (0, ((own_ref, 0), (own_ref, half))),
        ):
            member = (place_ref[0] + step) & (RING - 1)
            begin = pl.multiple_of(member * held, held)
            value = dot(rows_ref[pl.ds(begin, held)], ref[...]).astype(BF16)
            for part, (out_ref, start) in enumerate(pieces):
                out_ref[start : start + half, columns] = value[part * half : (part + 1) * half]


def relay_kernel(next_ref, previous_ref, from_left_ref, from_right_ref, to_right_ref, to_left_ref):
    half = next_ref.shape[0]
    to_right_ref[...] = (next_ref[...].astype(F32) + from_left_ref[:half].astype(F32)).astype(BF16)
    to_left_ref[...] = (previous_ref[...].astype(F32) + from_right_ref[half:].astype(F32)).astype(BF16)


def window_kernel(
    place_ref,
    own_ref,
    from_left_ref,
    from_right_ref,
    far_left_ref,
    far_right_ref,
    kept_ref,
    to_right_ref,
    to_left_ref,
    across_ref,
    window_ref,
):
    half = far_left_ref.shape[0]
    window_ref[:half] = (
        own_ref[:half].astype(F32) + from_right_ref[:half].astype(F32) + far_left_ref[...].astype(F32)
    )
    window_ref[half:] = (
        own_ref[half:].astype(F32) + from_left_ref[half:].astype(F32) + far_right_ref[...].astype(F32)
    )
    share = kept_ref.shape[0]
    for step, ref in ((1, to_right_ref), (RING - 1, to_left_ref), (RING // 2, across_ref), (0, kept_ref)):
        member = (lax.shift_right_logical(place_ref[0], 2) + step) & (RING - 1)
        begin = pl.multiple_of(member * share, share)
        ref[...] = window_ref[pl.ds(begin, share)].astype(BF16)


def middle_kernel(kept_ref, from_left_ref, from_right_ref, across_ref, out_ref):
    hidden = kept_ref.shape[1] // 3

    def summed(index):
        columns = slice(index * hidden, (index + 1) * hidden)
        refs = (kept_ref, from_left_ref, from_right_ref, across_ref)
        return sum(ref[:, columns].astype(F32) for ref in refs)

    gate, up, grad = summed(0), summed(1), summed(2)
    sigmoid = jax.nn.sigmoid(gate)
    gated = gate * sigmoid
    hidden_value = (gated * up).astype(BF16)
    out_ref[:, :hidden] = hidden_value
    out_ref[:, hidden : 2 * hidden] = (grad * up * sigmoid * (1.0 + gate * (1.0 - sigmoid))).astype(BF16)
    out_ref[:, 2 * hidden : 3 * hidden] = (grad * gated).astype(BF16)
    score = jnp.sum(hidden_value.astype(F32) * grad, axis=1, keepdims=True)
    lane = iota((gate.shape[0], LANES), 1)
    packed = jnp.zeros(lane.shape, F32)
    for index, part in enumerate(three_parts(score)):
        packed = jnp.where(lane == SCORE_LANE + index, part.astype(F32), packed)
    out_ref[:, 3 * hidden :] = packed.astype(BF16)


def gathered(full_ref, place_ref, own_ref, left_ref, right_ref, far_left_ref, far_right_ref):
    held = own_ref.shape[0]
    half = held // 2
    for ref, step, start in (
        (own_ref, 0, 0),
        (right_ref, 1, 0),
        (left_ref, RING - 1, 0),
        (far_left_ref, RING // 2, 0),
        (far_right_ref, RING // 2, half),
    ):
        member = (place_ref[0] + step) & (RING - 1)
        begin = pl.multiple_of(member * held + start, half)
        full_ref[pl.ds(begin, ref.shape[0])] = ref[...]


def gradient_kernel(
    place_ref,
    own_ref,
    left_ref,
    right_ref,
    far_left_ref,
    far_right_ref,
    tok_ref,
    scaled_ref,
    gate_ref,
    up_ref,
    down_ref,
    full_ref,
):
    hidden = gate_ref.shape[1]
    gathered(full_ref, place_ref, own_ref, left_ref, right_ref, far_left_ref, far_right_ref)
    for index, (rows_ref, out_ref) in enumerate(
        ((scaled_ref, down_ref), (tok_ref, gate_ref), (tok_ref, up_ref))
    ):
        columns = slice(index * hidden, (index + 1) * hidden)
        out_ref[...] = dot(rows_ref[...], full_ref[:, columns], CONTRACT_FIRST).astype(BF16)


def rows_kernel(
    place_ref,
    own_ref,
    left_ref,
    right_ref,
    far_left_ref,
    far_right_ref,
    gate_hbm,
    up_hbm,
    down_hbm,
    back_ref,
    full_ref,
    tiles_ref,
    gate_ref,
    up_ref,
    down_ref,
    sems,
):
    copies = fetch((gate_hbm, up_hbm, down_hbm), (gate_ref, up_ref, down_ref), sems)
    experts = back_ref.shape[0]
    width, hidden = gate_ref.shape
    block = SOURCES * GROUP
    per_tile = SOURCES * CAP
    gathered(full_ref, place_ref, own_ref, left_ref, right_ref, far_left_ref, far_right_ref)
    for copy in copies:
        copy.wait()
    out_rows = dot(full_ref[:, :hidden], down_ref[...], CONTRACT_LAST)
    in_rows = dot(full_ref[:, hidden : 2 * hidden], gate_ref[...], CONTRACT_LAST) + dot(
        full_ref[:, 2 * hidden : 3 * hidden], up_ref[...], CONTRACT_LAST
    )
    tiles_ref[0] = out_rows[:, :LANES]
    tiles_ref[1] = full_ref[:, 3 * hidden :].astype(F32)
    tiles_ref[1, :, : width - LANES] = out_rows[:, LANES:]
    tiles_ref[2] = in_rows[:, :LANES]
    tiles_ref[3] = jnp.zeros(tiles_ref.shape[1:], F32)
    tiles_ref[3, :, : width - LANES] = in_rows[:, LANES:]
    restore = reorder_matrix(iota((block, block), 1), iota((block, block), 0))
    for b in range(experts // SOURCES):
        place = slice(b * per_tile, (b + 1) * per_tile)
        stacked = tiles_ref[:, place].astype(BF16).reshape(block, LANES)
        back_ref[b * SOURCES : (b + 1) * SOURCES] = (
            dot(restore, stacked).astype(BF16).reshape(SOURCES, GROUP, LANES)
        )


def choose_kernel(plan_ref, chosen_ref, scored_ref):
    experts = plan_ref.shape[0] // 2
    token_count = plan_ref.shape[1]
    rows = experts * GROUP
    plan = plan_ref[...].T
    rank, scale = plan[:, :experts], plan[:, experts:]
    spread = one_zero(expert_of_row(iota((experts, rows), 1), iota((experts, rows), 0)))
    tile, slot = tile_and_slot(iota((1, rows), 1))
    taken = dot(rank.astype(BF16), spread) == slot.astype(F32)
    for order, part in enumerate(three_parts(scale)[:WEIGHT_PARTS]):
        row_scale = jnp.where(taken, dot(part, spread), 0.0)
        for index in range(2):
            place = (index * WEIGHT_PARTS + order) * token_count
            chosen_ref[place : place + token_count] = jnp.where(tile == index, row_scale, 0.0).astype(BF16)
    taken = jnp.where(taken, 1.0, 0.0)
    for index in range(2):
        place = (2 * WEIGHT_PARTS + index) * token_count
        chosen_ref[place : place + token_count] = jnp.where(tile == 2 + index, taken, 0.0).astype(BF16)
    scored_ref[...] = jnp.where(tile == 1, taken, 0.0).astype(BF16)


def combine_kernel(
    back_ref, chosen_ref, scored_ref, routes_ref, weight_ref, mixed_ref, input_ref, score_ref
):
    top_count, token_count = routes_ref.shape
    experts = back_ref.shape[0]
    width = mixed_ref.shape[0]
    rows = experts * GROUP
    back = back_ref[...].reshape(rows, LANES)
    values = dot(chosen_ref[...], back)
    blocks = [values[i * token_count : (i + 1) * token_count] for i in range(2 * WEIGHT_PARTS + 2)]
    low, high = sum(blocks[:WEIGHT_PARTS]), sum(blocks[WEIGHT_PARTS : 2 * WEIGHT_PARTS])
    for ref, low, high in (
        (mixed_ref, low, high),
        (input_ref, blocks[2 * WEIGHT_PARTS], blocks[2 * WEIGHT_PARTS + 1]),
    ):
        ref[:LANES] = low.T.astype(BF16)
        ref[LANES:] = high.T[: width - LANES].astype(BF16)
    lane_of_part = iota((8, LANES), 1) - SCORE_LANE == iota((8, LANES), 0)
    row_score = dot(one_zero(lane_of_part & (iota((8, LANES), 0) < 3)), back, CONTRACT_LAST)
    here = expert_of_row(iota((experts, rows), 1), iota((experts, rows), 0))
    spread = jnp.concatenate(
        [jnp.where(here, row_score[i : i + 1], 0.0).astype(BF16) for i in range(3)], axis=0
    )
    by_expert = dot(spread, scored_ref[...], CONTRACT_LAST)
    by_expert = sum(by_expert[i * experts : (i + 1) * experts] for i in range(3))
    expert = iota((experts, token_count), 0)
    for k in range(top_count):
        hit = routes_ref[k : k + 1] == expert
        value = jnp.sum(jnp.where(hit, by_expert, 0.0), axis=0, keepdims=True)
        score_ref[k : k + 1] = value / weight_ref[k : k + 1]


def kernel_call(body, out_shape, flops, moved, spaces=None, scratch=()):
    places = {}
    if spaces is not None:
        kinds = {"s": pltpu.SMEM, "v": pltpu.VMEM, "a": pl.ANY}
        places["in_specs"] = [pl.BlockSpec(memory_space=kinds[kind]) for kind in spaces]
    return pl.pallas_call(
        body,
        out_shape=out_shape,
        scratch_shapes=scratch,
        compiler_params=pltpu.CompilerParams(vmem_limit_bytes=VMEM_LIMIT),
        cost_estimate=pl.CostEstimate(flops=flops, bytes_accessed=moved, transcendentals=0),
        **places,
    )


def held_copies(*arrays):
    return [pltpu.VMEM(array.shape, array.dtype) for array in arrays] + [
        pltpu.SemaphoreType.DMA((len(arrays),))
    ]


def shifted(block, distance):
    parts = lax.axis_size("expert")
    return lax.ppermute(block, "expert", [(i, (i + distance) % parts) for i in range(parts)])


def per_device(
    tokens, cotangent, routes, route_weights, owner_slots, gate_weight, up_weight, down_weight
):
    experts = lax.axis_size("dp")
    parts = lax.axis_size("expert")
    token_count, width = tokens.shape
    hidden = gate_weight.shape[2]
    row_count = experts * CAP
    held = row_count // RING
    shape = jax.ShapeDtypeStruct
    exchanged = shape((experts, GROUP, LANES), BF16)
    rows = shape((row_count, width), BF16)
    whole, halved = (shape((size, 3 * hidden), BF16) for size in (held, held // 2))
    groups = [list(range(i, parts, RING)) for i in range(RING)]
    member = lax.axis_index("expert").astype(jnp.int32).reshape(1)
    weights = (gate_weight[0], up_weight[0], down_weight[0].T)
    arguments = (routes.T, route_weights.T, owner_slots.reshape(1, experts), tokens.T, cotangent.T)
    send, plan = kernel_call(
        dispatch_kernel,
        (exchanged, shape((2 * experts, token_count), F32)),
        300_000_000,
        1_000_000,
        spaces="aaaaa",
        scratch=held_copies(*arguments),
    )(*arguments)
    arrived = lax.all_to_all(send, "dp", split_axis=0, concat_axis=0, tiled=True)
    own, to_right, to_left, following, previous, token_rows, scaled_rows = kernel_call(
        partial_kernel,
        (whole, whole, whole, halved, halved, rows, rows),
        700_000_000,
        4_500_000,
        spaces="svaaa",
        scratch=held_copies(*weights),
    )(member, arrived, *weights)
    from_left, from_right = shifted(to_right, 1), shifted(to_left, -1)
    relay_right, relay_left = kernel_call(relay_kernel, (halved, halved), 300_000, 1_500_000)(
        following, previous, from_left, from_right
    )
    far_left, far_right = shifted(relay_right, 1), shifted(relay_left, -1)
    chunk = shape((row_count // parts, 3 * hidden), BF16)
    kept, to_right, to_left, across = kernel_call(
        window_kernel,
        (chunk, chunk, chunk, chunk),
        600_000,
        2_000_000,
        spaces="svvvvv",
        scratch=[pltpu.VMEM(whole.shape, F32)],
    )(member, own, from_left, from_right, far_left, far_right)
    share = kernel_call(
        middle_kernel, shape((row_count // parts, 3 * hidden + LANES), BF16), 1_000_000, 700_000
    )(
        kept,
        shifted(to_right, RING),
        shifted(to_left, -RING),
        shifted(across, parts // 2),
    )
    own = lax.all_gather(share, "expert", axis=0, tiled=True, axis_index_groups=groups)
    half = held // 2
    left, right = shifted(own, 1), shifted(own, -1)
    pieces = (own, left, right, shifted(left[:half], 1), shifted(right[half:], -1))
    full = pltpu.VMEM((row_count, 3 * hidden + LANES), BF16)
    back = kernel_call(
        rows_kernel,
        exchanged,
        700_000_000,
        4_500_000,
        spaces="svvvvvaaa",
        scratch=[full, pltpu.VMEM((TILES, row_count, LANES), F32)] + held_copies(*weights),
    )(member, *pieces, *weights)
    returned = lax.all_to_all(back, "dp", split_axis=0, concat_axis=0, tiled=True)
    matrix = shape((width, hidden), BF16)
    gate_grad, up_grad, down_grad = kernel_call(
        gradient_kernel,
        (matrix, matrix, matrix),
        700_000_000,
        4_500_000,
        spaces="svvvvvvv",
        scratch=[full],
    )(member, *pieces, token_rows, scaled_rows)
    down_grad = down_grad.T
    token_shape = shape((width, token_count), BF16)
    slots = experts * GROUP
    chosen, scored = kernel_call(
        choose_kernel,
        (
            shape(((2 * WEIGHT_PARTS + 2) * token_count, slots), BF16),
            shape((token_count, slots), BF16),
        ),
        200_000_000,
        3_000_000,
    )(plan)
    mixed, input_gradient, route_gradient = kernel_call(
        combine_kernel,
        (token_shape, token_shape, shape(arguments[0].shape, F32)),
        500_000_000,
        1_000_000,
    )(returned, chosen, scored, arguments[0], arguments[1])
    return (
        mixed.T,
        input_gradient.T,
        route_gradient.T,
        gate_grad[None],
        up_grad[None],
        down_grad[None],
    )


def solution(mesh):
    return jax.shard_map(
        per_device,
        mesh=mesh,
        in_specs=(
            P("dp", "expert"),
            P("dp", "expert"),
            P("dp", None),
            P("dp", None),
            P(),
            P("dp", "expert", None),
            P("dp", "expert", None),
            P("dp", None, "expert"),
        ),
        out_specs=(
            P("dp", "expert"),
            P("dp", "expert"),
            P("dp", None),
            P("dp", "expert", None),
            P("dp", "expert", None),
            P("dp", None, "expert"),
        ),
        check_vma=False,
    )
```

```python
import jax
import jax.numpy as jnp
from jax import lax
from jax.experimental import pallas as pl
from jax.experimental.pallas import tpu as pltpu
from jax.sharding import PartitionSpec as P

CAP = 6
SPARE = 2
LANES = 128
TILES = 4
GROUP = CAP * TILES
SOURCES = 16
RING = 4
SCORE_LANE = 96
WEIGHT_PARTS = 2
VMEM_LIMIT = 24 * 1024 * 1024

F32 = jnp.float32
BF16 = jnp.bfloat16
CONTRACT_LAST = (((1,), (1,)), ((), ()))
CONTRACT_FIRST = (((0,), (0,)), ((), ()))


def dot(left, right, dims=(((1,), (0,)), ((), ()))):
    return lax.dot_general(left, right, dims, preferred_element_type=F32)


def one_zero(condition):
    return jnp.where(condition, 1.0, 0.0).astype(BF16)


def three_parts(value):
    high = value.astype(BF16)
    rest = value - high.astype(F32)
    middle = rest.astype(BF16)
    return high, middle, (rest - middle.astype(F32)).astype(BF16)


def iota(shape, axis):
    return lax.broadcasted_iota(jnp.int32, shape, axis)


def expert_of_row(row, expert):
    offset = row - GROUP * expert
    return (offset >= 0) & (offset < GROUP)


def tile_and_slot(row):
    place = row - GROUP * lax.shift_right_logical(row * 2731, 16)
    tile = (
        (place >= CAP).astype(jnp.int32)
        + (place >= 2 * CAP).astype(jnp.int32)
        + (place >= 3 * CAP).astype(jnp.int32)
    )
    return tile, place - CAP * tile


def reorder_matrix(sorted_row, sent_row):
    per_tile = SOURCES * CAP
    tile = (
        (sorted_row >= per_tile).astype(jnp.int32)
        + (sorted_row >= 2 * per_tile).astype(jnp.int32)
        + (sorted_row >= 3 * per_tile).astype(jnp.int32)
    )
    within = sorted_row - per_tile * tile
    source = lax.shift_right_logical(within * 43, 8)
    return one_zero(sent_row == within + (GROUP - CAP) * source + CAP * tile)


def fetch(sources, targets, sems):
    copies = [
        pltpu.make_async_copy(source, target, sems.at[i])
        for i, (source, target) in enumerate(zip(sources, targets))
    ]
    for copy in copies:
        copy.start()
    return copies


def dispatch_kernel(
    routes_hbm,
    weight_hbm,
    slots_hbm,
    tok_hbm,
    cot_hbm,
    send_ref,
    plan_ref,
    routes_ref,
    weight_ref,
    slots_ref,
    tok_ref,
    cot_ref,
    sems,
):
    arguments = (routes_hbm, weight_hbm, slots_hbm, tok_hbm, cot_hbm)
    held = (routes_ref, weight_ref, slots_ref, tok_ref, cot_ref)
    for copy in fetch(arguments, held, sems):
        copy.wait()
    top_count, token_count = routes_ref.shape
    experts = slots_ref.shape[1]
    rows = experts * GROUP
    expert = iota((experts, token_count), 0)
    named = jnp.zeros((experts, token_count), F32)
    scale = jnp.zeros((experts, token_count), F32)
    for k in range(top_count):
        hit = routes_ref[k : k + 1] == expert
        named = named + jnp.where(hit, 1.0, 0.0)
        scale = scale + jnp.where(hit, weight_ref[k : k + 1], 0.0)
    earlier = one_zero(iota((token_count, token_count), 0) < iota((token_count, token_count), 1))
    rank = dot(named.astype(BF16), earlier)
    diagonal = iota((experts, experts), 0) == iota((experts, experts), 1)
    limit = jnp.sum(jnp.where(diagonal, slots_ref[...].astype(F32), 0.0), axis=1, keepdims=True)
    rank = jnp.where((named > 0.0) & (rank < limit + float(SPARE)), rank, -1.0)
    plan_ref[:experts] = rank
    plan_ref[experts:] = scale
    spread = one_zero(expert_of_row(iota((rows, experts), 0), iota((rows, experts), 1)))
    tile, slot = tile_and_slot(iota((rows, token_count), 0))
    taken = dot(spread, rank.astype(BF16)) == slot.astype(F32)
    row_scale = sum(dot(spread, part) for part in three_parts(scale))
    row_scale = jnp.sum(jnp.where(taken, row_scale, 0.0), axis=1, keepdims=True)
    row_scale = jnp.where(tile[:, :1] >= 2, row_scale, 1.0)
    width = tok_ref.shape[0]
    picked = jnp.zeros((rows, LANES), F32)
    for index, ref in ((0, tok_ref), (2, cot_ref)):
        high = jnp.concatenate(
            [ref[LANES:], jnp.zeros((2 * LANES - width, token_count), BF16)], axis=0
        )
        picked = picked + dot(one_zero(taken & (tile == index)), ref[:LANES], CONTRACT_LAST)
        picked = picked + dot(one_zero(taken & (tile == index + 1)), high, CONTRACT_LAST)
    send_ref[...] = (picked * row_scale).astype(BF16).reshape(send_ref.shape)


def partial_kernel(
    place_ref,
    recv_ref,
    gate_hbm,
    up_hbm,
    down_hbm,
    own_ref,
    to_right_ref,
    to_left_ref,
    next_ref,
    previous_ref,
    tok_ref,
    scaled_ref,
    gate_ref,
    up_ref,
    down_ref,
    sems,
):
    copies = fetch((gate_hbm, up_hbm, down_hbm), (gate_ref, up_ref, down_ref), sems)
    experts = recv_ref.shape[0]
    width, hidden = gate_ref.shape
    block = SOURCES * GROUP
    per_tile = SOURCES * CAP
    reorder = reorder_matrix(iota((block, block), 0), iota((block, block), 1))
    for b in range(experts // SOURCES):
        sent = recv_ref[b * SOURCES : (b + 1) * SOURCES].reshape(block, LANES)
        rows = dot(reorder, sent).astype(BF16)
        place = slice(b * per_tile, (b + 1) * per_tile)
        for ref, index in ((tok_ref, 0), (scaled_ref, 2)):
            ref[place, :LANES] = rows[index * per_tile : (index + 1) * per_tile]
            ref[place, LANES:] = rows[(index + 1) * per_tile : (index + 2) * per_tile, : width - LANES]
    held = tok_ref.shape[0] // RING
    half = held // 2
    for copy in copies:
        copy.wait()
    for index, (rows_ref, ref) in enumerate(
        ((tok_ref, gate_ref), (tok_ref, up_ref), (scaled_ref, down_ref))
    ):
        columns = slice(index * hidden, (index + 1) * hidden)
        for step, pieces in (
            (RING // 2, ((to_right_ref, 0), (to_left_ref, half))),
            (1, ((next_ref, 0), (to_right_ref, half))),
            (RING - 1, ((to_left_ref, 0), (previous_ref, 0))),
            (0, ((own_ref, 0), (own_ref, half))),
        ):
            member = (place_ref[0] + step) & (RING - 1)
            begin = pl.multiple_of(member * held, held)
            value = dot(rows_ref[pl.ds(begin, held)], ref[...]).astype(BF16)
            for part, (out_ref, start) in enumerate(pieces):
                out_ref[start : start + half, columns] = value[part * half : (part + 1) * half]


def relay_kernel(next_ref, previous_ref, from_left_ref, from_right_ref, to_right_ref, to_left_ref):
    half = next_ref.shape[0]
    to_right_ref[...] = (next_ref[...].astype(F32) + from_left_ref[:half].astype(F32)).astype(BF16)
    to_left_ref[...] = (previous_ref[...].astype(F32) + from_right_ref[half:].astype(F32)).astype(BF16)


def window_kernel(
    place_ref,
    own_ref,
    from_left_ref,
    from_right_ref,
    far_left_ref,
    far_right_ref,
    kept_ref,
    to_right_ref,
    to_left_ref,
    across_ref,
    window_ref,
):
    half = far_left_ref.shape[0]
    window_ref[:half] = (
        own_ref[:half].astype(F32) + from_right_ref[:half].astype(F32) + far_left_ref[...].astype(F32)
    )
    window_ref[half:] = (
        own_ref[half:].astype(F32) + from_left_ref[half:].astype(F32) + far_right_ref[...].astype(F32)
    )
    share = kept_ref.shape[0]
    for step, ref in ((1, to_right_ref), (RING - 1, to_left_ref), (RING // 2, across_ref), (0, kept_ref)):
        member = (lax.shift_right_logical(place_ref[0], 2) + step) & (RING - 1)
        begin = pl.multiple_of(member * share, share)
        ref[...] = window_ref[pl.ds(begin, share)].astype(BF16)


def middle_kernel(kept_ref, from_left_ref, from_right_ref, across_ref, out_ref):
    hidden = kept_ref.shape[1] // 3

    def summed(index):
        columns = slice(index * hidden, (index + 1) * hidden)
        refs = (kept_ref, from_left_ref, from_right_ref, across_ref)
        return sum(ref[:, columns].astype(F32) for ref in refs)

    gate, up, grad = summed(0), summed(1), summed(2)
    sigmoid = jax.nn.sigmoid(gate)
    gated = gate * sigmoid
    hidden_value = (gated * up).astype(BF16)
    out_ref[:, :hidden] = hidden_value
    out_ref[:, hidden : 2 * hidden] = (grad * up * sigmoid * (1.0 + gate * (1.0 - sigmoid))).astype(BF16)
    out_ref[:, 2 * hidden : 3 * hidden] = (grad * gated).astype(BF16)
    score = jnp.sum(hidden_value.astype(F32) * grad, axis=1, keepdims=True)
    lane = iota((gate.shape[0], LANES), 1)
    packed = jnp.zeros(lane.shape, F32)
    for index, part in enumerate(three_parts(score)):
        packed = jnp.where(lane == SCORE_LANE + index, part.astype(F32), packed)
    out_ref[:, 3 * hidden :] = packed.astype(BF16)


def gathered(full_ref, place_ref, own_ref, left_ref, right_ref, far_left_ref, far_right_ref):
    held = own_ref.shape[0]
    half = held // 2
    for ref, step, start in (
        (own_ref, 0, 0),
        (right_ref, 1, 0),
        (left_ref, RING - 1, 0),
        (far_left_ref, RING // 2, 0),
        (far_right_ref, RING // 2, half),
    ):
        member = (place_ref[0] + step) & (RING - 1)
        begin = pl.multiple_of(member * held + start, half)
        full_ref[pl.ds(begin, ref.shape[0])] = ref[...]


def gradient_kernel(
    place_ref,
    own_ref,
    left_ref,
    right_ref,
    far_left_ref,
    far_right_ref,
    tok_ref,
    scaled_ref,
    gate_ref,
    up_ref,
    down_ref,
    full_ref,
):
    hidden = gate_ref.shape[1]
    gathered(full_ref, place_ref, own_ref, left_ref, right_ref, far_left_ref, far_right_ref)
    for index, (rows_ref, out_ref) in enumerate(
        ((scaled_ref, down_ref), (tok_ref, gate_ref), (tok_ref, up_ref))
    ):
        columns = slice(index * hidden, (index + 1) * hidden)
        out_ref[...] = dot(rows_ref[...], full_ref[:, columns], CONTRACT_FIRST).astype(BF16)


def rows_kernel(
    place_ref,
    own_ref,
    left_ref,
    right_ref,
    far_left_ref,
    far_right_ref,
    gate_hbm,
    up_hbm,
    down_hbm,
    back_ref,
    full_ref,
    tiles_ref,
    gate_ref,
    up_ref,
    down_ref,
    sems,
):
    copies = fetch((gate_hbm, up_hbm, down_hbm), (gate_ref, up_ref, down_ref), sems)
    experts = back_ref.shape[0]
    width, hidden = gate_ref.shape
    block = SOURCES * GROUP
    per_tile = SOURCES * CAP
    gathered(full_ref, place_ref, own_ref, left_ref, right_ref, far_left_ref, far_right_ref)
    for copy in copies:
        copy.wait()
    out_rows = dot(full_ref[:, :hidden], down_ref[...], CONTRACT_LAST)
    in_rows = dot(full_ref[:, hidden : 2 * hidden], gate_ref[...], CONTRACT_LAST) + dot(
        full_ref[:, 2 * hidden : 3 * hidden], up_ref[...], CONTRACT_LAST
    )
    tiles_ref[0] = out_rows[:, :LANES]
    tiles_ref[1] = full_ref[:, 3 * hidden :].astype(F32)
    tiles_ref[1, :, : width - LANES] = out_rows[:, LANES:]
    tiles_ref[2] = in_rows[:, :LANES]
    tiles_ref[3] = jnp.zeros(tiles_ref.shape[1:], F32)
    tiles_ref[3, :, : width - LANES] = in_rows[:, LANES:]
    restore = reorder_matrix(iota((block, block), 1), iota((block, block), 0))
    for b in range(experts // SOURCES):
        place = slice(b * per_tile, (b + 1) * per_tile)
        stacked = tiles_ref[:, place].astype(BF16).reshape(block, LANES)
        back_ref[b * SOURCES : (b + 1) * SOURCES] = (
            dot(restore, stacked).astype(BF16).reshape(SOURCES, GROUP, LANES)
        )


def combine_kernel(
    back_ref, plan_ref, routes_ref, weight_ref, mixed_ref, input_ref, score_ref, chosen_ref
):
    top_count, token_count = routes_ref.shape
    experts = back_ref.shape[0]
    width = mixed_ref.shape[0]
    rows = experts * GROUP
    back = back_ref[...].reshape(rows, LANES)
    plan = plan_ref[...].T
    rank, scale = plan[:, :experts], plan[:, experts:]
    spread = one_zero(expert_of_row(iota((experts, rows), 1), iota((experts, rows), 0)))
    tile, slot = tile_and_slot(iota((1, rows), 1))
    taken = dot(rank.astype(BF16), spread) == slot.astype(F32)
    for order, part in enumerate(three_parts(scale)[:WEIGHT_PARTS]):
        row_scale = jnp.where(taken, dot(part, spread), 0.0)
        for index in range(2):
            place = (index * WEIGHT_PARTS + order) * token_count
            chosen_ref[place : place + token_count] = jnp.where(tile == index, row_scale, 0.0).astype(BF16)
    taken = jnp.where(taken, 1.0, 0.0)
    for index in range(2):
        place = (2 * WEIGHT_PARTS + index) * token_count
        chosen_ref[place : place + token_count] = jnp.where(tile == 2 + index, taken, 0.0).astype(BF16)
    scored = jnp.where(tile == 1, taken, 0.0).astype(BF16)
    values = dot(chosen_ref[...], back)
    blocks = [values[i * token_count : (i + 1) * token_count] for i in range(2 * WEIGHT_PARTS + 2)]
    low, high = sum(blocks[:WEIGHT_PARTS]), sum(blocks[WEIGHT_PARTS : 2 * WEIGHT_PARTS])
    for ref, low, high in (
        (mixed_ref, low, high),
        (input_ref, blocks[2 * WEIGHT_PARTS], blocks[2 * WEIGHT_PARTS + 1]),
    ):
        ref[:LANES] = low.T.astype(BF16)
        ref[LANES:] = high.T[: width - LANES].astype(BF16)
    lane_of_part = iota((8, LANES), 1) - SCORE_LANE == iota((8, LANES), 0)
    row_score = dot(one_zero(lane_of_part & (iota((8, LANES), 0) < 3)), back, CONTRACT_LAST)
    spread = spread.astype(F32)
    spread = jnp.concatenate([(spread * row_score[i : i + 1]).astype(BF16) for i in range(3)], axis=0)
    by_expert = dot(spread, scored, CONTRACT_LAST)
    by_expert = sum(by_expert[i * experts : (i + 1) * experts] for i in range(3))
    expert = iota((experts, token_count), 0)
    for k in range(top_count):
        hit = routes_ref[k : k + 1] == expert
        value = jnp.sum(jnp.where(hit, by_expert, 0.0), axis=0, keepdims=True)
        score_ref[k : k + 1] = value / weight_ref[k : k + 1]


def kernel_call(body, out_shape, flops, moved, spaces=None, scratch=()):
    places = {}
    if spaces is not None:
        kinds = {"s": pltpu.SMEM, "v": pltpu.VMEM, "a": pl.ANY}
        places["in_specs"] = [pl.BlockSpec(memory_space=kinds[kind]) for kind in spaces]
    return pl.pallas_call(
        body,
        out_shape=out_shape,
        scratch_shapes=scratch,
        compiler_params=pltpu.CompilerParams(vmem_limit_bytes=VMEM_LIMIT),
        cost_estimate=pl.CostEstimate(flops=flops, bytes_accessed=moved, transcendentals=0),
        **places,
    )


def held_copies(*arrays):
    return [pltpu.VMEM(array.shape, array.dtype) for array in arrays] + [
        pltpu.SemaphoreType.DMA((len(arrays),))
    ]


def shifted(block, distance):
    parts = lax.axis_size("expert")
    return lax.ppermute(block, "expert", [(i, (i + distance) % parts) for i in range(parts)])


def per_device(
    tokens, cotangent, routes, route_weights, owner_slots, gate_weight, up_weight, down_weight
):
    experts = lax.axis_size("dp")
    parts = lax.axis_size("expert")
    token_count, width = tokens.shape
    hidden = gate_weight.shape[2]
    row_count = experts * CAP
    held = row_count // RING
    shape = jax.ShapeDtypeStruct
    exchanged = shape((experts, GROUP, LANES), BF16)
    rows = shape((row_count, width), BF16)
    whole, halved = (shape((size, 3 * hidden), BF16) for size in (held, held // 2))
    groups = [list(range(i, parts, RING)) for i in range(RING)]
    member = lax.axis_index("expert").astype(jnp.int32).reshape(1)
    weights = (gate_weight[0], up_weight[0], down_weight[0].T)
    arguments = (routes.T, route_weights.T, owner_slots.reshape(1, experts), tokens.T, cotangent.T)
    send, plan = kernel_call(
        dispatch_kernel,
        (exchanged, shape((2 * experts, token_count), F32)),
        300_000_000,
        1_000_000,
        spaces="aaaaa",
        scratch=held_copies(*arguments),
    )(*arguments)
    arrived = lax.all_to_all(send, "dp", split_axis=0, concat_axis=0, tiled=True)
    own, to_right, to_left, following, previous, token_rows, scaled_rows = kernel_call(
        partial_kernel,
        (whole, whole, whole, halved, halved, rows, rows),
        700_000_000,
        4_500_000,
        spaces="svaaa",
        scratch=held_copies(*weights),
    )(member, arrived, *weights)
    from_left, from_right = shifted(to_right, 1), shifted(to_left, -1)
    relay_right, relay_left = kernel_call(relay_kernel, (halved, halved), 300_000, 1_500_000)(
        following, previous, from_left, from_right
    )
    far_left, far_right = shifted(relay_right, 1), shifted(relay_left, -1)
    chunk = shape((row_count // parts, 3 * hidden), BF16)
    kept, to_right, to_left, across = kernel_call(
        window_kernel,
        (chunk, chunk, chunk, chunk),
        600_000,
        2_000_000,
        spaces="svvvvv",
        scratch=[pltpu.VMEM(whole.shape, F32)],
    )(member, own, from_left, from_right, far_left, far_right)
    share = kernel_call(
        middle_kernel, shape((row_count // parts, 3 * hidden + LANES), BF16), 1_000_000, 700_000
    )(
        kept,
        shifted(to_right, RING),
        shifted(to_left, -RING),
        shifted(across, parts // 2),
    )
    own = lax.all_gather(share, "expert", axis=0, tiled=True, axis_index_groups=groups)
    half = held // 2
    left, right = shifted(own, 1), shifted(own, -1)
    pieces = (own, left, right, shifted(left[:half], 1), shifted(right[half:], -1))
    full = pltpu.VMEM((row_count, 3 * hidden + LANES), BF16)
    back = kernel_call(
        rows_kernel,
        exchanged,
        700_000_000,
        4_500_000,
        spaces="svvvvvaaa",
        scratch=[full, pltpu.VMEM((TILES, row_count, LANES), F32)] + held_copies(*weights),
    )(member, *pieces, *weights)
    returned = lax.all_to_all(back, "dp", split_axis=0, concat_axis=0, tiled=True)
    matrix = shape((width, hidden), BF16)
    gate_grad, up_grad, down_grad = kernel_call(
        gradient_kernel,
        (matrix, matrix, matrix),
        700_000_000,
        4_500_000,
        spaces="svvvvvvv",
        scratch=[full],
    )(member, *pieces, token_rows, scaled_rows)
    down_grad = down_grad.T
    token_shape = shape((width, token_count), BF16)
    mixed, input_gradient, route_gradient = kernel_call(
        combine_kernel,
        (token_shape, token_shape, shape(arguments[0].shape, F32)),
        500_000_000,
        1_000_000,
        scratch=[pltpu.VMEM(((2 * WEIGHT_PARTS + 2) * token_count, experts * GROUP), BF16)],
    )(returned, plan, arguments[0], arguments[1])
    return (
        mixed.T,
        input_gradient.T,
        route_gradient.T,
        gate_grad[None],
        up_grad[None],
        down_grad[None],
    )


def solution(mesh):
    return jax.shard_map(
        per_device,
        mesh=mesh,
        in_specs=(
            P("dp", "expert"),
            P("dp", "expert"),
            P("dp", None),
            P("dp", None),
            P(),
            P("dp", "expert", None),
            P("dp", "expert", None),
            P("dp", None, "expert"),
        ),
        out_specs=(
            P("dp", "expert"),
            P("dp", "expert"),
            P("dp", None),
            P("dp", "expert", None),
            P("dp", "expert", None),
            P("dp", None, "expert"),
        ),
        check_vma=False,
    )
```

```python
import jax
import jax.numpy as jnp
from jax import lax
from jax.experimental import pallas as pl
from jax.experimental.pallas import tpu as pltpu
from jax.sharding import PartitionSpec as P

CAP = 6
SPARE = 2
LANES = 128
TILES = 4
GROUP = CAP * TILES
SOURCES = 16
RING = 4
SCORE_LANE = 96
WEIGHT_PARTS = 2
PLACE_BITS = 4
VMEM_LIMIT = 24 * 1024 * 1024

F32 = jnp.float32
BF16 = jnp.bfloat16
CONTRACT_LAST = (((1,), (1,)), ((), ()))
CONTRACT_FIRST = (((0,), (0,)), ((), ()))


def dot(left, right, dims=(((1,), (0,)), ((), ()))):
    return lax.dot_general(left, right, dims, preferred_element_type=F32)


def one_zero(condition):
    return jnp.where(condition, 1.0, 0.0).astype(BF16)


def three_parts(value):
    high = value.astype(BF16)
    rest = value - high.astype(F32)
    middle = rest.astype(BF16)
    return high, middle, (rest - middle.astype(F32)).astype(BF16)


def iota(shape, axis):
    return lax.broadcasted_iota(jnp.int32, shape, axis)


def expert_of_row(row, expert):
    offset = row - GROUP * expert
    return (offset >= 0) & (offset < GROUP)


def tile_and_slot(row):
    place = row - GROUP * lax.shift_right_logical(row * 2731, 16)
    tile = (
        (place >= CAP).astype(jnp.int32)
        + (place >= 2 * CAP).astype(jnp.int32)
        + (place >= 3 * CAP).astype(jnp.int32)
    )
    return tile, place - CAP * tile


def reorder_matrix(sorted_row, sent_row):
    per_tile = SOURCES * CAP
    tile = (
        (sorted_row >= per_tile).astype(jnp.int32)
        + (sorted_row >= 2 * per_tile).astype(jnp.int32)
        + (sorted_row >= 3 * per_tile).astype(jnp.int32)
    )
    within = sorted_row - per_tile * tile
    source = lax.shift_right_logical(within * 43, 8)
    return one_zero(sent_row == within + (GROUP - CAP) * source + CAP * tile)


def member_at(base, place_ref, step):
    sign = 1 - 2 * lax.shift_right_logical(place_ref[0], PLACE_BITS)
    return (base + sign * step) & (RING - 1)


def fetch(sources, targets, sems):
    copies = [
        pltpu.make_async_copy(source, target, sems.at[i])
        for i, (source, target) in enumerate(zip(sources, targets))
    ]
    for copy in copies:
        copy.start()
    return copies


def dispatch_kernel(
    routes_hbm,
    weight_hbm,
    slots_hbm,
    tok_hbm,
    cot_hbm,
    send_ref,
    plan_ref,
    routes_ref,
    weight_ref,
    slots_ref,
    tok_ref,
    cot_ref,
    sems,
):
    arguments = (routes_hbm, weight_hbm, slots_hbm, tok_hbm, cot_hbm)
    held = (routes_ref, weight_ref, slots_ref, tok_ref, cot_ref)
    for copy in fetch(arguments, held, sems):
        copy.wait()
    top_count, token_count = routes_ref.shape
    experts = slots_ref.shape[1]
    rows = experts * GROUP
    expert = iota((experts, token_count), 0)
    named = jnp.zeros((experts, token_count), F32)
    scale = jnp.zeros((experts, token_count), F32)
    for k in range(top_count):
        hit = routes_ref[k : k + 1] == expert
        named = named + jnp.where(hit, 1.0, 0.0)
        scale = scale + jnp.where(hit, weight_ref[k : k + 1], 0.0)
    earlier = one_zero(iota((token_count, token_count), 0) < iota((token_count, token_count), 1))
    rank = dot(named.astype(BF16), earlier)
    diagonal = iota((experts, experts), 0) == iota((experts, experts), 1)
    limit = jnp.sum(jnp.where(diagonal, slots_ref[...].astype(F32), 0.0), axis=1, keepdims=True)
    rank = jnp.where((named > 0.0) & (rank < limit + float(SPARE)), rank, -1.0)
    plan_ref[:experts] = rank
    plan_ref[experts:] = scale
    spread = one_zero(expert_of_row(iota((rows, experts), 0), iota((rows, experts), 1)))
    tile, slot = tile_and_slot(iota((rows, token_count), 0))
    taken = dot(spread, rank.astype(BF16)) == slot.astype(F32)
    row_scale = sum(dot(spread, part) for part in three_parts(scale))
    row_scale = jnp.sum(jnp.where(taken, row_scale, 0.0), axis=1, keepdims=True)
    row_scale = jnp.where(tile[:, :1] >= 2, row_scale, 1.0)
    width = tok_ref.shape[0]
    picked = jnp.zeros((rows, LANES), F32)
    for index, ref in ((0, tok_ref), (2, cot_ref)):
        high = jnp.concatenate(
            [ref[LANES:], jnp.zeros((2 * LANES - width, token_count), BF16)], axis=0
        )
        picked = picked + dot(one_zero(taken & (tile == index)), ref[:LANES], CONTRACT_LAST)
        picked = picked + dot(one_zero(taken & (tile == index + 1)), high, CONTRACT_LAST)
    send_ref[...] = (picked * row_scale).astype(BF16).reshape(send_ref.shape)


def partial_kernel(
    place_ref,
    recv_ref,
    gate_hbm,
    up_hbm,
    down_hbm,
    own_ref,
    to_right_ref,
    to_left_ref,
    next_ref,
    previous_ref,
    tok_ref,
    scaled_ref,
    gate_ref,
    up_ref,
    down_ref,
    sems,
):
    copies = fetch((gate_hbm, up_hbm, down_hbm), (gate_ref, up_ref, down_ref), sems)
    experts = recv_ref.shape[0]
    width, hidden = gate_ref.shape
    block = SOURCES * GROUP
    per_tile = SOURCES * CAP
    reorder = reorder_matrix(iota((block, block), 0), iota((block, block), 1))
    for b in range(experts // SOURCES):
        sent = recv_ref[b * SOURCES : (b + 1) * SOURCES].reshape(block, LANES)
        rows = dot(reorder, sent).astype(BF16)
        place = slice(b * per_tile, (b + 1) * per_tile)
        for ref, index in ((tok_ref, 0), (scaled_ref, 2)):
            ref[place, :LANES] = rows[index * per_tile : (index + 1) * per_tile]
            ref[place, LANES:] = rows[(index + 1) * per_tile : (index + 2) * per_tile, : width - LANES]
    held = tok_ref.shape[0] // RING
    half = held // 2
    for copy in copies:
        copy.wait()
    for index, (rows_ref, ref) in enumerate(
        ((tok_ref, gate_ref), (tok_ref, up_ref), (scaled_ref, down_ref))
    ):
        columns = slice(index * hidden, (index + 1) * hidden)
        for step, pieces in (
            (RING // 2, ((to_right_ref, 0), (to_left_ref, half))),
            (1, ((next_ref, 0), (to_right_ref, half))),
            (RING - 1, ((to_left_ref, 0), (previous_ref, 0))),
            (0, ((own_ref, 0), (own_ref, half))),
        ):
            member = member_at(place_ref[0], place_ref, step)
            begin = pl.multiple_of(member * held, held)
            value = dot(rows_ref[pl.ds(begin, held)], ref[...]).astype(BF16)
            for part, (out_ref, start) in enumerate(pieces):
                out_ref[start : start + half, columns] = value[part * half : (part + 1) * half]


def relay_kernel(next_ref, previous_ref, from_left_ref, from_right_ref, to_right_ref, to_left_ref):
    half = next_ref.shape[0]
    to_right_ref[...] = (next_ref[...].astype(F32) + from_left_ref[:half].astype(F32)).astype(BF16)
    to_left_ref[...] = (previous_ref[...].astype(F32) + from_right_ref[half:].astype(F32)).astype(BF16)


def window_kernel(
    place_ref,
    own_ref,
    from_left_ref,
    from_right_ref,
    far_left_ref,
    far_right_ref,
    kept_ref,
    to_right_ref,
    to_left_ref,
    next_ref,
    previous_ref,
    window_ref,
):
    half = far_left_ref.shape[0]
    window_ref[:half] = (
        own_ref[:half].astype(F32) + from_right_ref[:half].astype(F32) + far_left_ref[...].astype(F32)
    )
    window_ref[half:] = (
        own_ref[half:].astype(F32) + from_left_ref[half:].astype(F32) + far_right_ref[...].astype(F32)
    )
    share, columns = kept_ref.shape
    split = columns // 2

    def chunk(step, part):
        member = member_at(lax.shift_right_logical(place_ref[0], 2), place_ref, step)
        begin = pl.multiple_of(member * share, share)
        return window_ref[pl.ds(begin, share), part].astype(BF16)

    low, high = slice(0, split), slice(split, columns)
    kept_ref[...] = chunk(0, slice(0, columns))
    to_right_ref[:, low] = chunk(RING // 2, low)
    to_right_ref[:, high] = chunk(1, high)
    to_left_ref[:, low] = chunk(RING - 1, low)
    to_left_ref[:, high] = chunk(RING // 2, high)
    next_ref[...] = chunk(1, low)
    previous_ref[...] = chunk(RING - 1, high)


def second_relay_kernel(
    next_ref, previous_ref, from_left_ref, from_right_ref, to_right_ref, to_left_ref
):
    split = next_ref.shape[1]
    to_right_ref[...] = (next_ref[...].astype(F32) + from_left_ref[:, :split].astype(F32)).astype(BF16)
    to_left_ref[...] = (
        previous_ref[...].astype(F32) + from_right_ref[:, split:].astype(F32)
    ).astype(BF16)


def middle_kernel(
    kept_ref, from_left_ref, from_right_ref, far_left_ref, far_right_ref, out_ref, sum_ref
):
    hidden = kept_ref.shape[1] // 3
    split = far_left_ref.shape[1]
    sum_ref[:, :split] = (
        kept_ref[:, :split].astype(F32)
        + from_right_ref[:, :split].astype(F32)
        + far_left_ref[...].astype(F32)
    )
    sum_ref[:, split:] = (
        kept_ref[:, split:].astype(F32)
        + from_left_ref[:, split:].astype(F32)
        + far_right_ref[...].astype(F32)
    )
    gate, up, grad = (sum_ref[:, i * hidden : (i + 1) * hidden] for i in range(3))
    sigmoid = jax.nn.sigmoid(gate)
    gated = gate * sigmoid
    hidden_value = (gated * up).astype(BF16)
    out_ref[:, :hidden] = hidden_value
    out_ref[:, hidden : 2 * hidden] = (grad * up * sigmoid * (1.0 + gate * (1.0 - sigmoid))).astype(BF16)
    out_ref[:, 2 * hidden : 3 * hidden] = (grad * gated).astype(BF16)
    score = jnp.sum(hidden_value.astype(F32) * grad, axis=1, keepdims=True)
    lane = iota((gate.shape[0], LANES), 1)
    packed = jnp.zeros(lane.shape, F32)
    for index, part in enumerate(three_parts(score)):
        packed = jnp.where(lane == SCORE_LANE + index, part.astype(F32), packed)
    out_ref[:, 3 * hidden :] = packed.astype(BF16)


def gathered(full_ref, place_ref, own_ref, left_ref, right_ref, far_left_ref, far_right_ref):
    held = own_ref.shape[0]
    half = held // 2
    for ref, step, start in (
        (own_ref, 0, 0),
        (right_ref, 1, 0),
        (left_ref, RING - 1, 0),
        (far_left_ref, RING // 2, 0),
        (far_right_ref, RING // 2, half),
    ):
        member = member_at(place_ref[0], place_ref, step)
        begin = pl.multiple_of(member * held + start, half)
        full_ref[pl.ds(begin, ref.shape[0])] = ref[...]


def gradient_kernel(
    place_ref,
    own_ref,
    left_ref,
    right_ref,
    far_left_ref,
    far_right_ref,
    tok_ref,
    scaled_ref,
    gate_ref,
    up_ref,
    down_ref,
    full_ref,
):
    hidden = gate_ref.shape[1]
    gathered(full_ref, place_ref, own_ref, left_ref, right_ref, far_left_ref, far_right_ref)
    for index, (rows_ref, out_ref) in enumerate(
        ((scaled_ref, down_ref), (tok_ref, gate_ref), (tok_ref, up_ref))
    ):
        columns = slice(index * hidden, (index + 1) * hidden)
        out_ref[...] = dot(rows_ref[...], full_ref[:, columns], CONTRACT_FIRST).astype(BF16)


def rows_kernel(
    place_ref,
    own_ref,
    left_ref,
    right_ref,
    far_left_ref,
    far_right_ref,
    gate_hbm,
    up_hbm,
    down_hbm,
    back_ref,
    full_ref,
    tiles_ref,
    gate_ref,
    up_ref,
    down_ref,
    sems,
):
    copies = fetch((gate_hbm, up_hbm, down_hbm), (gate_ref, up_ref, down_ref), sems)
    experts = back_ref.shape[0]
    width, hidden = gate_ref.shape
    block = SOURCES * GROUP
    per_tile = SOURCES * CAP
    gathered(full_ref, place_ref, own_ref, left_ref, right_ref, far_left_ref, far_right_ref)
    for copy in copies:
        copy.wait()
    out_rows = dot(full_ref[:, :hidden], down_ref[...], CONTRACT_LAST)
    in_rows = dot(full_ref[:, hidden : 2 * hidden], gate_ref[...], CONTRACT_LAST) + dot(
        full_ref[:, 2 * hidden : 3 * hidden], up_ref[...], CONTRACT_LAST
    )
    tiles_ref[0] = out_rows[:, :LANES]
    tiles_ref[1] = full_ref[:, 3 * hidden :].astype(F32)
    tiles_ref[1, :, : width - LANES] = out_rows[:, LANES:]
    tiles_ref[2] = in_rows[:, :LANES]
    tiles_ref[3] = jnp.zeros(tiles_ref.shape[1:], F32)
    tiles_ref[3, :, : width - LANES] = in_rows[:, LANES:]
    restore = reorder_matrix(iota((block, block), 1), iota((block, block), 0))
    for b in range(experts // SOURCES):
        place = slice(b * per_tile, (b + 1) * per_tile)
        stacked = tiles_ref[:, place].astype(BF16).reshape(block, LANES)
        back_ref[b * SOURCES : (b + 1) * SOURCES] = (
            dot(restore, stacked).astype(BF16).reshape(SOURCES, GROUP, LANES)
        )


def combine_kernel(
    back_ref, plan_ref, routes_ref, weight_ref, mixed_ref, input_ref, score_ref, chosen_ref
):
    top_count, token_count = routes_ref.shape
    experts = back_ref.shape[0]
    width = mixed_ref.shape[0]
    rows = experts * GROUP
    back = back_ref[...].reshape(rows, LANES)
    plan = plan_ref[...].T
    rank, scale = plan[:, :experts], plan[:, experts:]
    spread = one_zero(expert_of_row(iota((experts, rows), 1), iota((experts, rows), 0)))
    tile, slot = tile_and_slot(iota((1, rows), 1))
    taken = dot(rank.astype(BF16), spread) == slot.astype(F32)
    for order, part in enumerate(three_parts(scale)[:WEIGHT_PARTS]):
        row_scale = jnp.where(taken, dot(part, spread), 0.0)
        for index in range(2):
            place = (index * WEIGHT_PARTS + order) * token_count
            chosen_ref[place : place + token_count] = jnp.where(tile == index, row_scale, 0.0).astype(BF16)
    taken = jnp.where(taken, 1.0, 0.0)
    for index in range(2):
        place = (2 * WEIGHT_PARTS + index) * token_count
        chosen_ref[place : place + token_count] = jnp.where(tile == 2 + index, taken, 0.0).astype(BF16)
    scored = jnp.where(tile == 1, taken, 0.0).astype(BF16)
    values = dot(chosen_ref[...], back)
    blocks = [values[i * token_count : (i + 1) * token_count] for i in range(2 * WEIGHT_PARTS + 2)]
    low, high = sum(blocks[:WEIGHT_PARTS]), sum(blocks[WEIGHT_PARTS : 2 * WEIGHT_PARTS])
    for ref, low, high in (
        (mixed_ref, low, high),
        (input_ref, blocks[2 * WEIGHT_PARTS], blocks[2 * WEIGHT_PARTS + 1]),
    ):
        ref[:LANES] = low.T.astype(BF16)
        ref[LANES:] = high.T[: width - LANES].astype(BF16)
    lane_of_part = iota((8, LANES), 1) - SCORE_LANE == iota((8, LANES), 0)
    row_score = dot(one_zero(lane_of_part & (iota((8, LANES), 0) < 3)), back, CONTRACT_LAST)
    spread = spread.astype(F32)
    spread = jnp.concatenate([(spread * row_score[i : i + 1]).astype(BF16) for i in range(3)], axis=0)
    by_expert = dot(spread, scored, CONTRACT_LAST)
    by_expert = sum(by_expert[i * experts : (i + 1) * experts] for i in range(3))
    expert = iota((experts, token_count), 0)
    for k in range(top_count):
        hit = routes_ref[k : k + 1] == expert
        value = jnp.sum(jnp.where(hit, by_expert, 0.0), axis=0, keepdims=True)
        score_ref[k : k + 1] = value / weight_ref[k : k + 1]


def kernel_call(body, out_shape, flops, moved, spaces=None, scratch=()):
    places = {}
    if spaces is not None:
        kinds = {"s": pltpu.SMEM, "v": pltpu.VMEM, "a": pl.ANY}
        places["in_specs"] = [pl.BlockSpec(memory_space=kinds[kind]) for kind in spaces]
    return pl.pallas_call(
        body,
        out_shape=out_shape,
        scratch_shapes=scratch,
        compiler_params=pltpu.CompilerParams(vmem_limit_bytes=VMEM_LIMIT),
        cost_estimate=pl.CostEstimate(flops=flops, bytes_accessed=moved, transcendentals=0),
        **places,
    )


def held_copies(*arrays):
    return [pltpu.VMEM(array.shape, array.dtype) for array in arrays] + [
        pltpu.SemaphoreType.DMA((len(arrays),))
    ]


def shifted(block, distance):
    parts, columns = lax.axis_size("expert"), lax.axis_size("dp")
    route = [
        (part * columns + column, (part + (1 - 2 * (column % 2)) * distance) % parts * columns + column)
        for part in range(parts)
        for column in range(columns)
    ]
    return lax.ppermute(block, ("expert", "dp"), route)


def per_device(
    tokens, cotangent, routes, route_weights, owner_slots, gate_weight, up_weight, down_weight
):
    experts = lax.axis_size("dp")
    parts = lax.axis_size("expert")
    token_count, width = tokens.shape
    hidden = gate_weight.shape[2]
    row_count = experts * CAP
    held = row_count // RING
    shape = jax.ShapeDtypeStruct
    exchanged = shape((experts, GROUP, LANES), BF16)
    rows = shape((row_count, width), BF16)
    whole, halved = (shape((size, 3 * hidden), BF16) for size in (held, held // 2))
    groups = [list(range(i, parts, RING)) for i in range(RING)]
    member = lax.axis_index("expert") + ((lax.axis_index("dp") & 1) << PLACE_BITS)
    member = member.astype(jnp.int32).reshape(1)
    weights = (gate_weight[0], up_weight[0], down_weight[0].T)
    arguments = (routes.T, route_weights.T, owner_slots.reshape(1, experts), tokens.T, cotangent.T)
    send, plan = kernel_call(
        dispatch_kernel,
        (exchanged, shape((2 * experts, token_count), F32)),
        300_000_000,
        1_000_000,
        spaces="aaaaa",
        scratch=held_copies(*arguments),
    )(*arguments)
    arrived = lax.all_to_all(send, "dp", split_axis=0, concat_axis=0, tiled=True)
    own, to_right, to_left, following, previous, token_rows, scaled_rows = kernel_call(
        partial_kernel,
        (whole, whole, whole, halved, halved, rows, rows),
        700_000_000,
        4_500_000,
        spaces="svaaa",
        scratch=held_copies(*weights),
    )(member, arrived, *weights)
    from_left, from_right = shifted(to_right, 1), shifted(to_left, -1)
    relay_right, relay_left = kernel_call(relay_kernel, (halved, halved), 300_000, 1_500_000)(
        following, previous, from_left, from_right
    )
    far_left, far_right = shifted(relay_right, 1), shifted(relay_left, -1)
    chunk, chunk_half = (
        shape((row_count // parts, columns), BF16) for columns in (3 * hidden, 3 * hidden // 2)
    )
    kept, to_right, to_left, following, previous = kernel_call(
        window_kernel,
        (chunk, chunk, chunk, chunk_half, chunk_half),
        600_000,
        2_000_000,
        spaces="svvvvv",
        scratch=[pltpu.VMEM(whole.shape, F32)],
    )(member, own, from_left, from_right, far_left, far_right)
    from_left, from_right = shifted(to_right, RING), shifted(to_left, -RING)
    relay_right, relay_left = kernel_call(
        second_relay_kernel, (chunk_half, chunk_half), 100_000, 400_000
    )(following, previous, from_left, from_right)
    far_left, far_right = shifted(relay_right, RING), shifted(relay_left, -RING)
    share = kernel_call(
        middle_kernel,
        shape((row_count // parts, 3 * hidden + LANES), BF16),
        1_000_000,
        700_000,
        scratch=[pltpu.VMEM(chunk.shape, F32)],
    )(kept, from_left, from_right, far_left, far_right)
    own = lax.all_gather(share, "expert", axis=0, tiled=True, axis_index_groups=groups)
    half = held // 2
    left, right = shifted(own, 1), shifted(own, -1)
    pieces = (own, left, right, shifted(left[:half], 1), shifted(right[half:], -1))
    full = pltpu.VMEM((row_count, 3 * hidden + LANES), BF16)
    back = kernel_call(
        rows_kernel,
        exchanged,
        700_000_000,
        4_500_000,
        spaces="svvvvvaaa",
        scratch=[full, pltpu.VMEM((TILES, row_count, LANES), F32)] + held_copies(*weights),
    )(member, *pieces, *weights)
    returned = lax.all_to_all(back, "dp", split_axis=0, concat_axis=0, tiled=True)
    matrix = shape((width, hidden), BF16)
    gate_grad, up_grad, down_grad = kernel_call(
        gradient_kernel,
        (matrix, matrix, matrix),
        700_000_000,
        4_500_000,
        spaces="svvvvvvv",
        scratch=[full],
    )(member, *pieces, token_rows, scaled_rows)
    down_grad = down_grad.T
    token_shape = shape((width, token_count), BF16)
    mixed, input_gradient, route_gradient = kernel_call(
        combine_kernel,
        (token_shape, token_shape, shape(arguments[0].shape, F32)),
        500_000_000,
        1_000_000,
        scratch=[pltpu.VMEM(((2 * WEIGHT_PARTS + 2) * token_count, experts * GROUP), BF16)],
    )(returned, plan, arguments[0], arguments[1])
    return (
        mixed.T,
        input_gradient.T,
        route_gradient.T,
        gate_grad[None],
        up_grad[None],
        down_grad[None],
    )


def solution(mesh):
    return jax.shard_map(
        per_device,
        mesh=mesh,
        in_specs=(
            P("dp", "expert"),
            P("dp", "expert"),
            P("dp", None),
            P("dp", None),
            P(),
            P("dp", "expert", None),
            P("dp", "expert", None),
            P("dp", None, "expert"),
        ),
        out_specs=(
            P("dp", "expert"),
            P("dp", "expert"),
            P("dp", None),
            P("dp", "expert", None),
            P("dp", "expert", None),
            P("dp", None, "expert"),
        ),
        check_vma=False,
    )
```

```python
import jax
import jax.numpy as jnp
from jax import lax
from jax.experimental import pallas as pl
from jax.experimental.pallas import tpu as pltpu
from jax.sharding import PartitionSpec as P

CAP = 6
SPARE = 2
LANES = 128
TILES = 4
GROUP = CAP * TILES
SOURCES = 16
RING = 4
SCORE_LANE = 96
WEIGHT_PARTS = 2
PLACE_BITS = 4
VMEM_LIMIT = 24 * 1024 * 1024

F32 = jnp.float32
BF16 = jnp.bfloat16
CONTRACT_LAST = (((1,), (1,)), ((), ()))
CONTRACT_FIRST = (((0,), (0,)), ((), ()))


def dot(left, right, dims=(((1,), (0,)), ((), ()))):
    return lax.dot_general(left, right, dims, preferred_element_type=F32)


def one_zero(condition):
    return jnp.where(condition, 1.0, 0.0).astype(BF16)


def three_parts(value):
    high = value.astype(BF16)
    rest = value - high.astype(F32)
    middle = rest.astype(BF16)
    return high, middle, (rest - middle.astype(F32)).astype(BF16)


def iota(shape, axis):
    return lax.broadcasted_iota(jnp.int32, shape, axis)


def expert_of_row(row, expert):
    offset = row - GROUP * expert
    return (offset >= 0) & (offset < GROUP)


def tile_and_slot(row):
    place = row - GROUP * lax.shift_right_logical(row * 2731, 16)
    tile = (
        (place >= CAP).astype(jnp.int32)
        + (place >= 2 * CAP).astype(jnp.int32)
        + (place >= 3 * CAP).astype(jnp.int32)
    )
    return tile, place - CAP * tile


def reorder_matrix(sorted_row, sent_row):
    per_tile = SOURCES * CAP
    tile = (
        (sorted_row >= per_tile).astype(jnp.int32)
        + (sorted_row >= 2 * per_tile).astype(jnp.int32)
        + (sorted_row >= 3 * per_tile).astype(jnp.int32)
    )
    within = sorted_row - per_tile * tile
    source = lax.shift_right_logical(within * 43, 8)
    return one_zero(sent_row == within + (GROUP - CAP) * source + CAP * tile)


def member_at(base, place_ref, step):
    sign = 1 - 2 * lax.shift_right_logical(place_ref[0], PLACE_BITS)
    return (base + sign * step) & (RING - 1)


def fetch(sources, targets, sems):
    copies = [
        pltpu.make_async_copy(source, target, sems.at[i])
        for i, (source, target) in enumerate(zip(sources, targets))
    ]
    for copy in copies:
        copy.start()
    return copies


def dispatch_kernel(
    routes_hbm,
    weight_hbm,
    slots_hbm,
    tok_hbm,
    cot_hbm,
    send_ref,
    plan_ref,
    routes_ref,
    weight_ref,
    slots_ref,
    tok_ref,
    cot_ref,
    sems,
):
    arguments = (routes_hbm, weight_hbm, slots_hbm, tok_hbm, cot_hbm)
    held = (routes_ref, weight_ref, slots_ref, tok_ref, cot_ref)
    for copy in fetch(arguments, held, sems):
        copy.wait()
    top_count, token_count = routes_ref.shape
    experts = slots_ref.shape[1]
    rows = experts * GROUP
    expert = iota((experts, token_count), 0)
    named = jnp.zeros((experts, token_count), F32)
    scale = jnp.zeros((experts, token_count), F32)
    for k in range(top_count):
        hit = routes_ref[k : k + 1] == expert
        named = named + jnp.where(hit, 1.0, 0.0)
        scale = scale + jnp.where(hit, weight_ref[k : k + 1], 0.0)
    earlier = one_zero(iota((token_count, token_count), 0) < iota((token_count, token_count), 1))
    rank = dot(named.astype(BF16), earlier)
    diagonal = iota((experts, experts), 0) == iota((experts, experts), 1)
    limit = jnp.sum(jnp.where(diagonal, slots_ref[...].astype(F32), 0.0), axis=1, keepdims=True)
    rank = jnp.where((named > 0.0) & (rank < limit + float(SPARE)), rank, -1.0)
    plan_ref[:experts] = rank
    plan_ref[experts:] = scale
    spread = one_zero(expert_of_row(iota((rows, experts), 0), iota((rows, experts), 1)))
    tile, slot = tile_and_slot(iota((rows, token_count), 0))
    taken = dot(spread, rank.astype(BF16)) == slot.astype(F32)
    row_scale = sum(dot(spread, part) for part in three_parts(scale))
    row_scale = jnp.sum(jnp.where(taken, row_scale, 0.0), axis=1, keepdims=True)
    row_scale = jnp.where(tile[:, :1] >= 2, row_scale, 1.0)
    width = tok_ref.shape[0]
    picked = jnp.zeros((rows, LANES), F32)
    for index, ref in ((0, tok_ref), (2, cot_ref)):
        high = jnp.concatenate(
            [ref[LANES:], jnp.zeros((2 * LANES - width, token_count), BF16)], axis=0
        )
        picked = picked + dot(one_zero(taken & (tile == index)), ref[:LANES], CONTRACT_LAST)
        picked = picked + dot(one_zero(taken & (tile == index + 1)), high, CONTRACT_LAST)
    send_ref[...] = (picked * row_scale).astype(BF16).reshape(send_ref.shape)


def window_partials(place_ref, products, own_ref, to_right_ref, to_left_ref, next_ref, previous_ref):
    held = own_ref.shape[0]
    half = held // 2
    for index, (rows_ref, ref) in enumerate(products):
        hidden = ref.shape[1]
        columns = slice(index * hidden, (index + 1) * hidden)
        for step, pieces in (
            (RING // 2, ((to_right_ref, 0), (to_left_ref, half))),
            (1, ((next_ref, 0), (to_right_ref, half))),
            (RING - 1, ((to_left_ref, 0), (previous_ref, 0))),
            (0, ((own_ref, 0), (own_ref, half))),
        ):
            member = member_at(place_ref[0], place_ref, step)
            begin = pl.multiple_of(member * held, held)
            value = dot(rows_ref[pl.ds(begin, held)], ref[...]).astype(BF16)
            for part, (out_ref, start) in enumerate(pieces):
                out_ref[start : start + half, columns] = value[part * half : (part + 1) * half]


def partial_kernel(
    place_ref,
    recv_ref,
    gate_hbm,
    up_hbm,
    own_ref,
    to_right_ref,
    to_left_ref,
    next_ref,
    previous_ref,
    tok_ref,
    scaled_ref,
    gate_ref,
    up_ref,
    sems,
):
    copies = fetch((gate_hbm, up_hbm), (gate_ref, up_ref), sems)
    experts = recv_ref.shape[0]
    width = gate_ref.shape[0]
    block = SOURCES * GROUP
    per_tile = SOURCES * CAP
    reorder = reorder_matrix(iota((block, block), 0), iota((block, block), 1))
    for b in range(experts // SOURCES):
        sent = recv_ref[b * SOURCES : (b + 1) * SOURCES].reshape(block, LANES)
        rows = dot(reorder, sent).astype(BF16)
        place = slice(b * per_tile, (b + 1) * per_tile)
        for ref, index in ((tok_ref, 0), (scaled_ref, 2)):
            ref[place, :LANES] = rows[index * per_tile : (index + 1) * per_tile]
            ref[place, LANES:] = rows[(index + 1) * per_tile : (index + 2) * per_tile, : width - LANES]
    for copy in copies:
        copy.wait()
    products = ((tok_ref, gate_ref), (tok_ref, up_ref))
    window_partials(
        place_ref, products, own_ref, to_right_ref, to_left_ref, next_ref, previous_ref
    )


def backward_partial_kernel(
    place_ref, scaled_ref, down_ref, own_ref, to_right_ref, to_left_ref, next_ref, previous_ref
):
    products = ((scaled_ref, down_ref),)
    window_partials(
        place_ref, products, own_ref, to_right_ref, to_left_ref, next_ref, previous_ref
    )


def relay_kernel(next_ref, previous_ref, from_left_ref, from_right_ref, to_right_ref, to_left_ref):
    half = next_ref.shape[0]
    to_right_ref[...] = (next_ref[...].astype(F32) + from_left_ref[:half].astype(F32)).astype(BF16)
    to_left_ref[...] = (previous_ref[...].astype(F32) + from_right_ref[half:].astype(F32)).astype(BF16)


def window_kernel(
    place_ref,
    own_ref,
    from_left_ref,
    from_right_ref,
    far_left_ref,
    far_right_ref,
    kept_ref,
    to_right_ref,
    to_left_ref,
    next_ref,
    previous_ref,
    window_ref,
):
    half = far_left_ref.shape[0]
    window_ref[:half] = (
        own_ref[:half].astype(F32) + from_right_ref[:half].astype(F32) + far_left_ref[...].astype(F32)
    )
    window_ref[half:] = (
        own_ref[half:].astype(F32) + from_left_ref[half:].astype(F32) + far_right_ref[...].astype(F32)
    )
    share, columns = kept_ref.shape
    split = columns // 2

    def chunk(step, part):
        member = member_at(lax.shift_right_logical(place_ref[0], 2), place_ref, step)
        begin = pl.multiple_of(member * share, share)
        return window_ref[pl.ds(begin, share), part].astype(BF16)

    low, high = slice(0, split), slice(split, columns)
    kept_ref[...] = chunk(0, slice(0, columns))
    to_right_ref[:, low] = chunk(RING // 2, low)
    to_right_ref[:, high] = chunk(1, high)
    to_left_ref[:, low] = chunk(RING - 1, low)
    to_left_ref[:, high] = chunk(RING // 2, high)
    next_ref[...] = chunk(1, low)
    previous_ref[...] = chunk(RING - 1, high)


def second_relay_kernel(
    next_ref, previous_ref, from_left_ref, from_right_ref, to_right_ref, to_left_ref
):
    split = next_ref.shape[1]
    to_right_ref[...] = (next_ref[...].astype(F32) + from_left_ref[:, :split].astype(F32)).astype(BF16)
    to_left_ref[...] = (
        previous_ref[...].astype(F32) + from_right_ref[:, split:].astype(F32)
    ).astype(BF16)


def chunk_sum(sum_ref, kept_ref, from_left_ref, from_right_ref, far_left_ref, far_right_ref):
    split = far_left_ref.shape[1]
    sum_ref[:, :split] = (
        kept_ref[:, :split].astype(F32)
        + from_right_ref[:, :split].astype(F32)
        + far_left_ref[...].astype(F32)
    )
    sum_ref[:, split:] = (
        kept_ref[:, split:].astype(F32)
        + from_left_ref[:, split:].astype(F32)
        + far_right_ref[...].astype(F32)
    )


def middle_kernel(*refs):
    forward, backward, (out_ref, sum_ref, grad_ref) = refs[:5], refs[5:10], refs[10:]
    chunk_sum(sum_ref, *forward)
    chunk_sum(grad_ref, *backward)
    hidden = grad_ref.shape[1]
    gate, up, grad = sum_ref[:, :hidden], sum_ref[:, hidden:], grad_ref[...]
    sigmoid = jax.nn.sigmoid(gate)
    gated = gate * sigmoid
    hidden_value = (gated * up).astype(BF16)
    out_ref[:, :hidden] = hidden_value
    out_ref[:, hidden : 2 * hidden] = (grad * up * sigmoid * (1.0 + gate * (1.0 - sigmoid))).astype(BF16)
    out_ref[:, 2 * hidden : 3 * hidden] = (grad * gated).astype(BF16)
    score = jnp.sum(hidden_value.astype(F32) * grad, axis=1, keepdims=True)
    lane = iota((gate.shape[0], LANES), 1)
    packed = jnp.zeros(lane.shape, F32)
    for index, part in enumerate(three_parts(score)):
        packed = jnp.where(lane == SCORE_LANE + index, part.astype(F32), packed)
    out_ref[:, 3 * hidden :] = packed.astype(BF16)


def gathered(full_ref, place_ref, own_ref, left_ref, right_ref, far_left_ref, far_right_ref):
    held = own_ref.shape[0]
    half = held // 2
    for ref, step, start in (
        (own_ref, 0, 0),
        (right_ref, 1, 0),
        (left_ref, RING - 1, 0),
        (far_left_ref, RING // 2, 0),
        (far_right_ref, RING // 2, half),
    ):
        member = member_at(place_ref[0], place_ref, step)
        begin = pl.multiple_of(member * held + start, half)
        full_ref[pl.ds(begin, ref.shape[0])] = ref[...]


def gradient_kernel(
    place_ref,
    own_ref,
    left_ref,
    right_ref,
    far_left_ref,
    far_right_ref,
    tok_ref,
    scaled_ref,
    gate_ref,
    up_ref,
    down_ref,
    full_ref,
):
    hidden = gate_ref.shape[1]
    gathered(full_ref, place_ref, own_ref, left_ref, right_ref, far_left_ref, far_right_ref)
    for index, (rows_ref, out_ref) in enumerate(
        ((scaled_ref, down_ref), (tok_ref, gate_ref), (tok_ref, up_ref))
    ):
        columns = slice(index * hidden, (index + 1) * hidden)
        out_ref[...] = dot(rows_ref[...], full_ref[:, columns], CONTRACT_FIRST).astype(BF16)


def rows_kernel(
    place_ref,
    own_ref,
    left_ref,
    right_ref,
    far_left_ref,
    far_right_ref,
    gate_hbm,
    up_hbm,
    down_hbm,
    back_ref,
    full_ref,
    tiles_ref,
    gate_ref,
    up_ref,
    down_ref,
    sems,
):
    copies = fetch((gate_hbm, up_hbm, down_hbm), (gate_ref, up_ref, down_ref), sems)
    experts = back_ref.shape[0]
    width, hidden = gate_ref.shape
    block = SOURCES * GROUP
    per_tile = SOURCES * CAP
    gathered(full_ref, place_ref, own_ref, left_ref, right_ref, far_left_ref, far_right_ref)
    for copy in copies:
        copy.wait()
    out_rows = dot(full_ref[:, :hidden], down_ref[...], CONTRACT_LAST)
    in_rows = dot(full_ref[:, hidden : 2 * hidden], gate_ref[...], CONTRACT_LAST) + dot(
        full_ref[:, 2 * hidden : 3 * hidden], up_ref[...], CONTRACT_LAST
    )
    tiles_ref[0] = out_rows[:, :LANES]
    tiles_ref[1] = full_ref[:, 3 * hidden :].astype(F32)
    tiles_ref[1, :, : width - LANES] = out_rows[:, LANES:]
    tiles_ref[2] = in_rows[:, :LANES]
    tiles_ref[3] = jnp.zeros(tiles_ref.shape[1:], F32)
    tiles_ref[3, :, : width - LANES] = in_rows[:, LANES:]
    restore = reorder_matrix(iota((block, block), 1), iota((block, block), 0))
    for b in range(experts // SOURCES):
        place = slice(b * per_tile, (b + 1) * per_tile)
        stacked = tiles_ref[:, place].astype(BF16).reshape(block, LANES)
        back_ref[b * SOURCES : (b + 1) * SOURCES] = (
            dot(restore, stacked).astype(BF16).reshape(SOURCES, GROUP, LANES)
        )


def combine_kernel(
    back_ref, plan_ref, routes_ref, weight_ref, mixed_ref, input_ref, score_ref, chosen_ref
):
    top_count, token_count = routes_ref.shape
    experts = back_ref.shape[0]
    width = mixed_ref.shape[0]
    rows = experts * GROUP
    back = back_ref[...].reshape(rows, LANES)
    plan = plan_ref[...].T
    rank, scale = plan[:, :experts], plan[:, experts:]
    spread = one_zero(expert_of_row(iota((experts, rows), 1), iota((experts, rows), 0)))
    tile, slot = tile_and_slot(iota((1, rows), 1))
    taken = dot(rank.astype(BF16), spread) == slot.astype(F32)
    for order, part in enumerate(three_parts(scale)[:WEIGHT_PARTS]):
        row_scale = jnp.where(taken, dot(part, spread), 0.0)
        for index in range(2):
            place = (index * WEIGHT_PARTS + order) * token_count
            chosen_ref[place : place + token_count] = jnp.where(tile == index, row_scale, 0.0).astype(BF16)
    taken = jnp.where(taken, 1.0, 0.0)
    for index in range(2):
        place = (2 * WEIGHT_PARTS + index) * token_count
        chosen_ref[place : place + token_count] = jnp.where(tile == 2 + index, taken, 0.0).astype(BF16)
    scored = jnp.where(tile == 1, taken, 0.0).astype(BF16)
    values = dot(chosen_ref[...], back)
    blocks = [values[i * token_count : (i + 1) * token_count] for i in range(2 * WEIGHT_PARTS + 2)]
    low, high = sum(blocks[:WEIGHT_PARTS]), sum(blocks[WEIGHT_PARTS : 2 * WEIGHT_PARTS])
    for ref, low, high in (
        (mixed_ref, low, high),
        (input_ref, blocks[2 * WEIGHT_PARTS], blocks[2 * WEIGHT_PARTS + 1]),
    ):
        ref[:LANES] = low.T.astype(BF16)
        ref[LANES:] = high.T[: width - LANES].astype(BF16)
    lane_of_part = iota((8, LANES), 1) - SCORE_LANE == iota((8, LANES), 0)
    row_score = dot(one_zero(lane_of_part & (iota((8, LANES), 0) < 3)), back, CONTRACT_LAST)
    spread = spread.astype(F32)
    spread = jnp.concatenate([(spread * row_score[i : i + 1]).astype(BF16) for i in range(3)], axis=0)
    by_expert = dot(spread, scored, CONTRACT_LAST)
    by_expert = sum(by_expert[i * experts : (i + 1) * experts] for i in range(3))
    expert = iota((experts, token_count), 0)
    for k in range(top_count):
        hit = routes_ref[k : k + 1] == expert
        value = jnp.sum(jnp.where(hit, by_expert, 0.0), axis=0, keepdims=True)
        score_ref[k : k + 1] = value / weight_ref[k : k + 1]


def kernel_call(body, out_shape, flops, moved, spaces=None, scratch=()):
    places = {}
    if spaces is not None:
        kinds = {"s": pltpu.SMEM, "v": pltpu.VMEM, "a": pl.ANY}
        places["in_specs"] = [pl.BlockSpec(memory_space=kinds[kind]) for kind in spaces]
    return pl.pallas_call(
        body,
        out_shape=out_shape,
        scratch_shapes=scratch,
        compiler_params=pltpu.CompilerParams(vmem_limit_bytes=VMEM_LIMIT),
        cost_estimate=pl.CostEstimate(flops=flops, bytes_accessed=moved, transcendentals=0),
        **places,
    )


def held_copies(*arrays):
    return [pltpu.VMEM(array.shape, array.dtype) for array in arrays] + [
        pltpu.SemaphoreType.DMA((len(arrays),))
    ]


def shifted(block, distance):
    parts, columns = lax.axis_size("expert"), lax.axis_size("dp")
    route = [
        (part * columns + column, (part + (1 - 2 * (column % 2)) * distance) % parts * columns + column)
        for part in range(parts)
        for column in range(columns)
    ]
    return lax.ppermute(block, ("expert", "dp"), route)


def partial_shapes(held, columns):
    whole, halved = (jax.ShapeDtypeStruct((size, columns), BF16) for size in (held, held // 2))
    return (whole, whole, whole, halved, halved)


def reduced(member, partials, parts):
    own, to_right, to_left, following, previous = partials
    held, columns = own.shape
    shape = jax.ShapeDtypeStruct
    halved = shape((held // 2, columns), BF16)
    from_left, from_right = shifted(to_right, 1), shifted(to_left, -1)
    relay_right, relay_left = kernel_call(relay_kernel, (halved, halved), 300_000, 1_500_000)(
        following, previous, from_left, from_right
    )
    far_left, far_right = shifted(relay_right, 1), shifted(relay_left, -1)
    chunk, chunk_half = (shape((held // (parts // RING), size), BF16) for size in (columns, columns // 2))
    kept, to_right, to_left, following, previous = kernel_call(
        window_kernel,
        (chunk, chunk, chunk, chunk_half, chunk_half),
        600_000,
        2_000_000,
        spaces="svvvvv",
        scratch=[pltpu.VMEM((held, columns), F32)],
    )(member, own, from_left, from_right, far_left, far_right)
    from_left, from_right = shifted(to_right, RING), shifted(to_left, -RING)
    relay_right, relay_left = kernel_call(
        second_relay_kernel, (chunk_half, chunk_half), 100_000, 400_000
    )(following, previous, from_left, from_right)
    far_left, far_right = shifted(relay_right, RING), shifted(relay_left, -RING)
    return [kept, from_left, from_right, far_left, far_right]


def per_device(
    tokens, cotangent, routes, route_weights, owner_slots, gate_weight, up_weight, down_weight
):
    experts = lax.axis_size("dp")
    parts = lax.axis_size("expert")
    token_count, width = tokens.shape
    hidden = gate_weight.shape[2]
    row_count = experts * CAP
    held = row_count // RING
    shape = jax.ShapeDtypeStruct
    exchanged = shape((experts, GROUP, LANES), BF16)
    rows = shape((row_count, width), BF16)
    groups = [list(range(i, parts, RING)) for i in range(RING)]
    member = lax.axis_index("expert") + ((lax.axis_index("dp") & 1) << PLACE_BITS)
    member = member.astype(jnp.int32).reshape(1)
    weights = (gate_weight[0], up_weight[0], down_weight[0].T)
    arguments = (routes.T, route_weights.T, owner_slots.reshape(1, experts), tokens.T, cotangent.T)
    send, plan = kernel_call(
        dispatch_kernel,
        (exchanged, shape((2 * experts, token_count), F32)),
        300_000_000,
        1_000_000,
        spaces="aaaaa",
        scratch=held_copies(*arguments),
    )(*arguments)
    arrived = lax.all_to_all(send, "dp", split_axis=0, concat_axis=0, tiled=True)
    columns = 2 * hidden
    *forward, token_rows, scaled_rows = kernel_call(
        partial_kernel,
        (*partial_shapes(held, columns), rows, rows),
        450_000_000,
        3_000_000,
        spaces="svaa",
        scratch=held_copies(*weights[:2]),
    )(member, arrived, *weights[:2])
    backward = kernel_call(
        backward_partial_kernel,
        partial_shapes(held, hidden),
        180_000_000,
        1_500_000,
        spaces="svv",
    )(member, scaled_rows, weights[2])
    summands = reduced(member, forward, parts) + reduced(member, backward, parts)
    share_rows = row_count // parts
    share = kernel_call(
        middle_kernel,
        shape((share_rows, 3 * hidden + LANES), BF16),
        1_000_000,
        700_000,
        scratch=[pltpu.VMEM((share_rows, columns), F32), pltpu.VMEM((share_rows, hidden), F32)],
    )(*summands)
    own = lax.all_gather(share, "expert", axis=0, tiled=True, axis_index_groups=groups)
    half = held // 2
    left, right = shifted(own, 1), shifted(own, -1)
    pieces = (own, left, right, shifted(left[:half], 1), shifted(right[half:], -1))
    full = pltpu.VMEM((row_count, 3 * hidden + LANES), BF16)
    back = kernel_call(
        rows_kernel,
        exchanged,
        700_000_000,
        4_500_000,
        spaces="svvvvvaaa",
        scratch=[full, pltpu.VMEM((TILES, row_count, LANES), F32)] + held_copies(*weights),
    )(member, *pieces, *weights)
    returned = lax.all_to_all(back, "dp", split_axis=0, concat_axis=0, tiled=True)
    matrix = shape((width, hidden), BF16)
    gate_grad, up_grad, down_grad = kernel_call(
        gradient_kernel,
        (matrix, matrix, matrix),
        700_000_000,
        4_500_000,
        spaces="svvvvvvv",
        scratch=[full],
    )(member, *pieces, token_rows, scaled_rows)
    down_grad = down_grad.T
    token_shape = shape((width, token_count), BF16)
    mixed, input_gradient, route_gradient = kernel_call(
        combine_kernel,
        (token_shape, token_shape, shape(arguments[0].shape, F32)),
        500_000_000,
        1_000_000,
        scratch=[pltpu.VMEM(((2 * WEIGHT_PARTS + 2) * token_count, experts * GROUP), BF16)],
    )(returned, plan, arguments[0], arguments[1])
    return (
        mixed.T,
        input_gradient.T,
        route_gradient.T,
        gate_grad[None],
        up_grad[None],
        down_grad[None],
    )


def solution(mesh):
    return jax.shard_map(
        per_device,
        mesh=mesh,
        in_specs=(
            P("dp", "expert"),
            P("dp", "expert"),
            P("dp", None),
            P("dp", None),
            P(),
            P("dp", "expert", None),
            P("dp", "expert", None),
            P("dp", None, "expert"),
        ),
        out_specs=(
            P("dp", "expert"),
            P("dp", "expert"),
            P("dp", None),
            P("dp", "expert", None),
            P("dp", "expert", None),
            P("dp", None, "expert"),
        ),
        check_vma=False,
    )
```

```python
import jax
import jax.numpy as jnp
from jax import lax
from jax.experimental import pallas as pl
from jax.experimental.pallas import tpu as pltpu
from jax.sharding import PartitionSpec as P

CAP = 6
SPARE = 2
LANES = 128
TILES = 4
GROUP = CAP * TILES
SOURCES = 16
RING = 4
SCORE_LANE = 96
WEIGHT_PARTS = 2
PLACE_BITS = 4
VMEM_LIMIT = 24 * 1024 * 1024

F32 = jnp.float32
BF16 = jnp.bfloat16
CONTRACT_LAST = (((1,), (1,)), ((), ()))
CONTRACT_FIRST = (((0,), (0,)), ((), ()))


def dot(left, right, dims=(((1,), (0,)), ((), ()))):
    return lax.dot_general(left, right, dims, preferred_element_type=F32)


def one_zero(condition):
    return jnp.where(condition, 1.0, 0.0).astype(BF16)


def three_parts(value):
    high = value.astype(BF16)
    rest = value - high.astype(F32)
    middle = rest.astype(BF16)
    return high, middle, (rest - middle.astype(F32)).astype(BF16)


def iota(shape, axis):
    return lax.broadcasted_iota(jnp.int32, shape, axis)


def expert_of_row(row, expert):
    offset = row - GROUP * expert
    return (offset >= 0) & (offset < GROUP)


def tile_and_slot(row):
    place = row - GROUP * lax.shift_right_logical(row * 2731, 16)
    tile = (
        (place >= CAP).astype(jnp.int32)
        + (place >= 2 * CAP).astype(jnp.int32)
        + (place >= 3 * CAP).astype(jnp.int32)
    )
    return tile, place - CAP * tile


def reorder_matrix(sorted_row, sent_row):
    per_tile = SOURCES * CAP
    tile = (
        (sorted_row >= per_tile).astype(jnp.int32)
        + (sorted_row >= 2 * per_tile).astype(jnp.int32)
        + (sorted_row >= 3 * per_tile).astype(jnp.int32)
    )
    within = sorted_row - per_tile * tile
    source = lax.shift_right_logical(within * 43, 8)
    return one_zero(sent_row == within + (GROUP - CAP) * source + CAP * tile)


def member_at(base, place_ref, step):
    sign = 1 - 2 * lax.shift_right_logical(place_ref[0], PLACE_BITS)
    return (base + sign * step) & (RING - 1)


def fetch(sources, targets, sems):
    copies = [
        pltpu.make_async_copy(source, target, sems.at[i])
        for i, (source, target) in enumerate(zip(sources, targets))
    ]
    for copy in copies:
        copy.start()
    return copies


def dispatch_kernel(
    routes_hbm,
    weight_hbm,
    slots_hbm,
    tok_hbm,
    cot_hbm,
    send_ref,
    plan_ref,
    routes_ref,
    weight_ref,
    slots_ref,
    tok_ref,
    cot_ref,
    sems,
):
    arguments = (routes_hbm, weight_hbm, slots_hbm, tok_hbm, cot_hbm)
    held = (routes_ref, weight_ref, slots_ref, tok_ref, cot_ref)
    for copy in fetch(arguments, held, sems):
        copy.wait()
    top_count, token_count = routes_ref.shape
    experts = slots_ref.shape[1]
    rows = experts * GROUP
    expert = iota((experts, token_count), 0)
    named = jnp.zeros((experts, token_count), F32)
    scale = jnp.zeros((experts, token_count), F32)
    for k in range(top_count):
        hit = routes_ref[k : k + 1] == expert
        named = named + jnp.where(hit, 1.0, 0.0)
        scale = scale + jnp.where(hit, weight_ref[k : k + 1], 0.0)
    earlier = one_zero(iota((token_count, token_count), 0) < iota((token_count, token_count), 1))
    rank = dot(named.astype(BF16), earlier)
    diagonal = iota((experts, experts), 0) == iota((experts, experts), 1)
    limit = jnp.sum(jnp.where(diagonal, slots_ref[...].astype(F32), 0.0), axis=1, keepdims=True)
    rank = jnp.where((named > 0.0) & (rank < limit + float(SPARE)), rank, -1.0)
    plan_ref[:experts] = rank
    plan_ref[experts:] = scale
    spread = one_zero(expert_of_row(iota((rows, experts), 0), iota((rows, experts), 1)))
    tile, slot = tile_and_slot(iota((rows, token_count), 0))
    taken = dot(spread, rank.astype(BF16)) == slot.astype(F32)
    row_scale = sum(dot(spread, part) for part in three_parts(scale))
    row_scale = jnp.sum(jnp.where(taken, row_scale, 0.0), axis=1, keepdims=True)
    row_scale = jnp.where(tile[:, :1] >= 2, row_scale, 1.0)
    width = tok_ref.shape[0]
    picked = jnp.zeros((rows, LANES), F32)
    for index, ref in ((0, tok_ref), (2, cot_ref)):
        high = jnp.concatenate(
            [ref[LANES:], jnp.zeros((2 * LANES - width, token_count), BF16)], axis=0
        )
        picked = picked + dot(one_zero(taken & (tile == index)), ref[:LANES], CONTRACT_LAST)
        picked = picked + dot(one_zero(taken & (tile == index + 1)), high, CONTRACT_LAST)
    send_ref[...] = (picked * row_scale).astype(BF16).reshape(send_ref.shape)


def partial_kernel(
    place_ref,
    recv_ref,
    gate_hbm,
    up_hbm,
    down_hbm,
    own_ref,
    to_right_ref,
    to_left_ref,
    next_ref,
    previous_ref,
    tok_ref,
    scaled_ref,
    gate_ref,
    up_ref,
    down_ref,
    sems,
):
    copies = fetch((gate_hbm, up_hbm, down_hbm), (gate_ref, up_ref, down_ref), sems)
    experts = recv_ref.shape[0]
    width, hidden = gate_ref.shape
    block = SOURCES * GROUP
    per_tile = SOURCES * CAP
    reorder = reorder_matrix(iota((block, block), 0), iota((block, block), 1))
    for b in range(experts // SOURCES):
        sent = recv_ref[b * SOURCES : (b + 1) * SOURCES].reshape(block, LANES)
        rows = dot(reorder, sent).astype(BF16)
        place = slice(b * per_tile, (b + 1) * per_tile)
        for ref, index in ((tok_ref, 0), (scaled_ref, 2)):
            ref[place, :LANES] = rows[index * per_tile : (index + 1) * per_tile]
            ref[place, LANES:] = rows[(index + 1) * per_tile : (index + 2) * per_tile, : width - LANES]
    held = tok_ref.shape[0] // RING
    half = held // 2
    for copy in copies:
        copy.wait()
    for index, (rows_ref, ref) in enumerate(
        ((tok_ref, gate_ref), (tok_ref, up_ref), (scaled_ref, down_ref))
    ):
        columns = slice(index * hidden, (index + 1) * hidden)
        for step, pieces in (
            (RING // 2, ((to_right_ref, 0), (to_left_ref, half))),
            (1, ((next_ref, 0), (to_right_ref, half))),
            (RING - 1, ((to_left_ref, 0), (previous_ref, 0))),
            (0, ((own_ref, 0), (own_ref, half))),
        ):
            member = member_at(place_ref[0], place_ref, step)
            begin = pl.multiple_of(member * held, held)
            value = dot(rows_ref[pl.ds(begin, held)], ref[...]).astype(BF16)
            for part, (out_ref, start) in enumerate(pieces):
                out_ref[start : start + half, columns] = value[part * half : (part + 1) * half]


def relay_kernel(next_ref, previous_ref, from_left_ref, from_right_ref, to_right_ref, to_left_ref):
    half = next_ref.shape[0]
    to_right_ref[...] = (next_ref[...].astype(F32) + from_left_ref[:half].astype(F32)).astype(BF16)
    to_left_ref[...] = (previous_ref[...].astype(F32) + from_right_ref[half:].astype(F32)).astype(BF16)


def window_kernel(own_ref, from_left_ref, from_right_ref, far_left_ref, far_right_ref, out_ref):
    half = far_left_ref.shape[0]
    out_ref[:half] = (
        own_ref[:half].astype(F32) + from_right_ref[:half].astype(F32) + far_left_ref[...].astype(F32)
    ).astype(BF16)
    out_ref[half:] = (
        own_ref[half:].astype(F32) + from_left_ref[half:].astype(F32) + far_right_ref[...].astype(F32)
    ).astype(BF16)


def middle_kernel(sum_ref, out_ref):
    hidden = sum_ref.shape[1] // 3
    share = out_ref.shape[0]

    def summed(index):
        values = sum_ref[:, index * hidden : (index + 1) * hidden].astype(F32)
        return sum(values[i * share : (i + 1) * share] for i in range(sum_ref.shape[0] // share))

    gate, up, grad = summed(0), summed(1), summed(2)
    sigmoid = jax.nn.sigmoid(gate)
    gated = gate * sigmoid
    hidden_value = (gated * up).astype(BF16)
    out_ref[:, :hidden] = hidden_value
    out_ref[:, hidden : 2 * hidden] = (grad * up * sigmoid * (1.0 + gate * (1.0 - sigmoid))).astype(BF16)
    out_ref[:, 2 * hidden : 3 * hidden] = (grad * gated).astype(BF16)
    score = jnp.sum(hidden_value.astype(F32) * grad, axis=1, keepdims=True)
    lane = iota((gate.shape[0], LANES), 1)
    packed = jnp.zeros(lane.shape, F32)
    for index, part in enumerate(three_parts(score)):
        packed = jnp.where(lane == SCORE_LANE + index, part.astype(F32), packed)
    out_ref[:, 3 * hidden :] = packed.astype(BF16)


def gathered(full_ref, place_ref, own_ref, left_ref, right_ref, far_left_ref, far_right_ref):
    held = own_ref.shape[0]
    half = held // 2
    for ref, step, start in (
        (own_ref, 0, 0),
        (right_ref, 1, 0),
        (left_ref, RING - 1, 0),
        (far_left_ref, RING // 2, 0),
        (far_right_ref, RING // 2, half),
    ):
        member = member_at(place_ref[0], place_ref, step)
        begin = pl.multiple_of(member * held + start, half)
        full_ref[pl.ds(begin, ref.shape[0])] = ref[...]


def gradient_kernel(
    place_ref,
    own_ref,
    left_ref,
    right_ref,
    far_left_ref,
    far_right_ref,
    tok_ref,
    scaled_ref,
    gate_ref,
    up_ref,
    down_ref,
    full_ref,
):
    hidden = gate_ref.shape[1]
    gathered(full_ref, place_ref, own_ref, left_ref, right_ref, far_left_ref, far_right_ref)
    for index, (rows_ref, out_ref) in enumerate(
        ((scaled_ref, down_ref), (tok_ref, gate_ref), (tok_ref, up_ref))
    ):
        columns = slice(index * hidden, (index + 1) * hidden)
        out_ref[...] = dot(rows_ref[...], full_ref[:, columns], CONTRACT_FIRST).astype(BF16)


def rows_kernel(
    place_ref,
    own_ref,
    left_ref,
    right_ref,
    far_left_ref,
    far_right_ref,
    gate_hbm,
    up_hbm,
    down_hbm,
    back_ref,
    full_ref,
    tiles_ref,
    gate_ref,
    up_ref,
    down_ref,
    sems,
):
    copies = fetch((gate_hbm, up_hbm, down_hbm), (gate_ref, up_ref, down_ref), sems)
    experts = back_ref.shape[0]
    width, hidden = gate_ref.shape
    block = SOURCES * GROUP
    per_tile = SOURCES * CAP
    gathered(full_ref, place_ref, own_ref, left_ref, right_ref, far_left_ref, far_right_ref)
    for copy in copies:
        copy.wait()
    out_rows = dot(full_ref[:, :hidden], down_ref[...], CONTRACT_LAST)
    in_rows = dot(full_ref[:, hidden : 2 * hidden], gate_ref[...], CONTRACT_LAST) + dot(
        full_ref[:, 2 * hidden : 3 * hidden], up_ref[...], CONTRACT_LAST
    )
    tiles_ref[0] = out_rows[:, :LANES]
    tiles_ref[1] = full_ref[:, 3 * hidden :].astype(F32)
    tiles_ref[1, :, : width - LANES] = out_rows[:, LANES:]
    tiles_ref[2] = in_rows[:, :LANES]
    tiles_ref[3] = jnp.zeros(tiles_ref.shape[1:], F32)
    tiles_ref[3, :, : width - LANES] = in_rows[:, LANES:]
    restore = reorder_matrix(iota((block, block), 1), iota((block, block), 0))
    for b in range(experts // SOURCES):
        place = slice(b * per_tile, (b + 1) * per_tile)
        stacked = tiles_ref[:, place].astype(BF16).reshape(block, LANES)
        back_ref[b * SOURCES : (b + 1) * SOURCES] = (
            dot(restore, stacked).astype(BF16).reshape(SOURCES, GROUP, LANES)
        )


def combine_kernel(
    back_ref, plan_ref, routes_ref, weight_ref, mixed_ref, input_ref, score_ref, chosen_ref
):
    top_count, token_count = routes_ref.shape
    experts = back_ref.shape[0]
    width = mixed_ref.shape[0]
    rows = experts * GROUP
    back = back_ref[...].reshape(rows, LANES)
    plan = plan_ref[...].T
    rank, scale = plan[:, :experts], plan[:, experts:]
    spread = one_zero(expert_of_row(iota((experts, rows), 1), iota((experts, rows), 0)))
    tile, slot = tile_and_slot(iota((1, rows), 1))
    taken = dot(rank.astype(BF16), spread) == slot.astype(F32)
    for order, part in enumerate(three_parts(scale)[:WEIGHT_PARTS]):
        row_scale = jnp.where(taken, dot(part, spread), 0.0)
        for index in range(2):
            place = (index * WEIGHT_PARTS + order) * token_count
            chosen_ref[place : place + token_count] = jnp.where(tile == index, row_scale, 0.0).astype(BF16)
    taken = jnp.where(taken, 1.0, 0.0)
    for index in range(2):
        place = (2 * WEIGHT_PARTS + index) * token_count
        chosen_ref[place : place + token_count] = jnp.where(tile == 2 + index, taken, 0.0).astype(BF16)
    scored = jnp.where(tile == 1, taken, 0.0).astype(BF16)
    values = dot(chosen_ref[...], back)
    blocks = [values[i * token_count : (i + 1) * token_count] for i in range(2 * WEIGHT_PARTS + 2)]
    low, high = sum(blocks[:WEIGHT_PARTS]), sum(blocks[WEIGHT_PARTS : 2 * WEIGHT_PARTS])
    for ref, low, high in (
        (mixed_ref, low, high),
        (input_ref, blocks[2 * WEIGHT_PARTS], blocks[2 * WEIGHT_PARTS + 1]),
    ):
        ref[:LANES] = low.T.astype(BF16)
        ref[LANES:] = high.T[: width - LANES].astype(BF16)
    lane_of_part = iota((8, LANES), 1) - SCORE_LANE == iota((8, LANES), 0)
    row_score = dot(one_zero(lane_of_part & (iota((8, LANES), 0) < 3)), back, CONTRACT_LAST)
    spread = spread.astype(F32)
    spread = jnp.concatenate([(spread * row_score[i : i + 1]).astype(BF16) for i in range(3)], axis=0)
    by_expert = dot(spread, scored, CONTRACT_LAST)
    by_expert = sum(by_expert[i * experts : (i + 1) * experts] for i in range(3))
    expert = iota((experts, token_count), 0)
    for k in range(top_count):
        hit = routes_ref[k : k + 1] == expert
        value = jnp.sum(jnp.where(hit, by_expert, 0.0), axis=0, keepdims=True)
        score_ref[k : k + 1] = value / weight_ref[k : k + 1]


def kernel_call(body, out_shape, flops, moved, spaces=None, scratch=()):
    places = {}
    if spaces is not None:
        kinds = {"s": pltpu.SMEM, "v": pltpu.VMEM, "a": pl.ANY}
        places["in_specs"] = [pl.BlockSpec(memory_space=kinds[kind]) for kind in spaces]
    return pl.pallas_call(
        body,
        out_shape=out_shape,
        scratch_shapes=scratch,
        compiler_params=pltpu.CompilerParams(vmem_limit_bytes=VMEM_LIMIT),
        cost_estimate=pl.CostEstimate(flops=flops, bytes_accessed=moved, transcendentals=0),
        **places,
    )


def held_copies(*arrays):
    return [pltpu.VMEM(array.shape, array.dtype) for array in arrays] + [
        pltpu.SemaphoreType.DMA((len(arrays),))
    ]


def shifted(block, distance):
    parts, columns = lax.axis_size("expert"), lax.axis_size("dp")
    route = [
        (part * columns + column, (part + (1 - 2 * (column % 2)) * distance) % parts * columns + column)
        for part in range(parts)
        for column in range(columns)
    ]
    return lax.ppermute(block, ("expert", "dp"), route)


def per_device(
    tokens, cotangent, routes, route_weights, owner_slots, gate_weight, up_weight, down_weight
):
    experts = lax.axis_size("dp")
    parts = lax.axis_size("expert")
    token_count, width = tokens.shape
    hidden = gate_weight.shape[2]
    row_count = experts * CAP
    held = row_count // RING
    shape = jax.ShapeDtypeStruct
    exchanged = shape((experts, GROUP, LANES), BF16)
    rows = shape((row_count, width), BF16)
    whole, halved = (shape((size, 3 * hidden), BF16) for size in (held, held // 2))
    groups = [list(range(i, parts, RING)) for i in range(RING)]
    member = lax.axis_index("expert") + ((lax.axis_index("dp") & 1) << PLACE_BITS)
    member = member.astype(jnp.int32).reshape(1)
    weights = (gate_weight[0], up_weight[0], down_weight[0].T)
    arguments = (routes.T, route_weights.T, owner_slots.reshape(1, experts), tokens.T, cotangent.T)
    send, plan = kernel_call(
        dispatch_kernel,
        (exchanged, shape((2 * experts, token_count), F32)),
        300_000_000,
        1_000_000,
        spaces="aaaaa",
        scratch=held_copies(*arguments),
    )(*arguments)
    arrived = lax.all_to_all(send, "dp", split_axis=0, concat_axis=0, tiled=True)
    own, to_right, to_left, following, previous, token_rows, scaled_rows = kernel_call(
        partial_kernel,
        (whole, whole, whole, halved, halved, rows, rows),
        700_000_000,
        4_500_000,
        spaces="svaaa",
        scratch=held_copies(*weights),
    )(member, arrived, *weights)
    from_left, from_right = shifted(to_right, 1), shifted(to_left, -1)
    relay_right, relay_left = kernel_call(relay_kernel, (halved, halved), 300_000, 1_500_000)(
        following, previous, from_left, from_right
    )
    far_left, far_right = shifted(relay_right, 1), shifted(relay_left, -1)
    window = kernel_call(window_kernel, whole, 600_000, 2_000_000)(
        own, from_left, from_right, far_left, far_right
    )
    summands = lax.all_to_all(
        window, "expert", split_axis=0, concat_axis=0, tiled=True, axis_index_groups=groups
    )
    share = kernel_call(
        middle_kernel, shape((row_count // parts, 3 * hidden + LANES), BF16), 1_000_000, 700_000
    )(summands)
    own = lax.all_gather(share, "expert", axis=0, tiled=True, axis_index_groups=groups)
    half = held // 2
    left, right = shifted(own, 1), shifted(own, -1)
    pieces = (own, left, right, shifted(left[:half], 1), shifted(right[half:], -1))
    full = pltpu.VMEM((row_count, 3 * hidden + LANES), BF16)
    back = kernel_call(
        rows_kernel,
        exchanged,
        700_000_000,
        4_500_000,
        spaces="svvvvvaaa",
        scratch=[full, pltpu.VMEM((TILES, row_count, LANES), F32)] + held_copies(*weights),
    )(member, *pieces, *weights)
    returned = lax.all_to_all(back, "dp", split_axis=0, concat_axis=0, tiled=True)
    matrix = shape((width, hidden), BF16)
    gate_grad, up_grad, down_grad = kernel_call(
        gradient_kernel,
        (matrix, matrix, matrix),
        700_000_000,
        4_500_000,
        spaces="svvvvvvv",
        scratch=[full],
    )(member, *pieces, token_rows, scaled_rows)
    down_grad = down_grad.T
    token_shape = shape((width, token_count), BF16)
    mixed, input_gradient, route_gradient = kernel_call(
        combine_kernel,
        (token_shape, token_shape, shape(arguments[0].shape, F32)),
        500_000_000,
        1_000_000,
        scratch=[pltpu.VMEM(((2 * WEIGHT_PARTS + 2) * token_count, experts * GROUP), BF16)],
    )(returned, plan, arguments[0], arguments[1])
    return (
        mixed.T,
        input_gradient.T,
        route_gradient.T,
        gate_grad[None],
        up_grad[None],
        down_grad[None],
    )


def solution(mesh):
    return jax.shard_map(
        per_device,
        mesh=mesh,
        in_specs=(
            P("dp", "expert"),
            P("dp", "expert"),
            P("dp", None),
            P("dp", None),
            P(),
            P("dp", "expert", None),
            P("dp", "expert", None),
            P("dp", None, "expert"),
        ),
        out_specs=(
            P("dp", "expert"),
            P("dp", "expert"),
            P("dp", None),
            P("dp", "expert", None),
            P("dp", "expert", None),
            P("dp", None, "expert"),
        ),
        check_vma=False,
    )
```

```python
import jax
import jax.numpy as jnp
from jax import lax
from jax.experimental import pallas as pl
from jax.experimental.pallas import tpu as pltpu
from jax.sharding import PartitionSpec as P

CAP = 6
SPARE = 2
LANES = 128
TILES = 4
GROUP = CAP * TILES
SOURCES = 16
RING = 4
SCORE_LANE = 96
WEIGHT_PARTS = 2
VMEM_LIMIT = 24 * 1024 * 1024

F32 = jnp.float32
BF16 = jnp.bfloat16
CONTRACT_LAST = (((1,), (1,)), ((), ()))
CONTRACT_FIRST = (((0,), (0,)), ((), ()))


def dot(left, right, dims=(((1,), (0,)), ((), ()))):
    return lax.dot_general(left, right, dims, preferred_element_type=F32)


def one_zero(condition):
    return jnp.where(condition, 1.0, 0.0).astype(BF16)


def three_parts(value):
    high = value.astype(BF16)
    rest = value - high.astype(F32)
    middle = rest.astype(BF16)
    return high, middle, (rest - middle.astype(F32)).astype(BF16)


def iota(shape, axis):
    return lax.broadcasted_iota(jnp.int32, shape, axis)


def expert_of_row(row, expert):
    offset = row - GROUP * expert
    return (offset >= 0) & (offset < GROUP)


def tile_and_slot(row):
    place = row - GROUP * lax.shift_right_logical(row * 2731, 16)
    tile = (
        (place >= CAP).astype(jnp.int32)
        + (place >= 2 * CAP).astype(jnp.int32)
        + (place >= 3 * CAP).astype(jnp.int32)
    )
    return tile, place - CAP * tile


def reorder_matrix(sorted_row, sent_row):
    per_tile = SOURCES * CAP
    tile = (
        (sorted_row >= per_tile).astype(jnp.int32)
        + (sorted_row >= 2 * per_tile).astype(jnp.int32)
        + (sorted_row >= 3 * per_tile).astype(jnp.int32)
    )
    within = sorted_row - per_tile * tile
    source = lax.shift_right_logical(within * 43, 8)
    return one_zero(sent_row == within + (GROUP - CAP) * source + CAP * tile)


def fetch(sources, targets, sems):
    copies = [
        pltpu.make_async_copy(source, target, sems.at[i])
        for i, (source, target) in enumerate(zip(sources, targets))
    ]
    for copy in copies:
        copy.start()
    return copies


def dispatch_kernel(
    routes_hbm,
    weight_hbm,
    slots_hbm,
    tok_hbm,
    cot_hbm,
    send_ref,
    plan_ref,
    routes_ref,
    weight_ref,
    slots_ref,
    tok_ref,
    cot_ref,
    sems,
):
    arguments = (routes_hbm, weight_hbm, slots_hbm, tok_hbm, cot_hbm)
    held = (routes_ref, weight_ref, slots_ref, tok_ref, cot_ref)
    for copy in fetch(arguments, held, sems):
        copy.wait()
    top_count, token_count = routes_ref.shape
    experts = slots_ref.shape[1]
    rows = experts * GROUP
    expert = iota((experts, token_count), 0)
    named = jnp.zeros((experts, token_count), F32)
    scale = jnp.zeros((experts, token_count), F32)
    for k in range(top_count):
        hit = routes_ref[k : k + 1] == expert
        named = named + jnp.where(hit, 1.0, 0.0)
        scale = scale + jnp.where(hit, weight_ref[k : k + 1], 0.0)
    earlier = one_zero(iota((token_count, token_count), 0) < iota((token_count, token_count), 1))
    rank = dot(named.astype(BF16), earlier)
    diagonal = iota((experts, experts), 0) == iota((experts, experts), 1)
    limit = jnp.sum(jnp.where(diagonal, slots_ref[...].astype(F32), 0.0), axis=1, keepdims=True)
    rank = jnp.where((named > 0.0) & (rank < limit + float(SPARE)), rank, -1.0)
    plan_ref[:experts] = rank
    plan_ref[experts:] = scale
    spread = one_zero(expert_of_row(iota((rows, experts), 0), iota((rows, experts), 1)))
    tile, slot = tile_and_slot(iota((rows, token_count), 0))
    taken = dot(spread, rank.astype(BF16)) == slot.astype(F32)
    row_scale = sum(dot(spread, part) for part in three_parts(scale))
    row_scale = jnp.sum(jnp.where(taken, row_scale, 0.0), axis=1, keepdims=True)
    row_scale = jnp.where(tile[:, :1] >= 2, row_scale, 1.0)
    width = tok_ref.shape[0]
    picked = jnp.zeros((rows, LANES), F32)
    for index, ref in ((0, tok_ref), (2, cot_ref)):
        high = jnp.concatenate(
            [ref[LANES:], jnp.zeros((2 * LANES - width, token_count), BF16)], axis=0
        )
        picked = picked + dot(one_zero(taken & (tile == index)), ref[:LANES], CONTRACT_LAST)
        picked = picked + dot(one_zero(taken & (tile == index + 1)), high, CONTRACT_LAST)
    send_ref[...] = (picked * row_scale).astype(BF16).reshape(send_ref.shape)


def partial_kernel(
    place_ref,
    recv_ref,
    gate_hbm,
    up_hbm,
    down_hbm,
    own_ref,
    to_right_ref,
    to_left_ref,
    next_ref,
    previous_ref,
    tok_ref,
    scaled_ref,
    gate_ref,
    up_ref,
    down_ref,
    sems,
):
    copies = fetch((gate_hbm, up_hbm, down_hbm), (gate_ref, up_ref, down_ref), sems)
    experts = recv_ref.shape[0]
    width, hidden = gate_ref.shape
    block = SOURCES * GROUP
    per_tile = SOURCES * CAP
    reorder = reorder_matrix(iota((block, block), 0), iota((block, block), 1))
    for b in range(experts // SOURCES):
        sent = recv_ref[b * SOURCES : (b + 1) * SOURCES].reshape(block, LANES)
        rows = dot(reorder, sent).astype(BF16)
        place = slice(b * per_tile, (b + 1) * per_tile)
        for ref, index in ((tok_ref, 0), (scaled_ref, 2)):
            ref[place, :LANES] = rows[index * per_tile : (index + 1) * per_tile]
            ref[place, LANES:] = rows[(index + 1) * per_tile : (index + 2) * per_tile, : width - LANES]
    held = tok_ref.shape[0] // RING
    half = held // 2
    for copy in copies:
        copy.wait()
    for index, (rows_ref, ref) in enumerate(
        ((tok_ref, gate_ref), (tok_ref, up_ref), (scaled_ref, down_ref))
    ):
        columns = slice(index * hidden, (index + 1) * hidden)
        for step, pieces in (
            (RING // 2, ((to_right_ref, 0), (to_left_ref, half))),
            (1, ((next_ref, 0), (to_right_ref, half))),
            (RING - 1, ((to_left_ref, 0), (previous_ref, 0))),
            (0, ((own_ref, 0), (own_ref, half))),
        ):
            member = (place_ref[0] + step) & (RING - 1)
            begin = pl.multiple_of(member * held, held)
            value = dot(rows_ref[pl.ds(begin, held)], ref[...]).astype(BF16)
            for part, (out_ref, start) in enumerate(pieces):
                out_ref[start : start + half, columns] = value[part * half : (part + 1) * half]


def relay_kernel(next_ref, previous_ref, from_left_ref, from_right_ref, to_right_ref, to_left_ref):
    half = next_ref.shape[0]
    to_right_ref[...] = (next_ref[...].astype(F32) + from_left_ref[:half].astype(F32)).astype(BF16)
    to_left_ref[...] = (previous_ref[...].astype(F32) + from_right_ref[half:].astype(F32)).astype(BF16)


def window_kernel(own_ref, from_left_ref, from_right_ref, far_left_ref, far_right_ref, out_ref):
    half = far_left_ref.shape[0]
    out_ref[:half] = (
        own_ref[:half].astype(F32) + from_right_ref[:half].astype(F32) + far_left_ref[...].astype(F32)
    ).astype(BF16)
    out_ref[half:] = (
        own_ref[half:].astype(F32) + from_left_ref[half:].astype(F32) + far_right_ref[...].astype(F32)
    ).astype(BF16)


def middle_kernel(sum_ref, out_ref):
    hidden = sum_ref.shape[1] // 3
    share = out_ref.shape[0]

    def summed(index):
        values = sum_ref[:, index * hidden : (index + 1) * hidden].astype(F32)
        return sum(values[i * share : (i + 1) * share] for i in range(sum_ref.shape[0] // share))

    gate, up, grad = summed(0), summed(1), summed(2)
    sigmoid = jax.nn.sigmoid(gate)
    gated = gate * sigmoid
    hidden_value = (gated * up).astype(BF16)
    out_ref[:, :hidden] = hidden_value
    out_ref[:, hidden : 2 * hidden] = (grad * up * sigmoid * (1.0 + gate * (1.0 - sigmoid))).astype(BF16)
    out_ref[:, 2 * hidden : 3 * hidden] = (grad * gated).astype(BF16)
    score = jnp.sum(hidden_value.astype(F32) * grad, axis=1, keepdims=True)
    lane = iota((gate.shape[0], LANES), 1)
    packed = jnp.zeros(lane.shape, F32)
    for index, part in enumerate(three_parts(score)):
        packed = jnp.where(lane == SCORE_LANE + index, part.astype(F32), packed)
    out_ref[:, 3 * hidden :] = packed.astype(BF16)


def gathered(full_ref, place_ref, own_ref, left_ref, right_ref, far_left_ref, far_right_ref):
    held = own_ref.shape[0]
    half = held // 2
    for ref, step, start in (
        (own_ref, 0, 0),
        (right_ref, 1, 0),
        (left_ref, RING - 1, 0),
        (far_left_ref, RING // 2, 0),
        (far_right_ref, RING // 2, half),
    ):
        member = (place_ref[0] + step) & (RING - 1)
        begin = pl.multiple_of(member * held + start, half)
        full_ref[pl.ds(begin, ref.shape[0])] = ref[...]


def gradient_kernel(
    place_ref,
    own_ref,
    left_ref,
    right_ref,
    far_left_ref,
    far_right_ref,
    tok_ref,
    scaled_ref,
    gate_ref,
    up_ref,
    down_ref,
    full_ref,
):
    hidden = gate_ref.shape[1]
    gathered(full_ref, place_ref, own_ref, left_ref, right_ref, far_left_ref, far_right_ref)
    for index, (rows_ref, out_ref) in enumerate(
        ((scaled_ref, down_ref), (tok_ref, gate_ref), (tok_ref, up_ref))
    ):
        columns = slice(index * hidden, (index + 1) * hidden)
        out_ref[...] = dot(rows_ref[...], full_ref[:, columns], CONTRACT_FIRST).astype(BF16)


def rows_kernel(
    place_ref,
    own_ref,
    left_ref,
    right_ref,
    far_left_ref,
    far_right_ref,
    gate_hbm,
    up_hbm,
    down_hbm,
    back_ref,
    full_ref,
    tiles_ref,
    gate_ref,
    up_ref,
    down_ref,
    sems,
):
    copies = fetch((gate_hbm, up_hbm, down_hbm), (gate_ref, up_ref, down_ref), sems)
    experts = back_ref.shape[0]
    width, hidden = gate_ref.shape
    block = SOURCES * GROUP
    per_tile = SOURCES * CAP
    gathered(full_ref, place_ref, own_ref, left_ref, right_ref, far_left_ref, far_right_ref)
    for copy in copies:
        copy.wait()
    out_rows = dot(full_ref[:, :hidden], down_ref[...], CONTRACT_LAST)
    in_rows = dot(full_ref[:, hidden : 2 * hidden], gate_ref[...], CONTRACT_LAST) + dot(
        full_ref[:, 2 * hidden : 3 * hidden], up_ref[...], CONTRACT_LAST
    )
    tiles_ref[0] = out_rows[:, :LANES]
    tiles_ref[1] = full_ref[:, 3 * hidden :].astype(F32)
    tiles_ref[1, :, : width - LANES] = out_rows[:, LANES:]
    tiles_ref[2] = in_rows[:, :LANES]
    tiles_ref[3] = jnp.zeros(tiles_ref.shape[1:], F32)
    tiles_ref[3, :, : width - LANES] = in_rows[:, LANES:]
    restore = reorder_matrix(iota((block, block), 1), iota((block, block), 0))
    for b in range(experts // SOURCES):
        place = slice(b * per_tile, (b + 1) * per_tile)
        stacked = tiles_ref[:, place].astype(BF16).reshape(block, LANES)
        back_ref[b * SOURCES : (b + 1) * SOURCES] = (
            dot(restore, stacked).astype(BF16).reshape(SOURCES, GROUP, LANES)
        )


def combine_kernel(
    back_ref, plan_ref, routes_ref, weight_ref, mixed_ref, input_ref, score_ref, chosen_ref
):
    top_count, token_count = routes_ref.shape
    experts = back_ref.shape[0]
    width = mixed_ref.shape[0]
    rows = experts * GROUP
    back = back_ref[...].reshape(rows, LANES)
    plan = plan_ref[...].T
    rank, scale = plan[:, :experts], plan[:, experts:]
    spread = one_zero(expert_of_row(iota((experts, rows), 1), iota((experts, rows), 0)))
    tile, slot = tile_and_slot(iota((1, rows), 1))
    taken = dot(rank.astype(BF16), spread) == slot.astype(F32)
    for order, part in enumerate(three_parts(scale)[:WEIGHT_PARTS]):
        row_scale = jnp.where(taken, dot(part, spread), 0.0)
        for index in range(2):
            place = (index * WEIGHT_PARTS + order) * token_count
            chosen_ref[place : place + token_count] = jnp.where(tile == index, row_scale, 0.0).astype(BF16)
    taken = jnp.where(taken, 1.0, 0.0)
    for index in range(2):
        place = (2 * WEIGHT_PARTS + index) * token_count
        chosen_ref[place : place + token_count] = jnp.where(tile == 2 + index, taken, 0.0).astype(BF16)
    scored = jnp.where(tile == 1, taken, 0.0).astype(BF16)
    values = dot(chosen_ref[...], back)
    blocks = [values[i * token_count : (i + 1) * token_count] for i in range(2 * WEIGHT_PARTS + 2)]
    low, high = sum(blocks[:WEIGHT_PARTS]), sum(blocks[WEIGHT_PARTS : 2 * WEIGHT_PARTS])
    for ref, low, high in (
        (mixed_ref, low, high),
        (input_ref, blocks[2 * WEIGHT_PARTS], blocks[2 * WEIGHT_PARTS + 1]),
    ):
        ref[:LANES] = low.T.astype(BF16)
        ref[LANES:] = high.T[: width - LANES].astype(BF16)
    lane_of_part = iota((8, LANES), 1) - SCORE_LANE == iota((8, LANES), 0)
    row_score = dot(one_zero(lane_of_part & (iota((8, LANES), 0) < 3)), back, CONTRACT_LAST)
    spread = spread.astype(F32)
    spread = jnp.concatenate([(spread * row_score[i : i + 1]).astype(BF16) for i in range(3)], axis=0)
    by_expert = dot(spread, scored, CONTRACT_LAST)
    by_expert = sum(by_expert[i * experts : (i + 1) * experts] for i in range(3))
    expert = iota((experts, token_count), 0)
    for k in range(top_count):
        hit = routes_ref[k : k + 1] == expert
        value = jnp.sum(jnp.where(hit, by_expert, 0.0), axis=0, keepdims=True)
        score_ref[k : k + 1] = value / weight_ref[k : k + 1]


def kernel_call(body, out_shape, flops, moved, spaces=None, scratch=()):
    places = {}
    if spaces is not None:
        kinds = {"s": pltpu.SMEM, "v": pltpu.VMEM, "a": pl.ANY}
        places["in_specs"] = [pl.BlockSpec(memory_space=kinds[kind]) for kind in spaces]
    return pl.pallas_call(
        body,
        out_shape=out_shape,
        scratch_shapes=scratch,
        compiler_params=pltpu.CompilerParams(vmem_limit_bytes=VMEM_LIMIT),
        cost_estimate=pl.CostEstimate(flops=flops, bytes_accessed=moved, transcendentals=0),
        **places,
    )


def held_copies(*arrays):
    return [pltpu.VMEM(array.shape, array.dtype) for array in arrays] + [
        pltpu.SemaphoreType.DMA((len(arrays),))
    ]


def shifted(block, distance):
    parts = lax.axis_size("expert")
    return lax.ppermute(block, "expert", [(i, (i + distance) % parts) for i in range(parts)])


def per_device(
    tokens, cotangent, routes, route_weights, owner_slots, gate_weight, up_weight, down_weight
):
    experts = lax.axis_size("dp")
    parts = lax.axis_size("expert")
    token_count, width = tokens.shape
    hidden = gate_weight.shape[2]
    row_count = experts * CAP
    held = row_count // RING
    shape = jax.ShapeDtypeStruct
    exchanged = shape((experts, GROUP, LANES), BF16)
    rows = shape((row_count, width), BF16)
    whole, halved = (shape((size, 3 * hidden), BF16) for size in (held, held // 2))
    groups = [list(range(i, parts, RING)) for i in range(RING)]
    member = lax.axis_index("expert").astype(jnp.int32).reshape(1)
    weights = (gate_weight[0], up_weight[0], down_weight[0].T)
    arguments = (routes.T, route_weights.T, owner_slots.reshape(1, experts), tokens.T, cotangent.T)
    send, plan = kernel_call(
        dispatch_kernel,
        (exchanged, shape((2 * experts, token_count), F32)),
        300_000_000,
        1_000_000,
        spaces="aaaaa",
        scratch=held_copies(*arguments),
    )(*arguments)
    arrived = lax.all_to_all(send, "dp", split_axis=0, concat_axis=0, tiled=True)
    own, to_right, to_left, following, previous, token_rows, scaled_rows = kernel_call(
        partial_kernel,
        (whole, whole, whole, halved, halved, rows, rows),
        700_000_000,
        4_500_000,
        spaces="svaaa",
        scratch=held_copies(*weights),
    )(member, arrived, *weights)
    from_left, from_right = shifted(to_right, 1), shifted(to_left, -1)
    relay_right, relay_left = kernel_call(relay_kernel, (halved, halved), 300_000, 1_500_000)(
        following, previous, from_left, from_right
    )
    far_left, far_right = shifted(relay_right, 1), shifted(relay_left, -1)
    window = kernel_call(window_kernel, whole, 600_000, 2_000_000)(
        own, from_left, from_right, far_left, far_right
    )
    summands = lax.all_to_all(
        window, "expert", split_axis=0, concat_axis=0, tiled=True, axis_index_groups=groups
    )
    share = kernel_call(
        middle_kernel, shape((row_count // parts, 3 * hidden + LANES), BF16), 1_000_000, 700_000
    )(summands)
    own = lax.all_gather(share, "expert", axis=0, tiled=True, axis_index_groups=groups)
    half = held // 2
    left, right = shifted(own, 1), shifted(own, -1)
    pieces = (own, left, right, shifted(left[:half], 1), shifted(right[half:], -1))
    full = pltpu.VMEM((row_count, 3 * hidden + LANES), BF16)
    back = kernel_call(
        rows_kernel,
        exchanged,
        700_000_000,
        4_500_000,
        spaces="svvvvvaaa",
        scratch=[full, pltpu.VMEM((TILES, row_count, LANES), F32)] + held_copies(*weights),
    )(member, *pieces, *weights)
    returned = lax.all_to_all(back, "dp", split_axis=0, concat_axis=0, tiled=True)
    matrix = shape((width, hidden), BF16)
    gate_grad, up_grad, down_grad = kernel_call(
        gradient_kernel,
        (matrix, matrix, matrix),
        700_000_000,
        4_500_000,
        spaces="svvvvvvv",
        scratch=[full],
    )(member, *pieces, token_rows, scaled_rows)
    down_grad = down_grad.T
    token_shape = shape((width, token_count), BF16)
    mixed, input_gradient, route_gradient = kernel_call(
        combine_kernel,
        (token_shape, token_shape, shape(arguments[0].shape, F32)),
        500_000_000,
        1_000_000,
        scratch=[pltpu.VMEM(((2 * WEIGHT_PARTS + 2) * token_count, experts * GROUP), BF16)],
    )(returned, plan, arguments[0], arguments[1])
    return (
        mixed.T,
        input_gradient.T,
        route_gradient.T,
        gate_grad[None],
        up_grad[None],
        down_grad[None],
    )


def solution(mesh):
    return jax.shard_map(
        per_device,
        mesh=mesh,
        in_specs=(
            P("dp", "expert"),
            P("dp", "expert"),
            P("dp", None),
            P("dp", None),
            P(),
            P("dp", "expert", None),
            P("dp", "expert", None),
            P("dp", None, "expert"),
        ),
        out_specs=(
            P("dp", "expert"),
            P("dp", "expert"),
            P("dp", None),
            P("dp", "expert", None),
            P("dp", "expert", None),
            P("dp", None, "expert"),
        ),
        check_vma=False,
    )
```
